128 devices in a mesh: frame: 16 (over y, x_lo, core), row: 4 (over z), col: 2 (over x_hi).
Axes of the slice: x: 4 (x_hi: 2, x_lo: 2; x = x_hi * 2 + x_lo), y: 4, z: 4, core: 2. Of those that a mesh axis runs over, the one named last changes fastest.
Arguments:
- images: bfloat16 [64, 8, 4, 2, 128, 128], P('frame', 'row', 'col'), may hold values from -36 to 36
- corners: int32 [2, 64, 8, 4], P(None, 'frame', 'row', 'col'), may hold values from -16 to 16
- window_kind_index: int32 [8, 4], P('row', 'col'), may hold values from 0 to 3
- coefficients: float32 [64, 8, 4, 36], P('frame', 'row', 'col'), may hold values from -2.5 to 2.5
- step_size: float32 [], replicated, may hold values from 0.1 to 0.4
- noise_weight: float32 [], replicated, may hold values from 0.5 to 4
- smooth_weight: float32 [], replicated, may hold values from 0.3 to 3
Outputs:
- coefficients_out: float32 [64, 8, 4, 36], P('frame', 'row', 'col')
- object_spectrum: float32 [2, 8, 4, 128, 128], P(None, 'row', 'col', 'frame')
The draws below stay inside these ranges and needn't reach their ends.
All inputs are finite; a program needn't handle non-finite values.
Results may differ from the reference program's by a relative error of at most 0.0003.
Values sent between devices are 32-bit elements; how exact they have to be, the bound alone decides.
A program may use at most 128 MiB of HBM per device.

```python
import math
import jax
import jax.numpy as jnp
from jax import lax

SUBFIELD_PIXELS = 128
ZERNIKE_COUNT = 36
CHANNEL_COUNT = 2
WINDOW_KINDS = 4
ITERS = 2
FRAME_COUNT = 64
SUBFIELD_ROWS = 8
SUBFIELD_COLUMNS = 4


def draw_images(key, part):
    key = jax.random.fold_in(key, 7)
    key_noise, key_scale = jax.random.split(key, 2)
    array_shape = (FRAME_COUNT, SUBFIELD_ROWS, SUBFIELD_COLUMNS, CHANNEL_COUNT, SUBFIELD_PIXELS, SUBFIELD_PIXELS)
    position = jnp.arange(FRAME_COUNT, dtype=jnp.float32) / max(FRAME_COUNT - 1, 1)
    jitter = jax.random.uniform(key_scale, (FRAME_COUNT,), jnp.float32, 0.0, 1.0)
    frame_scale = jnp.exp(math.log(3.0) * position + math.log(3.0) * jitter)
    values = jnp.clip(jax.random.normal(key_noise, array_shape, jnp.float32), -4.0, 4.0)
    return (frame_scale[:, None, None, None, None, None] * values).astype(jnp.bfloat16)


def touch_ends(drawn, key, least, largest):
    spot = [jax.random.randint(jax.random.fold_in(key, axis), (), 0, length) for axis, length in enumerate(drawn.shape)]
    main_axis = drawn.shape.index(max(drawn.shape))
    neighbour = spot[:main_axis] + [(spot[main_axis] + 1) % drawn.shape[main_axis]] + spot[main_axis + 1:]
    return drawn.at[tuple(spot)].set(least).at[tuple(neighbour)].set(largest)


def level_of(stream_key, dims, pieces, least, top_value):
    def one(dim, parts):
        steps = jax.random.uniform(jax.random.fold_in(jax.random.fold_in(stream_key, 6), dim), (parts,), jnp.float32, least / len(pieces), top_value / len(pieces))
        return jnp.repeat(jnp.exp(steps), dims[dim] // parts).reshape((-1,) + (1,) * (len(dims) - dim - 1))

    loudness = one(*pieces[0])
    for cut in pieces[1:]:
        loudness = loudness * one(*cut)
    return loudness


def gaussian(stream_key, dims, deviation, most, cuts=(), kind=jnp.bfloat16):
    loudness = level_of(stream_key, dims, cuts, -0.22, 0.18) if cuts else 1.0
    drawn = jax.random.normal(stream_key, dims, jnp.float32) * deviation * loudness
    return jnp.minimum(jnp.maximum(drawn, -most), most).astype(kind)


def setup_inputs(seed: int = 0) -> dict:
    seeds = jax.random.split(jax.random.key(seed), 8)
    images = draw_images(jax.random.fold_in(seeds[7], 71), 0)
    corners = touch_ends(jax.random.randint(seeds[1], (2, FRAME_COUNT, SUBFIELD_ROWS, SUBFIELD_COLUMNS), -16, 17), jax.random.fold_in(seeds[1], 1), -16, 16).astype(jnp.int32)
    window_kind_index = touch_ends(jax.random.randint(seeds[2], (SUBFIELD_ROWS, SUBFIELD_COLUMNS), 0, WINDOW_KINDS), jax.random.fold_in(seeds[2], 1), 0, WINDOW_KINDS - 1).astype(jnp.int32)
    coefficients = gaussian(seeds[3], (FRAME_COUNT, SUBFIELD_ROWS, SUBFIELD_COLUMNS, ZERNIKE_COUNT), 0.25, 2.5, ((0, 16), (1, 4), (2, 2)), jnp.float32)
    step_size = jnp.clip(jnp.exp(jax.random.uniform(seeds[4], (), jnp.float32, math.log(0.1), math.log(0.4))), 0.1, 0.4)
    noise_weight = jnp.clip(jnp.exp(jax.random.uniform(seeds[5], (), jnp.float32, math.log(0.5), math.log(4.0))), 0.5, 4.0)
    smooth_weight = jnp.clip(jnp.exp(jax.random.uniform(seeds[6], (), jnp.float32, math.log(0.3), math.log(3.0))), 0.3, 3.0)
    return dict(images=images, corners=corners, window_kind_index=window_kind_index, coefficients=coefficients, step_size=step_size, noise_weight=noise_weight, smooth_weight=smooth_weight)


DIVERSITY = 1.5
TINY = 1e-06
EXACT = lax.Precision.HIGHEST

def noll_order(mode_index):
    radial_order = (math.isqrt(8 * (mode_index - 1) + 1) - 1) // 2
    position = mode_index - radial_order * (radial_order + 1) // 2
    parity = radial_order % 2
    azimuth = (position + parity) // 2 * 2 - parity
    if azimuth != 0 and mode_index % 2 == 1:
        azimuth = -azimuth
    return (radial_order, azimuth)

def radial_poly(radial_order, azimuth, radius):
    summed = jnp.zeros(radius.shape, jnp.float32)
    for term_index in range((radial_order - azimuth) // 2 + 1):
        factor = (-1) ** term_index * math.factorial(radial_order - term_index) / (math.factorial(term_index) * math.factorial((radial_order + azimuth) // 2 - term_index) * math.factorial((radial_order - azimuth) // 2 - term_index))
        summed = summed + factor * radius ** (radial_order - 2 * term_index)
    return summed

def zernike_table(pixels, modes):
    offsets = (jnp.arange(pixels, dtype=jnp.float32) - pixels / 2.0) / (pixels // 4)
    ones_line = jnp.ones((pixels,), jnp.float32)
    rows_grid = offsets[:, None] * ones_line[None, :]
    cols_grid = ones_line[:, None] * offsets[None, :]
    radius = jnp.sqrt(rows_grid * rows_grid + cols_grid * cols_grid)
    azimuth_angle = jnp.arctan2(rows_grid, cols_grid)
    pupil_mask = jnp.where(radius <= 1.0, 1.0, 0.0).astype(jnp.float32)
    shapes = []
    for mode_index in range(2, modes + 2):
        radial_order, azimuth = noll_order(mode_index)
        radial = radial_poly(radial_order, abs(azimuth), radius)
        if azimuth == 0:
            mode_shape = math.sqrt(radial_order + 1) * radial
        elif azimuth > 0:
            mode_shape = math.sqrt(2 * (radial_order + 1)) * radial * jnp.cos(azimuth * azimuth_angle)
        else:
            mode_shape = math.sqrt(2 * (radial_order + 1)) * radial * jnp.sin(-azimuth * azimuth_angle)
        shapes.append(mode_shape * pupil_mask)
    return (jnp.stack(shapes).astype(jnp.float32), pupil_mask)

def dft_tables(pixels):
    indices = jnp.arange(pixels, dtype=jnp.int32)
    product = indices[:, None] * indices[None, :] % pixels
    angles = product.astype(jnp.float32) * (2.0 * math.pi / pixels)
    return (jnp.cos(angles), -jnp.sin(angles))

def transform(real_part, imag_part, cosine, sine):
    if imag_part is None:
        half_real = jnp.matmul(real_part, cosine, precision=EXACT)
        half_imag = jnp.matmul(real_part, sine, precision=EXACT)
    else:
        half_real = jnp.matmul(real_part, cosine, precision=EXACT) - jnp.matmul(imag_part, sine, precision=EXACT)
        half_imag = jnp.matmul(real_part, sine, precision=EXACT) + jnp.matmul(imag_part, cosine, precision=EXACT)
    out_real = jnp.einsum('uy,...yx->...ux', cosine, half_real, precision=EXACT) - jnp.einsum('uy,...yx->...ux', sine, half_imag, precision=EXACT)
    out_imag = jnp.einsum('uy,...yx->...ux', sine, half_real, precision=EXACT) + jnp.einsum('uy,...yx->...ux', cosine, half_imag, precision=EXACT)
    return (out_real, out_imag)

def window_table(pixels, kinds):
    positions = jnp.arange(pixels, dtype=jnp.int32)
    edges = jnp.minimum(positions, pixels - 1 - positions).astype(jnp.float32)
    widths = ((jnp.arange(kinds, dtype=jnp.int32) + 1) * pixels // 16).astype(jnp.float32)
    taper = jnp.where(edges[None, :] < widths[:, None], 0.5 - 0.5 * jnp.cos(math.pi * (edges[None, :] + 0.5) / widths[:, None]), 1.0)
    return taper[:, :, None] * taper[:, None, :]

def spectra(images, corners, window_kind_index, cosine, sine, kinds):
    pixels = images.shape[-1]
    tables = window_table(pixels, kinds)
    choose = (window_kind_index[..., None] == jnp.arange(kinds, dtype=jnp.int32)).astype(jnp.float32)
    window = jnp.einsum('rck,kyx->rcyx', choose, tables, precision=EXACT)
    windowed = images.astype(jnp.float32) * window[None, :, :, None]
    part_real, part_imag = transform(windowed, None, cosine, sine)
    frequency = jnp.arange(pixels, dtype=jnp.int32)
    shift_rows = corners[0][:, :, :, None, None, None]
    shift_cols = corners[1][:, :, :, None, None, None]
    phase_index = (frequency[:, None] * shift_rows % pixels + frequency[None, :] * shift_cols % pixels) % pixels
    angles = phase_index.astype(jnp.float32) * (2.0 * math.pi / pixels)
    ramp_real = jnp.cos(angles) / pixels
    ramp_imag = jnp.sin(angles) / pixels
    return (part_real * ramp_real - part_imag * ramp_imag, part_real * ramp_imag + part_imag * ramp_real)

def optics(values, basis, pupil_mask, cosine, sine):
    pixels = basis.shape[-1]
    flat_phase = jnp.matmul(values, basis.reshape(basis.shape[0], pixels * pixels), precision=EXACT)
    phases = flat_phase.reshape(values.shape[:-1] + (1, pixels, pixels))
    diverse = jnp.stack([jnp.zeros_like(basis[2]), DIVERSITY * basis[2]])
    phases = phases + diverse
    field_real = pupil_mask * jnp.cos(phases)
    field_imag = pupil_mask * jnp.sin(phases)
    spot_real, spot_imag = transform(field_real, field_imag, cosine, sine)
    spread = spot_real * spot_real + spot_imag * spot_imag
    spread = spread / lax.optimization_barrier(jnp.sum(spread, axis=(-2, -1), keepdims=True))
    return transform(spread, None, cosine, sine)

def reference(images, corners, window_kind_index, coefficients, step_size, noise_weight, smooth_weight):
    pixels = images.shape[-1]
    cosine, sine = dft_tables(pixels)
    basis, pupil_mask = zernike_table(pixels, coefficients.shape[-1])
    corner_frames = jnp.moveaxis(corners, 1, 0)

    def frame_data(image_frame, corner_frame):
        data_real, data_imag = spectra(image_frame[None], corner_frame[:, None], window_kind_index, cosine, sine, WINDOW_KINDS)
        return (data_real[0], data_imag[0])

    def frame_optics(values):
        otf_real, otf_imag = optics(values[None], basis, pupil_mask, cosine, sine)
        return (otf_real[0], otf_imag[0])
    object_real = None
    object_imag = None
    for iteration in range(ITERS):

        def accumulate(carry, inputs):
            image_frame, corner_frame, coeff_frame = inputs
            data_real, data_imag = frame_data(image_frame, corner_frame)
            otf_real, otf_imag = frame_optics(coeff_frame)
            cross_real = carry[0] + lax.optimization_barrier(jnp.sum(otf_real * data_real + otf_imag * data_imag, axis=2))
            cross_imag = carry[1] + lax.optimization_barrier(jnp.sum(otf_real * data_imag - otf_imag * data_real, axis=2))
            power_sum = carry[2] + lax.optimization_barrier(jnp.sum(otf_real * otf_real + otf_imag * otf_imag, axis=2))
            return ((cross_real, cross_imag, power_sum), None)
        empty = jnp.zeros(images.shape[1:3] + images.shape[4:], jnp.float32)
        sums, unused = lax.scan(accumulate, (empty, empty, empty), (images, corner_frames, coefficients))
        object_real = sums[0] / (sums[2] + noise_weight)
        object_imag = sums[1] / (sums[2] + noise_weight)

        def frame_gradient(inputs, object_real=object_real, object_imag=object_imag):
            image_frame, corner_frame, coeff_frame = inputs
            data_real, data_imag = frame_data(image_frame, corner_frame)
            (otf_real, otf_imag), pullback = jax.vjp(frame_optics, coeff_frame)
            full_real = object_real[:, :, None]
            full_imag = object_imag[:, :, None]
            res_real = data_real - (full_real * otf_real - full_imag * otf_imag)
            res_imag = data_imag - (full_real * otf_imag + full_imag * otf_real)
            cot_real = -2.0 * (res_real * full_real + res_imag * full_imag)
            cot_imag = 2.0 * (res_real * full_imag - res_imag * full_real)
            return pullback((cot_real, cot_imag))[0]
        grads = lax.map(frame_gradient, (images, corner_frames, coefficients))
        scale = jnp.sqrt(jnp.sum(grads * grads) / coefficients.size + TINY)
        padded = jnp.pad(coefficients, ((0, 0), (1, 1), (1, 1), (0, 0)))
        laplace = 4.0 * coefficients - padded[:, 2:, 1:-1] - padded[:, :-2, 1:-1] - padded[:, 1:-1, 2:] - padded[:, 1:-1, :-2]
        coefficients = coefficients - step_size * (grads / scale + smooth_weight * laplace)
    return (coefficients, jnp.stack([object_real, object_imag]))
```

```python
import functools
import math

import jax
import jax.numpy as jnp
import ml_dtypes
import numpy as np
from jax import lax
from jax.experimental import pallas as pl
from jax.experimental.pallas import tpu as pltpu
from jax.sharding import PartitionSpec as P

ITERS = 2
MODES = 36
DIVERSITY = 1.5
TINY = 1e-06
PIXELS = 128
RADIUS = 32
SIDE = 72
PAD = 80
HALF = 64
FRAMES = 4
FIELDS = 4
ITEMS = FRAMES * FIELDS
UNITS = 16
F32 = jnp.float32
BF16 = jnp.bfloat16
MESH = pl.DeviceIdType.MESH


def noll_order(mode_index):
    radial_order = (math.isqrt(8 * (mode_index - 1) + 1) - 1) // 2
    position = mode_index - radial_order * (radial_order + 1) // 2
    parity = radial_order % 2
    azimuth = (position + parity) // 2 * 2 - parity
    if azimuth != 0 and mode_index % 2 == 1:
        azimuth = -azimuth
    return (radial_order, azimuth)


def zernike():
    line = np.arange(-RADIUS, RADIUS + 1) / RADIUS
    rows, cols = np.meshgrid(line, line, indexing="ij")
    radius = np.sqrt(rows * rows + cols * cols)
    angle = np.arctan2(rows, cols)
    mask = (rows * rows + cols * cols <= 1.0).astype(np.float64)
    shapes = []
    for mode_index in range(2, MODES + 2):
        n, m = noll_order(mode_index)
        radial = np.zeros_like(radius)
        for t in range((n - abs(m)) // 2 + 1):
            factor = (-1) ** t * math.factorial(n - t)
            factor /= math.factorial(t)
            factor /= math.factorial((n + abs(m)) // 2 - t)
            factor /= math.factorial((n - abs(m)) // 2 - t)
            radial = radial + factor * radius ** (n - 2 * t)
        if m == 0:
            shape = math.sqrt(n + 1) * radial
        elif m > 0:
            shape = math.sqrt(2 * (n + 1)) * radial * np.cos(m * angle)
        else:
            shape = math.sqrt(2 * (n + 1)) * radial * np.sin(-m * angle)
        shapes.append(shape * mask)
    return np.stack(shapes), mask


def pieces(values, count):
    out = []
    rest = np.asarray(values, np.float64)
    for _ in range(count):
        piece = rest.astype(np.float32).astype(ml_dtypes.bfloat16)
        out.append(piece)
        rest = rest - piece.astype(np.float64)
    return out


def right_table(matrix):
    hi, lo = pieces(matrix, 2)
    return np.concatenate([hi, lo, hi], axis=0)


def left_table(matrix):
    hi, lo = pieces(matrix, 2)
    return np.concatenate([hi, lo, hi], axis=1)


def tables():
    basis, mask = zernike()
    lit = mask.sum()
    turn = 2.0 * math.pi / PIXELS
    freq = np.arange(PIXELS)
    half = np.arange(HALF)
    pupil = np.arange(-RADIUS, RADIUS + 1)

    ang = turn * (pupil[:, None] * freq[None, :] % PIXELS)
    w1 = np.zeros((256, 256))
    w1[:65, :128] = np.cos(ang)
    w1[:65, 128:] = -np.sin(ang)
    w1[128 : 128 + 65, :128] = np.sin(ang)
    w1[128 : 128 + 65, 128:] = np.cos(ang)

    l2 = np.zeros((128, PAD))
    ang = turn * (half[:, None] * pupil[None, :] % PIXELS)
    l2[:64, :65] = np.cos(ang)
    l2[64:, :65] = np.sin(ang)
    l2[64, :65] = np.cos(turn * (64 * pupil % PIXELS))

    ang = turn * (half[:, None] * half[None, :] % PIXELS)
    q = np.zeros((128, 128))
    q[:64, :64] = 2.0 * np.cos(ang)
    q[64:, 64:] = -2.0 * np.sin(ang)
    q[:64, 0] = 1.0
    q[:64, 64] = (-1.0) ** half
    q[64, :] = 0.0
    q[64, 1:64] = 2.0 * (-1.0) ** half[1:]
    q[64, 0] = 1.0
    q[64, 64] = 1.0
    q = q / (lit * PIXELS * PIXELS)

    weight = np.full((128,), -8.0)
    weight[0] = -4.0
    weight[64] = -4.0
    qt = q.T * weight[None, :]

    qd = np.zeros((128, 128))
    ang = turn * (half[:, None] * freq[None, :] % PIXELS)
    qd[:64] = np.cos(ang)
    qd[64:] = -np.sin(ang)
    qd[64] = (-1.0) ** freq

    ang = turn * (freq[:, None] * freq[None, :] % PIXELS)
    w4 = np.zeros((256, 256))
    w4[:128, :128] = np.cos(ang)
    w4[:128, 128:] = -np.sin(ang)
    w4[128:, :128] = np.sin(ang)
    w4[128:, 128:] = np.cos(ang)

    wide = np.zeros((MODES, SIDE, 128))
    wide[:, :65, :65] = basis
    zh, zm, zl = pieces(wide, 3)
    phase = np.zeros((256, SIDE, 128), ml_dtypes.bfloat16)
    for at, part in ((0, zh), (36, zh), (72, zm), (128, zh), (164, zl), (200, zm)):
        phase[at : at + MODES] = part
    phase = phase.reshape(256, SIDE // 2, 256).transpose(1, 0, 2)

    grad = np.zeros((SIDE, 128, 128), ml_dtypes.bfloat16)
    grad[:, :, :MODES] = zh.transpose(1, 2, 0)
    grad[:, :, 64 : 64 + MODES] = zm.transpose(1, 2, 0)
    grad = grad.reshape(SIDE // 2, 256, 128)

    lens = np.zeros((3, SIDE, 128), np.float32)
    lens[0, :65, :65] = mask
    lens[1] = np.cos(DIVERSITY * wide[2])
    lens[2] = np.sin(DIVERSITY * wide[2])

    edges = np.minimum(freq, PIXELS - 1 - freq)
    taper = np.zeros((8, 128), np.float32)
    for kind in range(4):
        width = (kind + 1) * PIXELS // 16
        taper[kind] = np.where(
            edges < width, 0.5 - 0.5 * np.cos(math.pi * (edges + 0.5) / width), 1.0
        )

    flip = np.zeros((128, 128))
    flip[(-freq) % PIXELS, freq] = 1.0
    flip = np.concatenate([flip] * 3, axis=0).astype(ml_dtypes.bfloat16)

    return dict(
        w1=right_table(w1),
        w1t=right_table(w1.T),
        l2=left_table(l2),
        l2t=left_table(l2.T),
        q=left_table(q),
        qt=left_table(qt),
        w4=right_table(w4),
        w4t=right_table(w4.T),
        qd=qd.astype(np.float32),
        phase=phase,
        grad=grad,
        lens=lens,
        taper=taper,
        flip=flip,
    )


NAMES = (
    "w1", "w1t", "l2", "l2t", "q", "qt", "w4", "w4t", "qd", "phase", "grad", "lens", "taper", "flip",
)


def sincos(x):
    k = jnp.floor(x * np.float32(1.0 / math.pi) + 0.5)
    r = x - k * np.float32(3.140625)
    r = r - k * np.float32(0.0009670257568359375)
    r = r - k * np.float32(6.2771141529083251953e-7)
    odd = k - 2.0 * jnp.floor(k * 0.5)
    sign = 1.0 - 2.0 * odd
    r2 = r * r
    s = np.float32(-2.3868346521031027639830001794722295e-8)
    for c in (
        2.7526e-6,
        -1.98408735e-4,
        8.33333114e-3,
        -1.66666667e-1,
    ):
        s = s * r2 + np.float32(c)
    s = (s * r2 * r + r) * sign
    c_ = np.float32(-2.6e-7)
    for c in (
        2.4771e-5,
        -1.38888e-3,
        4.16666e-2,
        -0.5,
        1.0,
    ):
        c_ = c_ * r2 + np.float32(c)
    return s, c_ * sign


def two(x):
    hi = x.astype(BF16)
    return hi, (x - hi.astype(F32)).astype(BF16)


def right(x, table):
    hi, lo = two(x)
    return jnp.dot(jnp.concatenate([hi, hi, lo], axis=1), table, preferred_element_type=F32)


def left(table, x):
    hi, lo = two(x)
    return jnp.dot(table, jnp.concatenate([hi, hi, lo], axis=0), preferred_element_type=F32)


def patched(whole, first):
    return jnp.concatenate([first, whole[8:]], axis=0)


def kernel(
    nf, nr, nc,
    images, corners, kinds, coefs_in, step, noise, smooth,
    w1, w1t, l2, l2t, q, qt, w4, w4t, qd, phase_tab, grad_tab, lens, taper, flip,
    coefs_out, object_out,
    coefs, halo, phase, dphase, fields, waves, otf, data, rotor, sums, parts, objs, norm1, norm2, turned,
    rs_send, rs_recv, ag_send, ag_recv, n1_send, n1_recv, n2_send, n2_recv, h_send, h_recv,
):
    me = lax.axis_index("frame")
    row = lax.axis_index("row")
    col = lax.axis_index("col")
    place = row * nc + col
    nplace = nr * nc
    per = UNITS // nf

    lanes = lax.broadcasted_iota(jnp.int32, (8, 128), 1)
    subs = lax.broadcasted_iota(jnp.int32, (8, 128), 0)
    m00 = (lanes == 0) & (subs == 0)
    m064 = (lanes == 64) & (subs == 0)

    halo[...] = jnp.zeros(halo.shape, F32)

    npeers = (nf - 1) + (nplace - 1)
    if npeers:
        barrier = pltpu.get_barrier_semaphore()

        def greet_frame(k, _):
            peer = lax.rem(me + k, nf)
            pl.semaphore_signal(barrier, inc=1, device_id={"frame": peer}, device_id_type=MESH)
            return 0

        def greet_place(k, _):
            peer = lax.rem(place + k, nplace)
            pl.semaphore_signal(
                barrier, inc=1,
                device_id={"row": peer // nc, "col": lax.rem(peer, nc)}, device_id_type=MESH,
            )
            return 0

        lax.fori_loop(1, nf, greet_frame, 0)
        lax.fori_loop(1, nplace, greet_place, 0)

    coefs[...] = jnp.zeros((16, 128), F32)
    for f in range(FRAMES):
        for s in range(FIELDS):
            coefs[pl.ds(s * 4 + f, 1), pl.ds(0, MODES)] = coefs_in[f, s // 2, pl.ds(s % 2, 1), :]

    rows64 = lax.broadcasted_iota(jnp.int32, (HALF, 128), 0).astype(F32)
    cols8 = lanes.astype(F32)

    def data_field(s, _):
        kind = kinds[s // 2, lax.rem(s, 2)]
        window = jnp.where(
            kind == 0, taper[pl.ds(0, 1), :],
            jnp.where(
                kind == 1, taper[pl.ds(1, 1), :],
                jnp.where(kind == 2, taper[pl.ds(2, 1), :], taper[pl.ds(3, 1), :]),
            ),
        )
        hi, lo = two(qd[...] * window)
        rotor[:, pl.ds(0, 128)] = hi
        rotor[:, pl.ds(128, 128)] = lo

        def data_item(f, _):
            c0 = corners[0, f, s // 2, lax.rem(s, 2)].astype(F32)
            c1 = corners[1, f, s // 2, lax.rem(s, 2)].astype(F32)
            pair = jnp.concatenate(
                [images[f, s // 2, lax.rem(s, 2), 0], images[f, s // 2, lax.rem(s, 2), 1]], axis=1
            )
            lines = jnp.dot(
                rotor[...], jnp.concatenate([pair, pair], axis=0), preferred_element_type=F32
            )
            lines = lines * jnp.concatenate([window, window], axis=1)
            cycles = rows64 * (c0 * np.float32(1.0 / PIXELS))
            cycles = cycles - jnp.floor(cycles + 0.5)
            rs, rc = sincos(cycles * np.float32(2.0 * math.pi))
            cycles = cols8 * (c1 * np.float32(1.0 / PIXELS))
            cycles = cycles - jnp.floor(cycles + 0.5)
            cs, cc = sincos(cycles * np.float32(2.0 * math.pi))
            cs = cs[:1] * np.float32(1.0 / PIXELS)
            cc = cc[:1] * np.float32(1.0 / PIXELS)
            c0h = c0 * 0.5
            alternate = (1.0 - 4.0 * jnp.abs(c0h - jnp.floor(c0h))) * np.float32(1.0 / PIXELS)
            ready = []
            middle = []
            for c in range(2):
                zr = lines[:64, c * 128 : c * 128 + 128]
                zi = lines[64:, c * 128 : c * 128 + 128]
                middle.append(jnp.sum(zi[:1], axis=1, keepdims=True) * alternate)
                zi = patched(zi, jnp.where(subs == 0, 0.0, zi[:8]))
                ready.append(jnp.concatenate([zr * rc - zi * rs, zr * rs + zi * rc], axis=1))
            spec = right(jnp.concatenate(ready, axis=0), w4[...])
            for c in range(2):
                dr = spec[c * 64 : c * 64 + 64, :128]
                di = spec[c * 64 : c * 64 + 64, 128:]
                data[s * 4 + f, pl.ds(c * 64, 64), pl.ds(0, 128)] = dr * cc - di * cs
                di = dr * cs + di * cc
                data[s * 4 + f, pl.ds(c * 64, 64), pl.ds(128, 128)] = patched(
                    di, jnp.where(m00, middle[c], di[:8])
                )
            return 0

        lax.fori_loop(0, FRAMES, data_item, 0)
        return 0

    lax.fori_loop(0, FIELDS, data_field, 0)

    if npeers:
        pl.semaphore_wait(barrier, npeers)

    def rs_copy(it, h, peer):
        return pltpu.make_async_remote_copy(
            src_ref=sums.at[it, h, pl.ds(peer * per, per)],
            dst_ref=parts.at[it, h, me],
            send_sem=rs_send.at[it, h, peer],
            recv_sem=rs_recv.at[it, h, me],
            device_id={"frame": peer}, device_id_type=MESH,
        )

    def rs_arrival(it, h, peer):
        return pltpu.make_async_remote_copy(
            src_ref=sums.at[it, h, pl.ds(me * per, per)],
            dst_ref=parts.at[it, h, peer],
            send_sem=rs_send.at[it, h, peer],
            recv_sem=rs_recv.at[it, h, peer],
            device_id={"frame": peer}, device_id_type=MESH,
        )

    def ag_copy(it, h, peer):
        return pltpu.make_async_remote_copy(
            src_ref=objs.at[it, h, pl.ds(me * per, per)],
            dst_ref=objs.at[it, h, pl.ds(me * per, per)],
            send_sem=ag_send.at[it, h, peer],
            recv_sem=ag_recv.at[it, h, me],
            device_id={"frame": peer}, device_id_type=MESH,
        )

    def ag_arrival(it, h, peer):
        return pltpu.make_async_remote_copy(
            src_ref=objs.at[it, h, pl.ds(peer * per, per)],
            dst_ref=objs.at[it, h, pl.ds(peer * per, per)],
            send_sem=ag_send.at[it, h, peer],
            recv_sem=ag_recv.at[it, h, peer],
            device_id={"frame": peer}, device_id_type=MESH,
        )

    def n1_copy(it, peer, slot):
        return pltpu.make_async_remote_copy(
            src_ref=norm1.at[it, me],
            dst_ref=norm1.at[it, slot],
            send_sem=n1_send.at[it, peer],
            recv_sem=n1_recv.at[it, slot],
            device_id={"frame": peer}, device_id_type=MESH,
        )

    def n2_copy(it, peer, slot):
        return pltpu.make_async_remote_copy(
            src_ref=norm2.at[it, place],
            dst_ref=norm2.at[it, slot],
            send_sem=n2_send.at[it, peer],
            recv_sem=n2_recv.at[it, slot],
            device_id={"row": peer // nc, "col": lax.rem(peer, nc)}, device_id_type=MESH,
        )

    def halo_copies(it):
        def one(axis, index, count, delta, src, slot):
            peer = jnp.clip(index + delta, 0, count - 1)
            there = (index + delta >= 0) & (index + delta < count)
            return there, pltpu.make_async_remote_copy(
                src_ref=src,
                dst_ref=halo.at[it, slot],
                send_sem=h_send.at[it, slot],
                recv_sem=h_recv.at[it, slot],
                device_id={axis: peer}, device_id_type=MESH,
            )

        src = halo.at[it, 4]
        out = []
        if nr > 1:
            out.append(one("row", row, nr, 1, src, 0))
            out.append(one("row", row, nr, -1, src, 1))
        if nc > 1:
            out.append(one("col", col, nc, 1, src, 2))
            out.append(one("col", col, nc, -1, src, 3))
        return out

    def halo_sides(it):
        out = []
        if nr > 1:
            out += [(0, row > 0), (1, row < nr - 1)]
        if nc > 1:
            out += [(2, col > 0), (3, col < nc - 1)]
        return out

    def each_peer(count, mine, act):
        if count > 1:
            def body(k, _):
                act(lax.rem(mine + k, count))
                return 0

            lax.fori_loop(1, count, body, 0)

    def reduce_pair(it, h):
        each_peer(nf, me, lambda peer: rs_arrival(it, h, peer).wait_recv())
        for j in range(per):
            unit = me * per + j
            total = sums[it, h, unit]

            def add(k, total):
                return total + parts[it, h, lax.rem(me + k, nf), j]

            if nf > 1:
                total = lax.fori_loop(1, nf, add, total)
            first = lax.rem(unit, 8) == 0
            real, imag, power = total[0], total[1], total[2]
            n = noise[0, 0]
            other = jnp.where(m00 & first, pltpu.roll(imag, 64, 1), power)
            objs[it, h, unit, 0] = real / (power + n)
            objs[it, h, unit, 1] = jnp.where(m064 & first, 0.0, imag / (other + n))
        each_peer(nf, me, lambda peer: ag_copy(it, h, peer).start())

    def forward(it, s, f):
        item = s * 4 + f
        sin0, cos0 = sincos(phase[pl.ds(item, SIDE, stride=16), :])
        mask = lens[0]
        cos0 = cos0 * mask
        sin0 = sin0 * mask
        cos1 = cos0 * lens[1] - sin0 * lens[2]
        sin1 = sin0 * lens[1] + cos0 * lens[2]
        fields[item, 0] = cos0
        fields[item, 1] = sin0
        fields[item, 2] = cos1
        fields[item, 3] = sin1
        none = jnp.zeros((PAD - SIDE, 256), F32)
        pupil = jnp.concatenate(
            [
                jnp.concatenate([cos0, sin0], axis=1), none,
                jnp.concatenate([cos1, sin1], axis=1), none,
            ],
            axis=0,
        )
        lines = right(pupil, w1[...])
        evens = []
        odds = []
        for c in range(2):
            wave = left(l2[...], lines[c * PAD : c * PAD + PAD])
            waves[item, c] = wave
            a, b = wave[:64, :128], wave[:64, 128:]
            e, d = wave[64:, :128], wave[64:, 128:]
            ab = a * a + b * b
            ed = e * e + d * d
            even = ab + ed
            odd = 2.0 * (a * d - b * e)
            evens.append(patched(even, jnp.where(subs == 0, ab[:8], even[:8])))
            odds.append(patched(odd, jnp.where(subs == 0, ed[:8], odd[:8])))
        spread = jnp.concatenate(
            [jnp.concatenate(evens, axis=1), jnp.concatenate(odds, axis=1)], axis=0
        )
        lines = left(q[...], spread)
        z = jnp.concatenate(
            [
                jnp.concatenate([lines[:64, c * 128 : c * 128 + 128], lines[64:, c * 128 : c * 128 + 128]], axis=1)
                for c in range(2)
            ],
            axis=0,
        )
        z = right(z, w4[...])
        otf[item] = z
        d = data[item]
        h = s // 2
        base = lax.rem(s, 2) * 8
        for t in range(8):
            cr = ci = pw = None
            for c in range(2):
                at = slice(c * 64 + t * 8, c * 64 + t * 8 + 8)
                zr, zi, dr, di = z[at, :128], z[at, 128:], d[at, :128], d[at, 128:]
                ii = zi * di
                zz = zi * zi
                im = zr * di - zi * dr
                if t == 0:
                    im = jnp.where(m00, ii, im)
                    im = jnp.where(m064, pltpu.roll(zz, 64, 1), im)
                    ii = jnp.where(m00, 0.0, ii)
                    zz = jnp.where(m00, 0.0, zz)
                re = zr * dr + ii
                p = zr * zr + zz
                cr = re if cr is None else cr + re
                ci = im if ci is None else ci + im
                pw = p if pw is None else pw + p
            sums[it, h, base + t, 0] += cr
            sums[it, h, base + t, 1] += ci
            sums[it, h, base + t, 2] += pw

    def backward(it, s, f):
        item = s * 4 + f
        h = s // 2
        base = lax.rem(s, 2) * 8
        z = otf[item]
        d = data[item]
        res = [[], []]
        for t in range(8):
            our = objs[it, h, base + t, 0]
            oui = objs[it, h, base + t, 1]
            for c in range(2):
                at = slice(c * 64 + t * 8, c * 64 + t * 8 + 8)
                zr, zi, dr, di = z[at, :128], z[at, 128:], d[at, :128], d[at, 128:]
                ii = oui * zi
                ri = oui * zr
                rr = our * zi
                if t == 0:
                    rr = jnp.where(m00, ii, rr)
                    ri = jnp.where(m00, 0.0, ri)
                    ii = jnp.where(m00, 0.0, ii)
                er = dr - (our * zr - ii)
                ei = di - (rr + ri)
                x = ei * oui
                y = ei * our
                w = er * oui
                if t == 0:
                    y = jnp.where(m00, x, y)
                    x = jnp.where(m00, 0.0, x)
                    w = jnp.where(m00, 0.0, w)
                res[c].append(jnp.concatenate([er * our + x, y - w], axis=1))
        dz = right(jnp.concatenate(res[0] + res[1], axis=0), w4t[...])
        lines = jnp.concatenate(
            [
                jnp.concatenate([dz[:64, :128], dz[64:, :128]], axis=1),
                jnp.concatenate([dz[:64, 128:], dz[64:, 128:]], axis=1),
            ],
            axis=0,
        )
        dspread = left(qt[...], lines)
        dlines = []
        for c in range(2):
            de = dspread[:64, c * 128 : c * 128 + 128]
            do = dspread[64:, c * 128 : c * 128 + 128]
            wave = waves[item, c]
            a, b = wave[:64, :128], wave[:64, 128:]
            e, d_ = wave[64:, :128], wave[64:, 128:]
            da = a * de + d_ * do
            db = b * de - e * do
            dc = e * de - b * do
            dd = d_ * de + a * do
            de8, do8 = de[:8], do[:8]
            zero = subs == 0
            da = patched(da, jnp.where(zero, a[:8] * de8, da[:8]))
            db = patched(db, jnp.where(zero, b[:8] * de8, db[:8]))
            dc = patched(dc, jnp.where(zero, e[:8] * do8, dc[:8]))
            dd = patched(dd, jnp.where(zero, d_[:8] * do8, dd[:8]))
            dwave = jnp.concatenate(
                [jnp.concatenate([da, db], axis=1), jnp.concatenate([dc, dd], axis=1)], axis=0
            )
            dlines.append(left(l2t[...], dwave))
        dpupil = right(jnp.concatenate(dlines, axis=0), w1t[...])
        total = None
        for c in range(2):
            part = (
                fields[item, 2 * c] * dpupil[c * PAD : c * PAD + SIDE, 128:]
                - fields[item, 2 * c + 1] * dpupil[c * PAD : c * PAD + SIDE, :128]
            )
            total = part if total is None else total + part
        dphase[pl.ds(item, SIDE, stride=16), :] = total

    def all_frames(act, it, s):
        def body(f, _):
            act(it, s, f)
            return 0

        lax.fori_loop(0, FRAMES, body, 0)

    def send_pair(it, h):
        each_peer(nf, me, lambda peer: rs_copy(it, h, peer).start())

    def iteration(it, _):
        halo[it, 4] = coefs[...]
        for there, copy in halo_copies(it):
            pl.when(there)(copy.start)

        cf = coefs[...]
        ch = cf.astype(BF16).astype(F32)
        cm = (cf - ch).astype(BF16).astype(F32)
        cl = (cf - ch - cm).astype(BF16).astype(F32)
        low = ch + pltpu.roll(cm, 36, 1) + pltpu.roll(ch, 72, 1)
        high = cl + pltpu.roll(ch, 36, 1) + pltpu.roll(cm, 72, 1)
        lhs = jnp.concatenate([low, high], axis=1).astype(BF16)

        def phase_rows(j, _):
            out = jnp.dot(lhs, phase_tab[j], preferred_element_type=F32)
            at = pl.multiple_of(j * 32, 32)
            phase[pl.ds(at, 16), :] = out[:, :128]
            phase[pl.ds(at + 16, 16), :] = out[:, 128:]
            return 0

        lax.fori_loop(0, SIDE // 2, phase_rows, 0)
        sums[it] = jnp.zeros(sums.shape[1:], F32)

        all_frames(forward, it, 0)
        all_frames(forward, it, 1)
        send_pair(it, 0)
        all_frames(forward, it, 2)
        reduce_pair(it, 0)
        all_frames(forward, it, 3)
        send_pair(it, 1)
        each_peer(nf, me, lambda peer: ag_arrival(it, 0, peer).wait_recv())
        all_frames(backward, it, 0)
        reduce_pair(it, 1)
        all_frames(backward, it, 1)
        each_peer(nf, me, lambda peer: ag_arrival(it, 1, peer).wait_recv())
        all_frames(backward, it, 2)
        all_frames(backward, it, 3)

        def grad_rows(j, acc):
            at = pl.multiple_of(j * 32, 32)
            x = jnp.concatenate([dphase[pl.ds(at, 16), :], dphase[pl.ds(at + 16, 16), :]], axis=1)
            hi, lo = two(x)
            return acc + jnp.dot(
                jnp.concatenate([hi, lo], axis=0), grad_tab[j], preferred_element_type=F32
            )

        acc = lax.fori_loop(0, SIDE // 2, grad_rows, jnp.zeros((32, 128), F32))
        grads = acc[:16] + pltpu.roll(acc[:16], 64, 1) + acc[16:]
        lane16 = lax.broadcasted_iota(jnp.int32, (16, 128), 1)
        grads = jnp.where(lane16 < MODES, grads, 0.0)

        sq = grads * grads
        norm1[it, me] = jnp.sum(sq[:8] + sq[8:], axis=0, keepdims=True)
        each_peer(nf, me, lambda peer: n1_copy(it, peer, me).start())
        each_peer(nf, me, lambda peer: n1_copy(it, peer, peer).wait_recv())
        norm2[it, place] = jnp.sum(norm1[it], axis=0)
        each_peer(nplace, place, lambda peer: n2_copy(it, peer, place).start())

        for slot, there in halo_sides(it):
            @pl.when(there)
            def _(slot=slot):
                pltpu.make_async_copy(halo.at[it, slot], halo.at[it, slot], h_recv.at[it, slot]).wait()

        above, below = halo[it, 0, 8:], halo[it, 1, :8]
        laplace = []
        for r in range(2):
            own = cf[r * 8 : r * 8 + 8]
            other = cf[8 - r * 8 : 16 - r * 8]
            beside = jnp.where(
                subs < 4,
                pltpu.roll(halo[it, 2, r * 8 : r * 8 + 8], 4, 0),
                pltpu.roll(halo[it, 3, r * 8 : r * 8 + 8], 4, 0),
            )
            out = 4.0 * own - other - pltpu.roll(own, 4, 0) - beside
            laplace.append(out - (above if r == 0 else below))
        laplace = jnp.concatenate(laplace, axis=0)

        each_peer(nplace, place, lambda peer: n2_copy(it, peer, peer).wait_recv())
        total = jnp.sum(jnp.sum(norm2[it], axis=0), axis=1, keepdims=True)
        count = ITEMS * MODES * nf * nplace
        scale = jnp.sqrt(total / count + TINY)
        coefs[...] = cf - step[0, 0] * (grads / scale + smooth[0, 0] * laplace)

        for h in range(2):
            each_peer(nf, me, lambda peer: rs_copy(it, h, peer).wait_send())
            each_peer(nf, me, lambda peer: ag_copy(it, h, peer).wait_send())
        each_peer(nf, me, lambda peer: n1_copy(it, peer, me).wait_send())
        each_peer(nplace, place, lambda peer: n2_copy(it, peer, place).wait_send())
        for there, copy in halo_copies(it):
            pl.when(there)(copy.wait_send)
        return 0

    lax.fori_loop(0, ITERS, iteration, 0)

    for f in range(FRAMES):
        for s in range(FIELDS):
            coefs_out[f, s // 2, pl.ds(s % 2, 1), :] = coefs[pl.ds(s * 4 + f, 1), pl.ds(0, MODES)]

    last = ITERS - 1
    for j in range(per):
        tile = me * per + j

        @pl.when(tile < 8)
        def _(j=j, tile=tile):
            for s in range(FIELDS):
                re = objs[last, s // 2, s % 2 * 8 + tile, 0]
                im = objs[last, s // 2, s % 2 * 8 + tile, 1]
                object_out[0, s // 2, s % 2, pl.ds(j * 8, 8), :] = re
                object_out[1, s // 2, s % 2, pl.ds(j * 8, 8), :] = jnp.where(m00 & (tile == 0), 0.0, im)

        @pl.when(tile >= 8)
        def _(j=j, tile=tile):
            g = tile - 8
            for s in range(FIELDS):
                base = s % 2 * 8
                for c in range(2):
                    at = (s * 2 + c) * 8
                    for i in range(1, 8):
                        turned[pl.ds(at + i, 1), :] = objs[last, s // 2, base + 7 - g, c, pl.ds(8 - i, 1), :]
                    zero = objs[last, s // 2, base + lax.rem(8 - g, 8), c, pl.ds(0, 1), :]
                    if c == 0:
                        middle = objs[last, s // 2, base, 1, pl.ds(0, 1), :]
                        middle = jnp.where(lanes[:1] == 0, middle, 0.0)
                    else:
                        middle = jnp.zeros((1, 128), F32)
                    turned[pl.ds(at, 1), :] = jnp.where(g == 0, middle, zero)
            x = turned[...]
            h = x.astype(BF16)
            rest = x - h.astype(F32)
            m = rest.astype(BF16)
            l = (rest - m.astype(F32)).astype(BF16)
            out = jnp.dot(jnp.concatenate([h, m, l], axis=1), flip[...], preferred_element_type=F32)
            for s in range(FIELDS):
                at = s * 16
                object_out[0, s // 2, s % 2, pl.ds(j * 8, 8), :] = out[at : at + 8]
                object_out[1, s // 2, s % 2, pl.ds(j * 8, 8), :] = -out[at + 8 : at + 16]


def solution(mesh):
    nf, nr, nc = (mesh.shape[name] for name in ("frame", "row", "col"))
    host = tables()
    per = UNITS // nf
    vmem = pl.BlockSpec(memory_space=pltpu.VMEM)
    smem = pl.BlockSpec(memory_space=pltpu.SMEM)

    def body(images, corners, kinds, coefs, step, noise, smooth):
        scratch = [
            pltpu.VMEM((16, 128), F32),
            pltpu.VMEM((ITERS, 5, 16, 128), F32),
            pltpu.VMEM((SIDE * 16, 128), F32),
            pltpu.VMEM((SIDE * 16, 128), F32),
            pltpu.VMEM((ITEMS, 4, SIDE, 128), F32),
            pltpu.VMEM((ITEMS, 2, 128, 256), F32),
            pltpu.VMEM((ITEMS, 128, 256), F32),
            pltpu.VMEM((ITEMS, 128, 256), F32),
            pltpu.VMEM((128, 256), BF16),
            pltpu.VMEM((ITERS, 2, UNITS, 3, 8, 128), F32),
            pltpu.VMEM((ITERS, 2, nf, per, 3, 8, 128), F32),
            pltpu.VMEM((ITERS, 2, UNITS, 2, 8, 128), F32),
            pltpu.VMEM((ITERS, nf, 1, 128), F32),
            pltpu.VMEM((ITERS, nr * nc, 1, 128), F32),
            pltpu.VMEM((HALF, 128), F32),
        ]
        dma = pltpu.SemaphoreType.DMA
        scratch += [dma((ITERS, 2, nf)) for _ in range(4)]
        scratch += [dma((ITERS, nf)) for _ in range(2)]
        scratch += [dma((ITERS, nr * nc)) for _ in range(2)]
        scratch += [dma((ITERS, 4)) for _ in range(2)]
        single = lambda x: x.reshape(1, 1)
        return pl.pallas_call(
            functools.partial(kernel, nf, nr, nc),
            out_shape=(
                jax.ShapeDtypeStruct((FRAMES, 2, 2, MODES), F32),
                jax.ShapeDtypeStruct((2, 2, 2, 8 * per, 128), F32),
            ),
            in_specs=[vmem, smem, smem, vmem, smem, smem, smem] + [vmem] * len(NAMES),
            out_specs=(vmem, vmem),
            scratch_shapes=scratch,
            compiler_params=pltpu.CompilerParams(
                collective_id=0 if nf * nr * nc > 1 else None,
                has_side_effects=True,
                vmem_limit_bytes=56 * 1024 * 1024,
            ),
        )(
            images, corners, kinds, coefs, single(step), single(noise), single(smooth),
            *[jnp.asarray(host[name]) for name in NAMES],
        )

    in_specs = (
        P("frame", "row", "col", None, None, None),
        P(None, "frame", "row", "col"),
        P("row", "col"),
        P("frame", "row", "col", None),
        P(),
        P(),
        P(),
    )
    out_specs = (P("frame", "row", "col", None), P(None, "row", "col", "frame", None))
    return jax.shard_map(body, mesh=mesh, in_specs=in_specs, out_specs=out_specs, check_vma=False)
```

```python
import functools
import math

import jax
import jax.numpy as jnp
import ml_dtypes
import numpy as np
from jax import lax
from jax.experimental import pallas as pl
from jax.experimental.pallas import tpu as pltpu
from jax.sharding import PartitionSpec as P

ITERS = 2
MODES = 36
DEGREE = 9
DIVERSITY = 1.5
TINY = 1e-06
PIXELS = 128
RADIUS = 32
SIDE = 72
PAD = 80
HALF = 64
FRAMES = 4
FIELDS = 4
ITEMS = FRAMES * FIELDS
TILES = 8
F32 = jnp.float32
BF16 = jnp.bfloat16
MESH = pl.DeviceIdType.MESH


def noll_order(mode_index):
    radial_order = (math.isqrt(8 * (mode_index - 1) + 1) - 1) // 2
    position = mode_index - radial_order * (radial_order + 1) // 2
    parity = radial_order % 2
    azimuth = (position + parity) // 2 * 2 - parity
    if azimuth != 0 and mode_index % 2 == 1:
        azimuth = -azimuth
    return (radial_order, azimuth)


def zernike():
    line = np.arange(-RADIUS, RADIUS + 1) / RADIUS
    rows, cols = np.meshgrid(line, line, indexing="ij")
    radius = np.sqrt(rows * rows + cols * cols)
    angle = np.arctan2(rows, cols)
    mask = (rows * rows + cols * cols <= 1.0).astype(np.float64)
    shapes = []
    for mode_index in range(2, MODES + 2):
        n, m = noll_order(mode_index)
        radial = np.zeros_like(radius)
        for t in range((n - abs(m)) // 2 + 1):
            factor = (-1) ** t * math.factorial(n - t)
            factor /= math.factorial(t)
            factor /= math.factorial((n + abs(m)) // 2 - t)
            factor /= math.factorial((n - abs(m)) // 2 - t)
            radial = radial + factor * radius ** (n - 2 * t)
        if m == 0:
            shape = math.sqrt(n + 1) * radial
        elif m > 0:
            shape = math.sqrt(2 * (n + 1)) * radial * np.cos(m * angle)
        else:
            shape = math.sqrt(2 * (n + 1)) * radial * np.sin(-m * angle)
        shapes.append(shape)
    return np.stack(shapes), mask


def pieces(values, count):
    out = []
    rest = np.asarray(values, np.float64)
    for _ in range(count):
        piece = rest.astype(np.float32).astype(ml_dtypes.bfloat16)
        out.append(piece)
        rest = rest - piece.astype(np.float64)
    return out


def right_table(matrix):
    hi, lo = pieces(matrix, 2)
    return np.concatenate([hi, lo, hi], axis=0)


def left_table(matrix):
    hi, lo = pieces(matrix, 2)
    return np.concatenate([hi, lo, hi], axis=1)


def tables():
    modes, mask = zernike()
    lit = mask.sum()
    turn = 2.0 * math.pi / PIXELS
    freq = np.arange(PIXELS)
    half = np.arange(HALF)
    pupil = np.arange(-RADIUS, RADIUS + 1)

    ang = turn * (pupil[:, None] * freq[None, :] % PIXELS)
    w1 = np.zeros((256, 256))
    w1[:65, :128] = np.cos(ang)
    w1[:65, 128:] = -np.sin(ang)
    w1[128 : 128 + 65, :128] = np.sin(ang)
    w1[128 : 128 + 65, 128:] = np.cos(ang)

    l2 = np.zeros((128, PAD))
    ang = turn * (half[:, None] * pupil[None, :] % PIXELS)
    l2[:64, :65] = np.cos(ang)
    l2[64:, :65] = np.sin(ang)
    l2[64, :65] = np.cos(turn * (64 * pupil % PIXELS))

    ang = turn * (half[:, None] * half[None, :] % PIXELS)
    q = np.zeros((128, 128))
    q[:64, :64] = 2.0 * np.cos(ang)
    q[64:, 64:] = -2.0 * np.sin(ang)
    q[:64, 0] = 1.0
    q[:64, 64] = (-1.0) ** half
    q[64, :] = 0.0
    q[64, 1:64] = 2.0 * (-1.0) ** half[1:]
    q[64, 0] = 1.0
    q[64, 64] = 1.0
    q = q / (lit * PIXELS * PIXELS)

    weight = np.full((128,), -8.0)
    weight[0] = -4.0
    weight[64] = -4.0
    qt = q.T * weight[None, :]

    qd = np.zeros((128, 128))
    ang = turn * (half[:, None] * freq[None, :] % PIXELS)
    qd[:64] = np.cos(ang)
    qd[64:] = -np.sin(ang)
    qd[64] = (-1.0) ** freq

    ang = turn * (freq[:, None] * freq[None, :] % PIXELS)
    w4 = np.zeros((256, 256))
    w4[:128, :128] = np.cos(ang)
    w4[:128, 128:] = -np.sin(ang)
    w4[128:, :128] = np.sin(ang)
    w4[128:, 128:] = np.cos(ang)

    rows_table = np.polynomial.legendre.legvander(pupil / RADIUS, DEGREE - 1)
    t = np.zeros((MODES, DEGREE, 128))
    t[:, :, :65] = np.einsum("ip,kpx->kix", np.linalg.pinv(rows_table), modes)
    th, tm, tl = pieces(t, 3)
    t1 = np.zeros((256, DEGREE * 128), ml_dtypes.bfloat16)
    for at, part in ((0, th), (36, th), (72, tm), (128, th), (164, tl), (200, tm)):
        t1[at : at + MODES] = part.reshape(MODES, -1)
    t2 = np.zeros((DEGREE * 128, 128), ml_dtypes.bfloat16)
    t2[:, :MODES] = th.reshape(MODES, -1).T
    t2[:, 64 : 64 + MODES] = tm.reshape(MODES, -1).T

    y = np.zeros((SIDE, 16))
    y[:65, :DEGREE] = rows_table
    yh, ym, yl = pieces(y, 3)
    y1 = np.concatenate([yh, yh, ym, yh, yl, ym], axis=1)
    y = np.zeros((16, PAD))
    y[:DEGREE, :65] = rows_table.T
    y2 = left_table(y)

    lens = np.zeros((3, SIDE, 128), np.float32)
    lens[0, :65, :65] = mask
    lens[1, :65, :65] = np.cos(DIVERSITY * modes[2] * mask)
    lens[2, :65, :65] = np.sin(DIVERSITY * modes[2] * mask)

    edges = np.minimum(freq, PIXELS - 1 - freq)
    taper = np.zeros((8, 128), np.float32)
    for kind in range(4):
        width = (kind + 1) * PIXELS // 16
        taper[kind] = np.where(
            edges < width, 0.5 - 0.5 * np.cos(math.pi * (edges + 0.5) / width), 1.0
        )

    flip = np.zeros((128, 128))
    flip[(-freq) % PIXELS, freq] = 1.0
    flip = np.concatenate([flip] * 3, axis=0).astype(ml_dtypes.bfloat16)

    return dict(
        w1=right_table(w1),
        w1t=right_table(w1.T),
        l2=left_table(l2),
        l2t=left_table(l2.T),
        q=left_table(q),
        qt=left_table(qt),
        w4=right_table(w4),
        w4t=right_table(w4.T),
        qd=qd.astype(np.float32),
        t1=t1,
        t2=t2,
        y1=y1,
        y2=y2,
        lens=lens,
        taper=taper,
        flip=flip,
    )


NAMES = (
    "w1", "w1t", "l2", "l2t", "q", "qt", "w4", "w4t", "qd", "t1", "t2", "y1", "y2", "lens", "taper", "flip",
)


def sincos(x):
    k = jnp.floor(x * np.float32(1.0 / math.pi) + 0.5)
    r = x - k * np.float32(3.140625)
    r = r - k * np.float32(0.0009670257568359375)
    r = r - k * np.float32(6.2771141529083251953e-7)
    odd = k - 2.0 * jnp.floor(k * 0.5)
    sign = 1.0 - 2.0 * odd
    r2 = r * r
    s = np.float32(-2.3868346521031027639830001794722295e-8)
    for c in (
        2.7526e-6,
        -1.98408735e-4,
        8.33333114e-3,
        -1.66666667e-1,
    ):
        s = s * r2 + np.float32(c)
    s = (s * r2 * r + r) * sign
    c_ = np.float32(-2.6e-7)
    for c in (
        2.4771e-5,
        -1.38888e-3,
        4.16666e-2,
        -0.5,
        1.0,
    ):
        c_ = c_ * r2 + np.float32(c)
    return s, c_ * sign


def two(x):
    hi = x.astype(BF16)
    return hi, (x - hi.astype(F32)).astype(BF16)


def three(x):
    hi = x.astype(BF16)
    rest = x - hi.astype(F32)
    mid = rest.astype(BF16)
    return hi, mid, (rest - mid.astype(F32)).astype(BF16)


def right(x, table):
    hi, lo = two(x)
    return jnp.dot(jnp.concatenate([hi, hi, lo], axis=1), table, preferred_element_type=F32)


def left(table, x):
    hi, lo = two(x)
    return jnp.dot(table, jnp.concatenate([hi, hi, lo], axis=0), preferred_element_type=F32)


def patched(whole, first):
    return jnp.concatenate([first, whole[8:]], axis=0)


def kernel(
    nf, nr, nc,
    images, corners, kinds, coefs_in, step, noise, smooth,
    w1, w1t, l2, l2t, q, qt, w4, w4t, qd, t1, t2, y1, y2, lens, taper, flip,
    coefs_out, object_out,
    coefs, halo, bent, dbent, fields, waves, otf, data, sums, parts, objs, norm1, norm2, turned,
    rs_send, rs_recv, ag_send, ag_recv, n1_send, n1_recv, n2_send, n2_recv, h_send, h_recv,
):
    me = lax.axis_index("frame")
    row = lax.axis_index("row")
    col = lax.axis_index("col")
    place = row * nc + col
    nplace = nr * nc
    per = 16 // nf
    own = min(per, TILES)
    owners = TILES // own
    pair = nf // 2
    chips = max(pair, 1) * nplace

    lanes = lax.broadcasted_iota(jnp.int32, (8, 128), 1)
    subs = lax.broadcasted_iota(jnp.int32, (8, 128), 0)
    m00 = (lanes == 0) & (subs == 0)
    m064 = (lanes == 64) & (subs == 0)

    def loop(first, last, act):
        def body(k, _):
            act(k)
            return 0

        if last > first:
            lax.fori_loop(first, last, body, 0)

    halo[...] = jnp.zeros(halo.shape, F32)

    def chip_at(k):
        mine = me // 2 * nplace + place
        chip = lax.rem(mine + k, chips)
        return chip // nplace * 2 + lax.rem(me, 2), lax.rem(chip, nplace)

    def there(frame, where):
        return {"frame": frame, "row": where // nc, "col": lax.rem(where, nc)}

    npeers = (nf - 1) + max(pair, 1) * (nplace - 1)
    if npeers:
        barrier = pltpu.get_barrier_semaphore()

        def greet_frame(k):
            pl.semaphore_signal(
                barrier, inc=1, device_id={"frame": lax.rem(me + k, nf)}, device_id_type=MESH
            )

        def greet_place(k):
            where = lax.rem(place + 1 + k // max(pair, 1), nplace)
            frame = lax.rem(k, max(pair, 1)) * 2 + lax.rem(me, 2)
            pl.semaphore_signal(barrier, inc=1, device_id=there(frame, where), device_id_type=MESH)

        loop(1, nf, greet_frame)
        loop(0, max(pair, 1) * (nplace - 1), greet_place)

    coefs[...] = jnp.zeros((ITEMS, 128), F32)
    bent[...] = jnp.zeros((ITEMS * 16, 128), F32)
    for f in range(FRAMES):
        for s in range(FIELDS):
            coefs[pl.ds(s * 4 + f, 1), pl.ds(0, MODES)] = coefs_in[f, s // 2, pl.ds(s % 2, 1), :]

    rows64 = lax.broadcasted_iota(jnp.int32, (HALF, 128), 0).astype(F32)
    cols8 = lanes.astype(F32)

    def data_field(s):
        r, c_ = s // 2, lax.rem(s, 2)
        kind = kinds[r, c_]
        window = jnp.where(
            kind == 0, taper[pl.ds(0, 1), :],
            jnp.where(
                kind == 1, taper[pl.ds(1, 1), :],
                jnp.where(kind == 2, taper[pl.ds(2, 1), :], taper[pl.ds(3, 1), :]),
            ),
        )
        rotor = jnp.concatenate(two(qd[...] * window), axis=1)
        both = jnp.concatenate([window, window], axis=1)
        ready = []
        middle = []
        turns = []
        for f in range(FRAMES):
            c0 = corners[0, r, c_, f].astype(F32)
            c1 = corners[1, r, c_, f].astype(F32)
            image = jnp.concatenate([images[f, r, c_, 0], images[f, r, c_, 1]], axis=1)
            lines = jnp.dot(
                rotor, jnp.concatenate([image, image], axis=0), preferred_element_type=F32
            )
            lines = lines * both
            cycles = rows64 * (c0 * np.float32(1.0 / PIXELS))
            cycles = cycles - jnp.floor(cycles + 0.5)
            rs, rc = sincos(cycles * np.float32(2.0 * math.pi))
            cycles = cols8 * (c1 * np.float32(1.0 / PIXELS))
            cycles = cycles - jnp.floor(cycles + 0.5)
            cs, cc = sincos(cycles * np.float32(2.0 * math.pi))
            turns.append((cs[:1] * np.float32(1.0 / PIXELS), cc[:1] * np.float32(1.0 / PIXELS)))
            c0h = c0 * 0.5
            alternate = (1.0 - 4.0 * jnp.abs(c0h - jnp.floor(c0h))) * np.float32(1.0 / PIXELS)
            for c in range(2):
                zr = lines[:64, c * 128 : c * 128 + 128]
                zi = lines[64:, c * 128 : c * 128 + 128]
                middle.append(jnp.sum(zi[:1], axis=1, keepdims=True) * alternate)
                zi = patched(zi, jnp.where(subs == 0, 0.0, zi[:8]))
                ready.append(jnp.concatenate([zr * rc - zi * rs, zr * rs + zi * rc], axis=1))
        spec = right(jnp.concatenate(ready, axis=0), w4[...])
        for f in range(FRAMES):
            cs, cc = turns[f]
            for c in range(2):
                at = (f * 2 + c) * 64
                dr = spec[at : at + 64, :128]
                di = spec[at : at + 64, 128:]
                data[s * 4 + f, pl.ds(c * 64, 64), pl.ds(0, 128)] = dr * cc - di * cs
                di = dr * cs + di * cc
                data[s * 4 + f, pl.ds(c * 64, 64), pl.ds(128, 128)] = patched(
                    di, jnp.where(m00, middle[f * 2 + c], di[:8])
                )

    loop(0, FIELDS, data_field)

    if npeers:
        pl.semaphore_wait(barrier, npeers)

    def remote(src, dst, send, recv, device):
        return pltpu.make_async_remote_copy(
            src_ref=src, dst_ref=dst, send_sem=send, recv_sem=recv,
            device_id=device, device_id_type=MESH,
        )

    def owner(s, k):
        return lax.rem(s, 2) * owners + k

    def rs_copy(it, s, k, slot):
        return remote(
            sums.at[it, s, pl.ds(k * own, own)], parts.at[it, s // 2, slot],
            rs_send.at[it, s, k], rs_recv.at[it, s // 2, slot], {"frame": owner(s, k)},
        )

    def send_field(it, s):
        if nf > 1:
            def act(k):
                pl.when(owner(s, k) != me)(lambda: rs_copy(it, s, k, me).start())

            loop(0, owners, act)

    def rs_arrival(it, s, peer):
        return remote(
            sums.at[it, s, pl.ds(0, own)], parts.at[it, s // 2, peer],
            rs_send.at[it, s, 0], rs_recv.at[it, s // 2, peer], {"frame": peer},
        )

    def ag_copy(it, s, k, peer):
        at = pl.ds(k * own, own)
        return remote(
            objs.at[it, s, at], objs.at[it, s, at],
            ag_send.at[it, s // 2, peer], ag_recv.at[it, s, k], {"frame": peer},
        )

    def mine(s):
        return me // owners == lax.rem(s, 2) if nf > 1 else s >= 0

    def reduce_field(it, s):
        @pl.when(mine(s))
        def _():
            k = lax.rem(me, owners)
            loop(1, nf, lambda j: rs_arrival(it, s, lax.rem(me + j, nf)).wait_recv())
            for j in range(own):
                tile = k * own + j
                total = sums[it, s, tile]
                for other in range(1, nf):
                    total = total + parts[it, s // 2, lax.rem(me + other, nf), j]
                first = tile == 0
                real, imag, power = total[0], total[1], total[2]
                n = noise[0, 0]
                other = jnp.where(m00 & first, pltpu.roll(imag, 64, 1), power)
                objs[it, s, tile, 0] = real / (power + n)
                objs[it, s, tile, 1] = jnp.where(m064 & first, 0.0, imag / (other + n))
            loop(1, nf, lambda j: ag_copy(it, s, k, lax.rem(me + j, nf)).start())

    def wait_field(it, s):
        if nf > 1:
            def act(k):
                peer = owner(s, k)
                pl.when(peer != me)(lambda: ag_copy(it, s, k, peer).wait_recv())

            loop(0, owners, act)

    def n1_copy(it, slot):
        return remote(
            norm1.at[it, lax.rem(me, 2)], norm1.at[it, slot],
            n1_send.at[it], n1_recv.at[it], {"frame": me + 1 - 2 * lax.rem(me, 2)},
        )

    def n2_copy(it, k):
        frame, where = chip_at(k)
        slot = me // 2 * nplace + place
        return remote(
            norm2.at[it, slot], norm2.at[it, slot],
            n2_send.at[it], n2_recv.at[it], there(frame, where),
        )

    def halo_copies(it):
        def one(axis, index, count, delta, slot):
            peer = jnp.clip(index + delta, 0, count - 1)
            inside = (index + delta >= 0) & (index + delta < count)
            return inside, remote(
                halo.at[it, 4], halo.at[it, slot], h_send.at[it, slot], h_recv.at[it, slot], {axis: peer}
            )

        out = []
        if nr > 1:
            out += [one("row", row, nr, 1, 0), one("row", row, nr, -1, 1)]
        if nc > 1:
            out += [one("col", col, nc, 1, 2), one("col", col, nc, -1, 3)]
        return out

    def halo_sides():
        out = []
        if nr > 1:
            out += [(0, row > 0), (1, row < nr - 1)]
        if nc > 1:
            out += [(2, col > 0), (3, col < nc - 1)]
        return out

    def forward(it, s):
        stacks = []
        for f in range(FRAMES):
            x = bent[pl.ds(pl.multiple_of((s * 4 + f) * 16, 16), 16), :]
            h, m, l = three(x)
            stacks.append(jnp.concatenate([h, m, h, l, h, m], axis=0))
        phases = jnp.dot(y1[...], jnp.concatenate(stacks, axis=1), preferred_element_type=F32)
        mask = lens[0]
        none = jnp.zeros((PAD - SIDE, 256), F32)
        pupil = []
        for f in range(FRAMES):
            item = s * 4 + f
            sin0, cos0 = sincos(phases[:, f * 128 : f * 128 + 128])
            cos0 = cos0 * mask
            sin0 = sin0 * mask
            cos1 = cos0 * lens[1] - sin0 * lens[2]
            sin1 = sin0 * lens[1] + cos0 * lens[2]
            fields[item, 0] = cos0
            fields[item, 1] = sin0
            fields[item, 2] = cos1
            fields[item, 3] = sin1
            pupil += [
                jnp.concatenate([cos0, sin0], axis=1), none,
                jnp.concatenate([cos1, sin1], axis=1), none,
            ]
        lines = right(jnp.concatenate(pupil, axis=0), w1[...])
        z = []
        for f in range(FRAMES):
            evens = []
            odds = []
            for c in range(2):
                at = (f * 2 + c) * PAD
                wave = left(l2[...], lines[at : at + PAD])
                waves[s * 4 + f, c] = wave
                a, b = wave[:64, :128], wave[:64, 128:]
                e, d = wave[64:, :128], wave[64:, 128:]
                ab = a * a + b * b
                ed = e * e + d * d
                even = ab + ed
                odd = 2.0 * (a * d - b * e)
                evens.append(patched(even, jnp.where(subs == 0, ab[:8], even[:8])))
                odds.append(patched(odd, jnp.where(subs == 0, ed[:8], odd[:8])))
            spread = jnp.concatenate(
                [jnp.concatenate(evens, axis=1), jnp.concatenate(odds, axis=1)], axis=0
            )
            half = left(q[...], spread)
            for c in range(2):
                at = slice(c * 128, c * 128 + 128)
                z.append(jnp.concatenate([half[:64, at], half[64:, at]], axis=1))
        z = right(jnp.concatenate(z, axis=0), w4[...])
        for f in range(FRAMES):
            otf[s * 4 + f] = z[f * 128 : f * 128 + 128]
        for t in range(TILES):
            cr = ci = pw = None
            for f in range(FRAMES):
                for c in range(2):
                    at = f * 128 + c * 64 + t * 8
                    zr, zi = z[at : at + 8, :128], z[at : at + 8, 128:]
                    dr = data[s * 4 + f, pl.ds(c * 64 + t * 8, 8), pl.ds(0, 128)]
                    di = data[s * 4 + f, pl.ds(c * 64 + t * 8, 8), pl.ds(128, 128)]
                    ii = zi * di
                    zz = zi * zi
                    im = zr * di - zi * dr
                    if t == 0:
                        im = jnp.where(m00, ii, im)
                        im = jnp.where(m064, pltpu.roll(zz, 64, 1), im)
                        ii = jnp.where(m00, 0.0, ii)
                        zz = jnp.where(m00, 0.0, zz)
                    re = zr * dr + ii
                    p = zr * zr + zz
                    cr = re if cr is None else cr + re
                    ci = im if ci is None else ci + im
                    pw = p if pw is None else pw + p
            sums[it, s, t, 0] = cr
            sums[it, s, t, 1] = ci
            sums[it, s, t, 2] = pw

    def backward(it, s):
        res = [[] for _ in range(2 * FRAMES)]
        for t in range(TILES):
            our = objs[it, s, t, 0]
            oui = objs[it, s, t, 1]
            for f in range(FRAMES):
                for c in range(2):
                    at = pl.ds(c * 64 + t * 8, 8)
                    item = s * 4 + f
                    zr, zi = otf[item, at, pl.ds(0, 128)], otf[item, at, pl.ds(128, 128)]
                    dr, di = data[item, at, pl.ds(0, 128)], data[item, at, pl.ds(128, 128)]
                    ii = oui * zi
                    ri = oui * zr
                    rr = our * zi
                    if t == 0:
                        rr = jnp.where(m00, ii, rr)
                        ri = jnp.where(m00, 0.0, ri)
                        ii = jnp.where(m00, 0.0, ii)
                    er = dr - (our * zr - ii)
                    ei = di - (rr + ri)
                    x = ei * oui
                    y = ei * our
                    w = er * oui
                    if t == 0:
                        y = jnp.where(m00, x, y)
                        x = jnp.where(m00, 0.0, x)
                        w = jnp.where(m00, 0.0, w)
                    res[f * 2 + c].append(jnp.concatenate([er * our + x, y - w], axis=1))
        dz = right(jnp.concatenate(sum(res, []), axis=0), w4t[...])
        dlines = []
        zero = subs == 0
        for f in range(FRAMES):
            at = f * 128
            half = jnp.concatenate(
                [
                    jnp.concatenate([dz[at : at + 64, :128], dz[at + 64 : at + 128, :128]], axis=1),
                    jnp.concatenate([dz[at : at + 64, 128:], dz[at + 64 : at + 128, 128:]], axis=1),
                ],
                axis=0,
            )
            dspread = left(qt[...], half)
            for c in range(2):
                de = dspread[:64, c * 128 : c * 128 + 128]
                do = dspread[64:, c * 128 : c * 128 + 128]
                wave = waves[s * 4 + f, c]
                a, b = wave[:64, :128], wave[:64, 128:]
                e, d = wave[64:, :128], wave[64:, 128:]
                da = a * de + d * do
                db = b * de - e * do
                dc = e * de - b * do
                dd = d * de + a * do
                de8, do8 = de[:8], do[:8]
                da = patched(da, jnp.where(zero, a[:8] * de8, da[:8]))
                db = patched(db, jnp.where(zero, b[:8] * de8, db[:8]))
                dc = patched(dc, jnp.where(zero, e[:8] * do8, dc[:8]))
                dd = patched(dd, jnp.where(zero, d[:8] * do8, dd[:8]))
                dwave = jnp.concatenate(
                    [jnp.concatenate([da, db], axis=1), jnp.concatenate([dc, dd], axis=1)], axis=0
                )
                dlines.append(left(l2t[...], dwave))
        dpupil = right(jnp.concatenate(dlines, axis=0), w1t[...])
        dphase = []
        for f in range(FRAMES):
            total = None
            for c in range(2):
                at = (f * 2 + c) * PAD
                part = (
                    fields[s * 4 + f, 2 * c] * dpupil[at : at + SIDE, 128:]
                    - fields[s * 4 + f, 2 * c + 1] * dpupil[at : at + SIDE, :128]
                )
                total = part if total is None else total + part
            dphase.append(total)
        dphase = jnp.concatenate(dphase, axis=1)
        dphase = jnp.concatenate([dphase, jnp.zeros((PAD - SIDE, FRAMES * 128), F32)], axis=0)
        out = left(y2[...], dphase)
        for f in range(FRAMES):
            dbent[pl.ds(pl.multiple_of((s * 4 + f) * 16, 16), 16), :] = out[:, f * 128 : f * 128 + 128]

    def iteration(it):
        halo[it, 4] = coefs[...]
        for inside, copy in halo_copies(it):
            pl.when(inside)(copy.start)

        cf = coefs[...]
        ch = cf.astype(BF16).astype(F32)
        cm = (cf - ch).astype(BF16).astype(F32)
        cl = (cf - ch - cm).astype(BF16).astype(F32)
        low = ch + pltpu.roll(cm, 36, 1) + pltpu.roll(ch, 72, 1)
        high = cl + pltpu.roll(ch, 36, 1) + pltpu.roll(cm, 72, 1)
        lhs = jnp.concatenate([low, high], axis=1).astype(BF16)
        out = jnp.dot(lhs, t1[...], preferred_element_type=F32)
        for i in range(DEGREE):
            bent[pl.ds(i, ITEMS, stride=16), :] = out[:, i * 128 : i * 128 + 128]

        def forward_step(s):
            forward(it, s)
            send_field(it, s)
            pl.when(s >= 2)(lambda: reduce_field(it, s - 2))

        def backward_step(s):
            pl.when(s < 2)(lambda: reduce_field(it, s + 2))
            wait_field(it, s)
            backward(it, s)

        loop(0, FIELDS, forward_step)
        loop(0, FIELDS, backward_step)

        x = jnp.concatenate([dbent[pl.ds(i, ITEMS, stride=16), :] for i in range(DEGREE)], axis=1)
        acc = jnp.dot(jnp.concatenate(two(x), axis=0), t2[...], preferred_element_type=F32)
        grads = acc[:16] + pltpu.roll(acc[:16], 64, 1) + acc[16:]
        lane16 = lax.broadcasted_iota(jnp.int32, (ITEMS, 128), 1)
        grads = jnp.where(lane16 < MODES, grads, 0.0)

        sq = grads * grads
        total = jnp.sum(sq[:8] + sq[8:], axis=0, keepdims=True)
        slot = me // 2 * nplace + place
        if nf > 1:
            norm1[it, lax.rem(me, 2)] = total
            n1_copy(it, lax.rem(me, 2)).start()
            n1_copy(it, 1 - lax.rem(me, 2)).wait_recv()
            total = norm1[it, 0] + norm1[it, 1]
        norm2[it, slot] = total
        loop(1, chips, lambda k: n2_copy(it, k).start())

        for side, inside in halo_sides():
            @pl.when(inside)
            def _(side=side):
                pltpu.make_async_copy(halo.at[it, side], halo.at[it, side], h_recv.at[it, side]).wait()

        above, below = halo[it, 0, 8:], halo[it, 1, :8]
        laplace = []
        for r in range(2):
            mine_ = cf[r * 8 : r * 8 + 8]
            other = cf[8 - r * 8 : 16 - r * 8]
            beside = jnp.where(
                subs < 4,
                pltpu.roll(halo[it, 2, r * 8 : r * 8 + 8], 4, 0),
                pltpu.roll(halo[it, 3, r * 8 : r * 8 + 8], 4, 0),
            )
            out = 4.0 * mine_ - other - pltpu.roll(mine_, 4, 0) - beside
            laplace.append(out - (above if r == 0 else below))
        laplace = jnp.concatenate(laplace, axis=0)

        if chips > 1:
            rest = pl.ds(0, chips - 1)
            pltpu.make_async_copy(norm2.at[it, rest], norm2.at[it, rest], n2_recv.at[it]).wait()
        total = jnp.sum(jnp.sum(norm2[it], axis=0), axis=1, keepdims=True)
        count = ITEMS * MODES * nf * nplace
        scale = jnp.sqrt(total / count + TINY)
        coefs[...] = cf - step[0, 0] * (grads / scale + smooth[0, 0] * laplace)

    def departures(it):
        if nf > 1:
            def field(s):
                def act(k):
                    pl.when(owner(s, k) != me)(lambda: rs_copy(it, s, k, me).wait_send())

                loop(0, owners, act)

                @pl.when(mine(s))
                def _():
                    k = lax.rem(me, owners)
                    loop(1, nf, lambda j: ag_copy(it, s, k, lax.rem(me + j, nf)).wait_send())

            loop(0, FIELDS, field)
            n1_copy(it, lax.rem(me, 2)).wait_send()
        if chips > 1:
            rest = pl.ds(0, chips - 1)
            pltpu.make_async_copy(norm2.at[it, rest], norm2.at[it, rest], n2_send.at[it]).wait()
        for inside, copy in halo_copies(it):
            pl.when(inside)(copy.wait_send)

    loop(0, ITERS, iteration)

    for f in range(FRAMES):
        for s in range(FIELDS):
            coefs_out[f, s // 2, pl.ds(s % 2, 1), :] = coefs[pl.ds(s * 4 + f, 1), pl.ds(0, MODES)]

    last = ITERS - 1
    for j in range(per):
        tile = me * per + j

        @pl.when(tile < 8)
        def _(j=j, tile=tile):
            for s in range(FIELDS):
                re = objs[last, s, tile, 0]
                im = objs[last, s, tile, 1]
                object_out[0, s // 2, s % 2, pl.ds(j * 8, 8), :] = re
                object_out[1, s // 2, s % 2, pl.ds(j * 8, 8), :] = jnp.where(m00 & (tile == 0), 0.0, im)

        @pl.when(tile >= 8)
        def _(j=j, tile=tile):
            g = tile - 8
            for s in range(FIELDS):
                for c in range(2):
                    at = (s * 2 + c) * 8
                    for i in range(1, 8):
                        turned[pl.ds(at + i, 1), :] = objs[last, s, 7 - g, c, pl.ds(8 - i, 1), :]
                    zero = objs[last, s, lax.rem(8 - g, 8), c, pl.ds(0, 1), :]
                    if c == 0:
                        middle = objs[last, s, 0, 1, pl.ds(0, 1), :]
                        middle = jnp.where(lanes[:1] == 0, middle, 0.0)
                    else:
                        middle = jnp.zeros((1, 128), F32)
                    turned[pl.ds(at, 1), :] = jnp.where(g == 0, middle, zero)
            out = jnp.dot(
                jnp.concatenate(three(turned[...]), axis=1), flip[...], preferred_element_type=F32
            )
            for s in range(FIELDS):
                at = s * 16
                object_out[0, s // 2, s % 2, pl.ds(j * 8, 8), :] = out[at : at + 8]
                object_out[1, s // 2, s % 2, pl.ds(j * 8, 8), :] = -out[at + 8 : at + 16]

    loop(0, ITERS, departures)


def solution(mesh):
    nf, nr, nc = (mesh.shape[name] for name in ("frame", "row", "col"))
    host = tables()
    per = 16 // nf
    vmem = pl.BlockSpec(memory_space=pltpu.VMEM)
    smem = pl.BlockSpec(memory_space=pltpu.SMEM)

    def body(images, corners, kinds, coefs, step, noise, smooth):
        own = min(per, TILES)
        chips = max(nf // 2, 1) * nr * nc
        scratch = [
            pltpu.VMEM((ITEMS, 128), F32),
            pltpu.VMEM((ITERS, 5, ITEMS, 128), F32),
            pltpu.VMEM((ITEMS * 16, 128), F32),
            pltpu.VMEM((ITEMS * 16, 128), F32),
            pltpu.VMEM((ITEMS, 4, SIDE, 128), F32),
            pltpu.VMEM((ITEMS, 2, 128, 256), F32),
            pltpu.VMEM((ITEMS, 128, 256), F32),
            pltpu.VMEM((ITEMS, 128, 256), F32),
            pltpu.VMEM((ITERS, FIELDS, TILES, 3, 8, 128), F32),
            pltpu.VMEM((ITERS, 2, nf, own, 3, 8, 128), F32),
            pltpu.VMEM((ITERS, FIELDS, TILES, 2, 8, 128), F32),
            pltpu.VMEM((ITERS, 2, 1, 128), F32),
            pltpu.VMEM((ITERS, chips, 1, 128), F32),
            pltpu.VMEM((HALF, 128), F32),
        ]
        dma = pltpu.SemaphoreType.DMA
        scratch += [dma((ITERS, FIELDS, TILES)), dma((ITERS, 2, nf))]
        scratch += [dma((ITERS, 2, nf)), dma((ITERS, FIELDS, TILES))]
        scratch += [dma((ITERS,)) for _ in range(4)]
        scratch += [dma((ITERS, 4)) for _ in range(2)]
        single = lambda x: x.reshape(1, 1)
        return pl.pallas_call(
            functools.partial(kernel, nf, nr, nc),
            out_shape=(
                jax.ShapeDtypeStruct((FRAMES, 2, 2, MODES), F32),
                jax.ShapeDtypeStruct((2, 2, 2, 8 * per, 128), F32),
            ),
            in_specs=[vmem, smem, smem, vmem, smem, smem, smem] + [vmem] * len(NAMES),
            out_specs=(vmem, vmem),
            scratch_shapes=scratch,
            compiler_params=pltpu.CompilerParams(
                collective_id=0 if nf * nr * nc > 1 else None,
                has_side_effects=True,
                vmem_limit_bytes=56 * 1024 * 1024,
            ),
        )(
            images, corners.transpose(0, 2, 3, 1), kinds, coefs, single(step), single(noise), single(smooth),
            *[jnp.asarray(host[name]) for name in NAMES],
        )

    in_specs = (
        P("frame", "row", "col", None, None, None),
        P(None, "frame", "row", "col"),
        P("row", "col"),
        P("frame", "row", "col", None),
        P(),
        P(),
        P(),
    )
    out_specs = (P("frame", "row", "col", None), P(None, "row", "col", "frame", None))
    return jax.shard_map(body, mesh=mesh, in_specs=in_specs, out_specs=out_specs, check_vma=False)
```

```python
import functools
import math

import jax
import jax.numpy as jnp
import ml_dtypes
import numpy as np
from jax import lax
from jax.experimental import pallas as pl
from jax.experimental.pallas import tpu as pltpu
from jax.sharding import PartitionSpec as P

ITERS = 2
MODES = 36
SKEW = 3
GROUP = 2
DEGREE = 9
TERMS = DEGREE + 1
DIVERSITY = 1.5
TINY = 1e-06
PIXELS = 128
RADIUS = 32
SIDE = 72
PAD = 80
HALF = 64
FRAMES = 4
FIELDS = 4
ITEMS = FRAMES * FIELDS
TILES = 8
F32 = jnp.float32
BF16 = jnp.bfloat16
MESH = pl.DeviceIdType.MESH


def noll_order(mode_index):
    radial_order = (math.isqrt(8 * (mode_index - 1) + 1) - 1) // 2
    position = mode_index - radial_order * (radial_order + 1) // 2
    parity = radial_order % 2
    azimuth = (position + parity) // 2 * 2 - parity
    if azimuth != 0 and mode_index % 2 == 1:
        azimuth = -azimuth
    return (radial_order, azimuth)


def zernike():
    line = np.arange(-RADIUS, RADIUS + 1) / RADIUS
    rows, cols = np.meshgrid(line, line, indexing="ij")
    radius = np.sqrt(rows * rows + cols * cols)
    angle = np.arctan2(rows, cols)
    mask = (rows * rows + cols * cols <= 1.0).astype(np.float64)
    shapes = []
    for mode_index in range(2, MODES + 2):
        n, m = noll_order(mode_index)
        radial = np.zeros_like(radius)
        for t in range((n - abs(m)) // 2 + 1):
            factor = (-1) ** t * math.factorial(n - t)
            factor /= math.factorial(t)
            factor /= math.factorial((n + abs(m)) // 2 - t)
            factor /= math.factorial((n - abs(m)) // 2 - t)
            radial = radial + factor * radius ** (n - 2 * t)
        if m == 0:
            shape = math.sqrt(n + 1) * radial
        elif m > 0:
            shape = math.sqrt(2 * (n + 1)) * radial * np.cos(m * angle)
        else:
            shape = math.sqrt(2 * (n + 1)) * radial * np.sin(-m * angle)
        shapes.append(shape)
    return np.stack(shapes), mask


def pieces(values, count):
    out = []
    rest = np.asarray(values, np.float64)
    for _ in range(count):
        piece = rest.astype(np.float32).astype(ml_dtypes.bfloat16)
        out.append(piece)
        rest = rest - piece.astype(np.float64)
    return out


def right_table(matrix):
    hi, lo = pieces(matrix, 2)
    return np.concatenate([hi, lo, hi], axis=0)


def left_table(matrix):
    hi, lo = pieces(matrix, 2)
    return np.concatenate([hi, lo, hi], axis=1)


def tables():
    modes, mask = zernike()
    lit = mask.sum()
    turn = 2.0 * math.pi / PIXELS
    freq = np.arange(PIXELS)
    half = np.arange(HALF)
    pupil = np.arange(-RADIUS, RADIUS + 1)

    ang = turn * (pupil[:64, None] * freq[None, :] % PIXELS)
    w1 = np.zeros((128, 256))
    w1[:64, :128] = np.cos(ang)
    w1[:64, 128:] = -np.sin(ang)
    w1[64:, :128] = np.sin(ang)
    w1[64:, 128:] = np.cos(ang)
    hi, lo = pieces(w1.T, 2)
    w1t = np.concatenate([np.concatenate([hi, lo], 1), np.concatenate([hi, 0 * lo], 1)], 0)
    turn65 = np.ones((8, 256), np.float32)
    turn65[1, :128] = turn65[1, 128:] = (-1.0) ** freq

    l2 = np.zeros((128, PAD))
    ang = turn * (half[:, None] * pupil[None, :] % PIXELS)
    l2[:64, :65] = np.cos(ang)
    l2[64:, :65] = np.sin(ang)
    l2[64, :65] = np.cos(turn * (64 * pupil % PIXELS))
    l2[:, 65] = l2[:, 32]

    ang = turn * (half[:, None] * half[None, :] % PIXELS)
    q = np.zeros((128, 128))
    q[:64, :64] = 2.0 * np.cos(ang)
    q[64:, 64:] = -2.0 * np.sin(ang)
    q[:64, 0] = 1.0
    q[:64, 64] = (-1.0) ** half
    q[64, :] = 0.0
    q[64, 1:64] = 2.0 * (-1.0) ** half[1:]
    q[64, 0] = 1.0
    q[64, 64] = 1.0
    q = q / (lit * PIXELS * PIXELS)

    weight = np.full((128,), -8.0)
    weight[0] = -4.0
    weight[64] = -4.0
    qt = q.T * weight[None, :]

    qd = np.zeros((128, 128))
    ang = turn * (half[:, None] * freq[None, :] % PIXELS)
    qd[:64] = np.cos(ang)
    qd[64:] = -np.sin(ang)
    qd[64] = (-1.0) ** freq

    ang = turn * (freq[:, None] * freq[None, :] % PIXELS)
    w4 = np.zeros((256, 256))
    w4[:128, :128] = np.cos(ang)
    w4[:128, 128:] = -np.sin(ang)
    w4[128:, :128] = np.sin(ang)
    w4[128:, 128:] = np.cos(ang)

    rows_table = np.polynomial.legendre.legvander(pupil / RADIUS, DEGREE - 1)
    t = np.zeros((MODES, TERMS, 128))
    t[:, :DEGREE, :64] = np.einsum("ip,kpx->kix", np.linalg.pinv(rows_table), modes)[:, :, :64]
    t[:, DEGREE, 0] = modes[:, 32, 64]
    t[:, :, 64:] = t[:, :, :64]
    th, tm, tl = pieces(t, 3)
    t1 = np.zeros((256, TERMS * 128), ml_dtypes.bfloat16)
    for at, part in ((0, th), (36, th), (72, tm), (128, th), (164, tl), (200, tm)):
        t1[at : at + MODES] = part.reshape(MODES, -1)
    t[:, :, :64] *= -1.0
    th, tm = pieces(t, 2)
    t2 = np.zeros((TERMS * 128, 128), ml_dtypes.bfloat16)
    t2[:, :MODES] = th.reshape(MODES, -1).T
    t2[:, 64 : 64 + MODES] = tm.reshape(MODES, -1).T

    y = np.zeros((SIDE, 16))
    y[:65, :DEGREE] = rows_table
    y[65, DEGREE] = 1.0
    yh, ym, yl = pieces(y, 3)
    y1 = np.concatenate([yh, yh, ym, yh, yl, ym], axis=1)
    y = np.zeros((16, PAD))
    y[:DEGREE, :65] = rows_table.T
    y[DEGREE, 65] = 1.0
    y2 = left_table(y)

    def packed(values, other):
        out = np.zeros((SIDE, 128))
        out[:65, :64] = values[:, :64]
        out[65, 0] = values[32, 64]
        out[:, 64:] = other * out[:, :64]
        return out

    lens = np.stack(
        [
            packed(mask, 1.0),
            packed(np.cos(DIVERSITY * modes[2] * mask), 1.0),
            packed(-np.sin(DIVERSITY * modes[2] * mask), -1.0),
        ]
    ).astype(np.float32)

    edges = np.minimum(freq, PIXELS - 1 - freq)
    taper = np.zeros((8, 128), np.float32)
    for kind in range(4):
        width = (kind + 1) * PIXELS // 16
        taper[kind] = np.where(
            edges < width, 0.5 - 0.5 * np.cos(math.pi * (edges + 0.5) / width), 1.0
        )

    flip = np.zeros((128, 128))
    flip[(-freq) % PIXELS, freq] = 1.0
    flip = np.concatenate([flip] * 3, axis=0).astype(ml_dtypes.bfloat16)

    return dict(
        w1=right_table(w1),
        w1t=w1t,
        turn65=turn65,
        l2=left_table(l2),
        l2t=left_table(l2.T),
        q=left_table(q),
        qt=left_table(qt),
        w4=right_table(w4),
        w4t=right_table(w4.T),
        qd=qd.astype(np.float32),
        t1=t1,
        t2=t2,
        y1=y1,
        y2=y2,
        lens=lens,
        taper=taper,
        flip=flip,
    )


NAMES = (
    "w1", "w1t", "turn65", "l2", "l2t", "q", "qt", "w4", "w4t", "qd", "t1", "t2", "y1", "y2", "lens", "taper", "flip",
)


def sincos(x):
    k = jnp.floor(x * np.float32(1.0 / math.pi) + 0.5)
    r = x - k * np.float32(3.140625)
    r = r - k * np.float32(0.0009670257568359375)
    r = r - k * np.float32(6.2771141529083251953e-7)
    odd = k - 2.0 * jnp.floor(k * 0.5)
    sign = 1.0 - 2.0 * odd
    r2 = r * r
    s = np.float32(-2.3868346521031027639830001794722295e-8)
    for c in (
        2.7526e-6,
        -1.98408735e-4,
        8.33333114e-3,
        -1.66666667e-1,
    ):
        s = s * r2 + np.float32(c)
    s = (s * r2 * r + r) * sign
    c_ = np.float32(-2.6e-7)
    for c in (
        2.4771e-5,
        -1.38888e-3,
        4.16666e-2,
        -0.5,
        1.0,
    ):
        c_ = c_ * r2 + np.float32(c)
    return s, c_ * sign


def cosine(x):
    k = jnp.floor(x * np.float32(1.0 / math.pi) + 0.5)
    r = x - k * np.float32(3.140625)
    r = r - k * np.float32(0.0009670257568359375)
    r = r - k * np.float32(6.2771141529083251953e-7)
    sign = 1.0 - 2.0 * (k - 2.0 * jnp.floor(k * 0.5))
    r2 = r * r
    out = np.float32(-2.6e-7)
    for c in (2.4771e-5, -1.38888e-3, 4.16666e-2, -0.5, 1.0):
        out = out * r2 + np.float32(c)
    return out * sign


def two(x):
    hi = x.astype(BF16)
    return hi, (x - hi.astype(F32)).astype(BF16)


def three(x):
    hi = x.astype(BF16)
    rest = x - hi.astype(F32)
    mid = rest.astype(BF16)
    return hi, mid, (rest - mid.astype(F32)).astype(BF16)


def right(x, table):
    hi, lo = two(x)
    return jnp.dot(jnp.concatenate([hi, hi, lo], axis=1), table, preferred_element_type=F32)


def left(table, x):
    hi, lo = two(x)
    return jnp.dot(table, jnp.concatenate([hi, hi, lo], axis=0), preferred_element_type=F32)


def skewed(count, ahead, first, second):
    waiting = []
    for i in range(count):
        waiting.append(first(i))
        if len(waiting) > ahead:
            second(waiting.pop(0))
    for x in waiting:
        second(x)


def patched(whole, first):
    return jnp.concatenate([first, whole[8:]], axis=0)


def kernel(
    nf, nr, nc,
    images, corners, kinds, coefs_in, step, noise, smooth,
    w1, w1t, turn65, l2, l2t, q, qt, w4, w4t, qd, t1, t2, y1, y2, lens, taper, flip,
    coefs_out, object_out,
    coefs, halo, bent, dbent, fields, waves, otf, data, sums, parts, objs, norm1, norm2, turned,
    rs_send, rs_recv, ag_send, ag_recv, n1_send, n1_recv, n2_send, n2_recv, h_send, h_recv,
):
    me = lax.axis_index("frame")
    row = lax.axis_index("row")
    col = lax.axis_index("col")
    place = row * nc + col
    nplace = nr * nc
    per = 16 // nf
    own = min(per, TILES)
    owners = TILES // own
    pair = nf // 2
    chips = max(pair, 1) * nplace

    lanes = lax.broadcasted_iota(jnp.int32, (8, 128), 1)
    subs = lax.broadcasted_iota(jnp.int32, (8, 128), 0)
    m00 = (lanes == 0) & (subs == 0)
    m064 = (lanes == 64) & (subs == 0)

    def loop(first, last, act):
        def body(k, _):
            act(k)
            return 0

        if last > first:
            lax.fori_loop(first, last, body, 0)

    halo[...] = jnp.zeros(halo.shape, F32)

    def chip_at(k):
        mine = me // 2 * nplace + place
        chip = lax.rem(mine + k, chips)
        return chip // nplace * 2 + lax.rem(me, 2), lax.rem(chip, nplace)

    def there(frame, where):
        return {"frame": frame, "row": where // nc, "col": lax.rem(where, nc)}

    npeers = (nf - 1) + max(pair, 1) * (nplace - 1)
    if npeers:
        barrier = pltpu.get_barrier_semaphore()

        def greet_frame(k):
            pl.semaphore_signal(
                barrier, inc=1, device_id={"frame": lax.rem(me + k, nf)}, device_id_type=MESH
            )

        def greet_place(k):
            where = lax.rem(place + 1 + k // max(pair, 1), nplace)
            frame = lax.rem(k, max(pair, 1)) * 2 + lax.rem(me, 2)
            pl.semaphore_signal(barrier, inc=1, device_id=there(frame, where), device_id_type=MESH)

        loop(1, nf, greet_frame)
        loop(0, max(pair, 1) * (nplace - 1), greet_place)

    coefs[...] = jnp.zeros((ITEMS, 128), F32)
    bent[...] = jnp.zeros((ITEMS * 16, 128), F32)
    for f in range(FRAMES):
        for s in range(FIELDS):
            coefs[pl.ds(s * 4 + f, 1), pl.ds(0, MODES)] = coefs_in[f, s // 2, pl.ds(s % 2, 1), :]

    rows64 = lax.broadcasted_iota(jnp.int32, (HALF, 128), 0).astype(F32)
    cols8 = lanes.astype(F32)

    def data_field(s):
        r, c_ = s // 2, lax.rem(s, 2)
        kind = kinds[r, c_]
        window = jnp.where(
            kind == 0, taper[pl.ds(0, 1), :],
            jnp.where(
                kind == 1, taper[pl.ds(1, 1), :],
                jnp.where(kind == 2, taper[pl.ds(2, 1), :], taper[pl.ds(3, 1), :]),
            ),
        )
        rotor = jnp.concatenate(two(qd[...] * window), axis=1)
        both = jnp.concatenate([window, window], axis=1)
        ready = []
        middle = []
        turns = []
        for f in range(FRAMES):
            c0 = corners[0, r, c_, f].astype(F32)
            c1 = corners[1, r, c_, f].astype(F32)
            image = jnp.concatenate([images[f, r, c_, 0], images[f, r, c_, 1]], axis=1)
            lines = jnp.dot(
                rotor, jnp.concatenate([image, image], axis=0), preferred_element_type=F32
            )
            lines = lines * both
            cycles = rows64 * (c0 * np.float32(1.0 / PIXELS))
            cycles = cycles - jnp.floor(cycles + 0.5)
            rs, rc = sincos(cycles * np.float32(2.0 * math.pi))
            cycles = cols8 * (c1 * np.float32(1.0 / PIXELS))
            cycles = cycles - jnp.floor(cycles + 0.5)
            cs, cc = sincos(cycles * np.float32(2.0 * math.pi))
            turns.append((cs[:1] * np.float32(1.0 / PIXELS), cc[:1] * np.float32(1.0 / PIXELS)))
            c0h = c0 * 0.5
            alternate = (1.0 - 4.0 * jnp.abs(c0h - jnp.floor(c0h))) * np.float32(1.0 / PIXELS)
            for c in range(2):
                zr = lines[:64, c * 128 : c * 128 + 128]
                zi = lines[64:, c * 128 : c * 128 + 128]
                middle.append(jnp.sum(zi[:1], axis=1, keepdims=True) * alternate)
                zi = patched(zi, jnp.where(subs == 0, 0.0, zi[:8]))
                ready.append(jnp.concatenate([zr * rc - zi * rs, zr * rs + zi * rc], axis=1))
        spec = right(jnp.concatenate(ready, axis=0), w4[...])
        for f in range(FRAMES):
            cs, cc = turns[f]
            for c in range(2):
                at = (f * 2 + c) * 64
                dr = spec[at : at + 64, :128]
                di = spec[at : at + 64, 128:]
                data[s * 4 + f, pl.ds(c * 64, 64), pl.ds(0, 128)] = dr * cc - di * cs
                di = dr * cs + di * cc
                data[s * 4 + f, pl.ds(c * 64, 64), pl.ds(128, 128)] = patched(
                    di, jnp.where(m00, middle[f * 2 + c], di[:8])
                )

    loop(0, FIELDS, data_field)

    def remote(src, dst, send, recv, device):
        return pltpu.make_async_remote_copy(
            src_ref=src, dst_ref=dst, send_sem=send, recv_sem=recv,
            device_id=device, device_id_type=MESH,
        )

    def owner(s, k):
        return lax.rem(s, 2) * owners + k

    def rs_copy(it, s, k, slot):
        return remote(
            sums.at[it, s, pl.ds(k * own, own)], parts.at[it, s // 2, slot],
            rs_send.at[it, s, k], rs_recv.at[it, s // 2, slot], {"frame": owner(s, k)},
        )

    def send_field(it, s):
        if nf > 1:
            def act(k):
                pl.when(owner(s, k) != me)(lambda: rs_copy(it, s, k, me).start())

            loop(0, owners, act)

    def rs_arrival(it, s, peer):
        return remote(
            sums.at[it, s, pl.ds(0, own)], parts.at[it, s // 2, peer],
            rs_send.at[it, s, 0], rs_recv.at[it, s // 2, peer], {"frame": peer},
        )

    def ag_copy(it, s, k, peer):
        at = pl.ds(k * own, own)
        return remote(
            objs.at[it, s, at], objs.at[it, s, at],
            ag_send.at[it, s // 2, peer], ag_recv.at[it, s, k], {"frame": peer},
        )

    def mine(s):
        return me // owners == lax.rem(s, 2) if nf > 1 else s >= 0

    def reduce_field(it, s):
        @pl.when(mine(s))
        def _():
            k = lax.rem(me, owners)
            loop(1, nf, lambda j: rs_arrival(it, s, lax.rem(me + j, nf)).wait_recv())
            for j in range(own):
                tile = k * own + j
                total = sums[it, s, tile]
                for other in range(1, nf):
                    total = total + parts[it, s // 2, lax.rem(me + other, nf), j]
                first = tile == 0
                real, imag, power = total[0], total[1], total[2]
                n = noise[0, 0]
                other = jnp.where(m00 & first, pltpu.roll(imag, 64, 1), power)
                objs[it, s, tile, 0] = real / (power + n)
                objs[it, s, tile, 1] = jnp.where(m064 & first, 0.0, imag / (other + n))
            loop(1, nf, lambda j: ag_copy(it, s, k, lax.rem(me + j, nf)).start())

    def wait_field(it, s):
        if nf > 1:
            def act(k):
                peer = owner(s, k)
                pl.when(peer != me)(lambda: ag_copy(it, s, k, peer).wait_recv())

            loop(0, owners, act)

    def n1_copy(it, slot):
        return remote(
            norm1.at[it, lax.rem(me, 2)], norm1.at[it, slot],
            n1_send.at[it], n1_recv.at[it], {"frame": me + 1 - 2 * lax.rem(me, 2)},
        )

    def n2_copy(it, k):
        frame, where = chip_at(k)
        slot = me // 2 * nplace + place
        return remote(
            norm2.at[it, slot], norm2.at[it, slot],
            n2_send.at[it], n2_recv.at[it], there(frame, where),
        )

    def halo_copies(it):
        def one(axis, index, count, delta, slot):
            peer = jnp.clip(index + delta, 0, count - 1)
            inside = (index + delta >= 0) & (index + delta < count)
            return inside, remote(
                halo.at[it, 4], halo.at[it, slot], h_send.at[it, slot], h_recv.at[it, slot], {axis: peer}
            )

        out = []
        if nr > 1:
            out += [one("row", row, nr, 1, 0), one("row", row, nr, -1, 1)]
        if nc > 1:
            out += [one("col", col, nc, 1, 2), one("col", col, nc, -1, 3)]
        return out

    def halo_sides():
        out = []
        if nr > 1:
            out += [(0, row > 0), (1, row < nr - 1)]
        if nc > 1:
            out += [(2, col > 0), (3, col < nc - 1)]
        return out

    def forward(it, s):
        stacks = []
        for f in range(FRAMES):
            x = bent[pl.ds(pl.multiple_of((s * 4 + f) * 16, 16), 16), :]
            h, m, l = three(x)
            stacks.append(jnp.concatenate([h, m, h, l, h, m], axis=0))
        phases = jnp.dot(y1[...], jnp.concatenate(stacks, axis=1), preferred_element_type=F32)
        quarter = jnp.where(lanes[:1] < 64, 0.0, np.float32(0.5 * math.pi))
        none = jnp.zeros((PAD - SIDE, 128), F32)
        lines = []
        for g in range(0, FRAMES, GROUP):
            pupil = []
            for f in range(g, g + GROUP):
                item = s * 4 + f
                one0 = cosine(phases[:, f * 128 : f * 128 + 128] - quarter) * lens[0]
                two0 = pltpu.roll(one0, 64, 1)
                one1 = one0 * lens[1] + two0 * lens[2]
                fields[item, 0] = two0
                fields[item, 1] = two0 * lens[1] - one0 * lens[2]
                pupil += [one0, none, one1, none]
            lines.append(right(jnp.concatenate(pupil, axis=0), w1[...]))
        lines = jnp.concatenate(lines, axis=0)
        z = []

        def first(f):
            evens = []
            odds = []
            for c in range(2):
                at = (f * 2 + c) * PAD
                wave = left(
                    l2[...],
                    jnp.concatenate(
                        [
                            lines[at : at + 64], lines[at + 64 : at + 72] * turn65[...],
                            lines[at + 72 : at + 80],
                        ],
                        axis=0,
                    ),
                )
                waves[s * 4 + f, c] = wave
                a, b = wave[:64, :128], wave[:64, 128:]
                e, d = wave[64:, :128], wave[64:, 128:]
                ab = a * a + b * b
                ed = e * e + d * d
                even = ab + ed
                odd = 2.0 * (a * d - b * e)
                evens.append(patched(even, jnp.where(subs == 0, ab[:8], even[:8])))
                odds.append(patched(odd, jnp.where(subs == 0, ed[:8], odd[:8])))
            return jnp.concatenate(
                [jnp.concatenate(evens, axis=1), jnp.concatenate(odds, axis=1)], axis=0
            )

        def second(spread):
            half = left(q[...], spread)
            for c in range(2):
                at = slice(c * 128, c * 128 + 128)
                z.append(jnp.concatenate([half[:64, at], half[64:, at]], axis=1))

        def third():
            if len(z) % (2 * GROUP) == 0:
                out.append(right(jnp.concatenate(z[-2 * GROUP :], axis=0), w4[...]))

        out = []
        skewed(FRAMES, SKEW, first, lambda x: (second(x), third()))
        z = jnp.concatenate(out, axis=0)
        for f in range(FRAMES):
            otf[s * 4 + f] = z[f * 128 : f * 128 + 128]
        for t in range(TILES):
            cr = ci = pw = None
            for f in range(FRAMES):
                for c in range(2):
                    at = f * 128 + c * 64 + t * 8
                    zr, zi = z[at : at + 8, :128], z[at : at + 8, 128:]
                    dr = data[s * 4 + f, pl.ds(c * 64 + t * 8, 8), pl.ds(0, 128)]
                    di = data[s * 4 + f, pl.ds(c * 64 + t * 8, 8), pl.ds(128, 128)]
                    ii = zi * di
                    zz = zi * zi
                    im = zr * di - zi * dr
                    if t == 0:
                        im = jnp.where(m00, ii, im)
                        im = jnp.where(m064, pltpu.roll(zz, 64, 1), im)
                        ii = jnp.where(m00, 0.0, ii)
                        zz = jnp.where(m00, 0.0, zz)
                    re = zr * dr + ii
                    p = zr * zr + zz
                    cr = re if cr is None else cr + re
                    ci = im if ci is None else ci + im
                    pw = p if pw is None else pw + p
            sums[it, s, t, 0] = cr
            sums[it, s, t, 1] = ci
            sums[it, s, t, 2] = pw

    def backward(it, s):
        dz = []
        for g in range(0, FRAMES, GROUP):
            res = [[] for _ in range(2 * GROUP)]
            for t in range(TILES):
                our = objs[it, s, t, 0]
                oui = objs[it, s, t, 1]
                oor = ooi = our * our + oui * oui
                if t == 0:
                    oor = jnp.where(m00, our * our, oor)
                    ooi = jnp.where(m00, oui * oui, ooi)
                for f in range(g, g + GROUP):
                    for c in range(2):
                        at = pl.ds(c * 64 + t * 8, 8)
                        item = s * 4 + f
                        zr, zi = otf[item, at, pl.ds(0, 128)], otf[item, at, pl.ds(128, 128)]
                        dr, di = data[item, at, pl.ds(0, 128)], data[item, at, pl.ds(128, 128)]
                        ii = di * oui
                        im = di * our - dr * oui
                        if t == 0:
                            im = jnp.where(m00, ii, im)
                            ii = jnp.where(m00, 0.0, ii)
                        real = dr * our + ii - oor * zr
                        res[(f - g) * 2 + c].append(jnp.concatenate([real, im - ooi * zi], axis=1))
            dz.append(right(jnp.concatenate(sum(res, []), axis=0), w4t[...]))
        dz = jnp.concatenate(dz, axis=0)
        dlines = []
        zero = subs == 0

        def first(f):
            at = f * 128
            half = jnp.concatenate(
                [
                    jnp.concatenate([dz[at : at + 64, :128], dz[at + 64 : at + 128, :128]], axis=1),
                    jnp.concatenate([dz[at : at + 64, 128:], dz[at + 64 : at + 128, 128:]], axis=1),
                ],
                axis=0,
            )
            dspread = left(qt[...], half)
            dwaves = []
            for c in range(2):
                de = dspread[:64, c * 128 : c * 128 + 128]
                do = dspread[64:, c * 128 : c * 128 + 128]
                wave = waves[s * 4 + f, c]
                a, b = wave[:64, :128], wave[:64, 128:]
                e, d = wave[64:, :128], wave[64:, 128:]
                da = a * de + d * do
                db = b * de - e * do
                dc = e * de - b * do
                dd = d * de + a * do
                de8, do8 = de[:8], do[:8]
                da = patched(da, jnp.where(zero, a[:8] * de8, da[:8]))
                db = patched(db, jnp.where(zero, b[:8] * de8, db[:8]))
                dc = patched(dc, jnp.where(zero, e[:8] * do8, dc[:8]))
                dd = patched(dd, jnp.where(zero, d[:8] * do8, dd[:8]))
                dwaves.append(jnp.concatenate(
                    [jnp.concatenate([da, db], axis=1), jnp.concatenate([dc, dd], axis=1)], axis=0
                ))
            return dwaves

        def second(dwaves):
            for dwave in dwaves:
                x = left(l2t[...], dwave)
                dlines.append(
                    jnp.concatenate([x[:64], x[64:72] * turn65[...], x[72:]], axis=0)
                )

        def third():
            if len(dlines) % (2 * GROUP) == 0:
                x = jnp.concatenate(dlines[-2 * GROUP :], axis=0)
                x = jnp.dot(
                    jnp.concatenate(two(x), axis=1), w1t[...], preferred_element_type=F32
                )
                dpupil.append(x[:, :128] + x[:, 128:])

        dpupil = []
        skewed(FRAMES, SKEW, first, lambda x: (second(x), third()))
        dpupil = jnp.concatenate(dpupil, axis=0)
        dphase = []
        for f in range(FRAMES):
            at = f * 2 * PAD
            dphase.append(
                fields[s * 4 + f, 0] * dpupil[at : at + SIDE]
                + fields[s * 4 + f, 1] * dpupil[at + PAD : at + PAD + SIDE]
            )
        dphase = jnp.concatenate(dphase, axis=1)
        dphase = jnp.concatenate([dphase, jnp.zeros((PAD - SIDE, FRAMES * 128), F32)], axis=0)
        out = left(y2[...], dphase)
        for f in range(FRAMES):
            dbent[pl.ds(pl.multiple_of((s * 4 + f) * 16, 16), 16), :] = out[:, f * 128 : f * 128 + 128]

    def iteration(it):
        cf = coefs[...]
        ch = cf.astype(BF16).astype(F32)
        cm = (cf - ch).astype(BF16).astype(F32)
        cl = (cf - ch - cm).astype(BF16).astype(F32)
        low = ch + pltpu.roll(cm, 36, 1) + pltpu.roll(ch, 72, 1)
        high = cl + pltpu.roll(ch, 36, 1) + pltpu.roll(cm, 72, 1)
        lhs = jnp.concatenate([low, high], axis=1).astype(BF16)
        out = jnp.dot(lhs, t1[...], preferred_element_type=F32)
        for i in range(TERMS):
            bent[pl.ds(i, ITEMS, stride=16), :] = out[:, i * 128 : i * 128 + 128]

        def forward_step(s):
            forward(it, s)
            if npeers:
                pl.when((it == 0) & (s == 0))(lambda: pl.semaphore_wait(barrier, npeers))
            send_field(it, s)
            pl.when(s >= 2)(lambda: reduce_field(it, s - 2))

        def backward_step(s):
            pl.when(s < 2)(lambda: reduce_field(it, s + 2))
            wait_field(it, s)
            backward(it, s)

        loop(0, FIELDS, forward_step)

        halo[it, 4] = cf
        for inside, copy in halo_copies(it):
            pl.when(inside)(copy.start)

        loop(0, FIELDS, backward_step)

        x = jnp.concatenate([dbent[pl.ds(i, ITEMS, stride=16), :] for i in range(TERMS)], axis=1)
        acc = jnp.dot(jnp.concatenate(two(x), axis=0), t2[...], preferred_element_type=F32)
        grads = acc[:16] + pltpu.roll(acc[:16], 64, 1) + acc[16:]
        lane16 = lax.broadcasted_iota(jnp.int32, (ITEMS, 128), 1)
        grads = jnp.where(lane16 < MODES, grads, 0.0)

        sq = grads * grads
        total = jnp.sum(sq[:8] + sq[8:], axis=0, keepdims=True)
        slot = me // 2 * nplace + place
        if nf > 1:
            norm1[it, lax.rem(me, 2)] = total
            n1_copy(it, lax.rem(me, 2)).start()
            n1_copy(it, 1 - lax.rem(me, 2)).wait_recv()
            total = norm1[it, 0] + norm1[it, 1]
        norm2[it, slot] = total
        loop(1, chips, lambda k: n2_copy(it, k).start())

        for side, inside in halo_sides():
            @pl.when(inside)
            def _(side=side):
                pltpu.make_async_copy(halo.at[it, side], halo.at[it, side], h_recv.at[it, side]).wait()

        above, below = halo[it, 0, 8:], halo[it, 1, :8]
        laplace = []
        for r in range(2):
            mine_ = cf[r * 8 : r * 8 + 8]
            other = cf[8 - r * 8 : 16 - r * 8]
            beside = jnp.where(
                subs < 4,
                pltpu.roll(halo[it, 2, r * 8 : r * 8 + 8], 4, 0),
                pltpu.roll(halo[it, 3, r * 8 : r * 8 + 8], 4, 0),
            )
            out = 4.0 * mine_ - other - pltpu.roll(mine_, 4, 0) - beside
            laplace.append(out - (above if r == 0 else below))
        laplace = jnp.concatenate(laplace, axis=0)

        if chips > 1:
            rest = pl.ds(0, chips - 1)
            pltpu.make_async_copy(norm2.at[it, rest], norm2.at[it, rest], n2_recv.at[it]).wait()
        total = jnp.sum(jnp.sum(norm2[it], axis=0), axis=1, keepdims=True)
        count = ITEMS * MODES * nf * nplace
        scale = jnp.sqrt(total / count + TINY)
        coefs[...] = cf - step[0, 0] * (grads / scale + smooth[0, 0] * laplace)

    def departures(it):
        if nf > 1:
            def field(s):
                def act(k):
                    pl.when(owner(s, k) != me)(lambda: rs_copy(it, s, k, me).wait_send())

                loop(0, owners, act)

                @pl.when(mine(s))
                def _():
                    k = lax.rem(me, owners)
                    loop(1, nf, lambda j: ag_copy(it, s, k, lax.rem(me + j, nf)).wait_send())

            loop(0, FIELDS, field)
            n1_copy(it, lax.rem(me, 2)).wait_send()
        if chips > 1:
            rest = pl.ds(0, chips - 1)
            pltpu.make_async_copy(norm2.at[it, rest], norm2.at[it, rest], n2_send.at[it]).wait()
        for inside, copy in halo_copies(it):
            pl.when(inside)(copy.wait_send)

    loop(0, ITERS, iteration)

    for f in range(FRAMES):
        for s in range(FIELDS):
            coefs_out[f, s // 2, pl.ds(s % 2, 1), :] = coefs[pl.ds(s * 4 + f, 1), pl.ds(0, MODES)]

    last = ITERS - 1
    for j in range(per):
        tile = me * per + j

        @pl.when(tile < 8)
        def _(j=j, tile=tile):
            for s in range(FIELDS):
                re = objs[last, s, tile, 0]
                im = objs[last, s, tile, 1]
                object_out[0, s // 2, s % 2, pl.ds(j * 8, 8), :] = re
                object_out[1, s // 2, s % 2, pl.ds(j * 8, 8), :] = jnp.where(m00 & (tile == 0), 0.0, im)

        @pl.when(tile >= 8)
        def _(j=j, tile=tile):
            g = tile - 8
            for s in range(FIELDS):
                for c in range(2):
                    at = (s * 2 + c) * 8
                    for i in range(1, 8):
                        turned[pl.ds(at + i, 1), :] = objs[last, s, 7 - g, c, pl.ds(8 - i, 1), :]
                    zero = objs[last, s, lax.rem(8 - g, 8), c, pl.ds(0, 1), :]
                    if c == 0:
                        middle = objs[last, s, 0, 1, pl.ds(0, 1), :]
                        middle = jnp.where(lanes[:1] == 0, middle, 0.0)
                    else:
                        middle = jnp.zeros((1, 128), F32)
                    turned[pl.ds(at, 1), :] = jnp.where(g == 0, middle, zero)
            out = jnp.dot(
                jnp.concatenate(three(turned[...]), axis=1), flip[...], preferred_element_type=F32
            )
            for s in range(FIELDS):
                at = s * 16
                object_out[0, s // 2, s % 2, pl.ds(j * 8, 8), :] = out[at : at + 8]
                object_out[1, s // 2, s % 2, pl.ds(j * 8, 8), :] = -out[at + 8 : at + 16]

    loop(0, ITERS, departures)


def solution(mesh):
    nf, nr, nc = (mesh.shape[name] for name in ("frame", "row", "col"))
    host = tables()
    per = 16 // nf
    vmem = pl.BlockSpec(memory_space=pltpu.VMEM)
    smem = pl.BlockSpec(memory_space=pltpu.SMEM)

    def body(images, corners, kinds, coefs, step, noise, smooth):
        own = min(per, TILES)
        chips = max(nf // 2, 1) * nr * nc
        scratch = [
            pltpu.VMEM((ITEMS, 128), F32),
            pltpu.VMEM((ITERS, 5, ITEMS, 128), F32),
            pltpu.VMEM((ITEMS * 16, 128), F32),
            pltpu.VMEM((ITEMS * 16, 128), F32),
            pltpu.VMEM((ITEMS, 2, SIDE, 128), F32),
            pltpu.VMEM((ITEMS, 2, 128, 256), F32),
            pltpu.VMEM((ITEMS, 128, 256), F32),
            pltpu.VMEM((ITEMS, 128, 256), F32),
            pltpu.VMEM((ITERS, FIELDS, TILES, 3, 8, 128), F32),
            pltpu.VMEM((ITERS, 2, nf, own, 3, 8, 128), F32),
            pltpu.VMEM((ITERS, FIELDS, TILES, 2, 8, 128), F32),
            pltpu.VMEM((ITERS, 2, 1, 128), F32),
            pltpu.VMEM((ITERS, chips, 1, 128), F32),
            pltpu.VMEM((HALF, 128), F32),
        ]
        dma = pltpu.SemaphoreType.DMA
        scratch += [dma((ITERS, FIELDS, TILES)), dma((ITERS, 2, nf))]
        scratch += [dma((ITERS, 2, nf)), dma((ITERS, FIELDS, TILES))]
        scratch += [dma((ITERS,)) for _ in range(4)]
        scratch += [dma((ITERS, 4)) for _ in range(2)]
        single = lambda x: x.reshape(1, 1)
        return pl.pallas_call(
            functools.partial(kernel, nf, nr, nc),
            out_shape=(
                jax.ShapeDtypeStruct((FRAMES, 2, 2, MODES), F32),
                jax.ShapeDtypeStruct((2, 2, 2, 8 * per, 128), F32),
            ),
            in_specs=[vmem, smem, smem, vmem, smem, smem, smem] + [vmem] * len(NAMES),
            out_specs=(vmem, vmem),
            scratch_shapes=scratch,
            compiler_params=pltpu.CompilerParams(
                collective_id=0 if nf * nr * nc > 1 else None,
                has_side_effects=True,
                vmem_limit_bytes=56 * 1024 * 1024,
            ),
        )(
            images, corners.transpose(0, 2, 3, 1), kinds, coefs, single(step), single(noise), single(smooth),
            *[jnp.asarray(host[name]) for name in NAMES],
        )

    in_specs = (
        P("frame", "row", "col", None, None, None),
        P(None, "frame", "row", "col"),
        P("row", "col"),
        P("frame", "row", "col", None),
        P(),
        P(),
        P(),
    )
    out_specs = (P("frame", "row", "col", None), P(None, "row", "col", "frame", None))
    return jax.shard_map(body, mesh=mesh, in_specs=in_specs, out_specs=out_specs, check_vma=False)
```

```python
import functools
import math

import jax
import jax.numpy as jnp
import ml_dtypes
import numpy as np
from jax import lax
from jax.experimental import pallas as pl
from jax.experimental.pallas import tpu as pltpu
from jax.sharding import PartitionSpec as P

ITERS = 2
MODES = 36
SKEW = 3
GROUP = 2
DEGREE = 9
TERMS = DEGREE + 1
DIVERSITY = 1.5
TINY = 1e-06
PIXELS = 128
RADIUS = 32
SIDE = 72
PAD = 80
HALF = 64
FRAMES = 4
FIELDS = 4
ITEMS = FRAMES * FIELDS
TILES = 8
F32 = jnp.float32
BF16 = jnp.bfloat16
MESH = pl.DeviceIdType.MESH


def noll_order(mode_index):
    radial_order = (math.isqrt(8 * (mode_index - 1) + 1) - 1) // 2
    position = mode_index - radial_order * (radial_order + 1) // 2
    parity = radial_order % 2
    azimuth = (position + parity) // 2 * 2 - parity
    if azimuth != 0 and mode_index % 2 == 1:
        azimuth = -azimuth
    return (radial_order, azimuth)


def zernike():
    line = np.arange(-RADIUS, RADIUS + 1) / RADIUS
    rows, cols = np.meshgrid(line, line, indexing="ij")
    radius = np.sqrt(rows * rows + cols * cols)
    angle = np.arctan2(rows, cols)
    mask = (rows * rows + cols * cols <= 1.0).astype(np.float64)
    shapes = []
    for mode_index in range(2, MODES + 2):
        n, m = noll_order(mode_index)
        radial = np.zeros_like(radius)
        for t in range((n - abs(m)) // 2 + 1):
            factor = (-1) ** t * math.factorial(n - t)
            factor /= math.factorial(t)
            factor /= math.factorial((n + abs(m)) // 2 - t)
            factor /= math.factorial((n - abs(m)) // 2 - t)
            radial = radial + factor * radius ** (n - 2 * t)
        if m == 0:
            shape = math.sqrt(n + 1) * radial
        elif m > 0:
            shape = math.sqrt(2 * (n + 1)) * radial * np.cos(m * angle)
        else:
            shape = math.sqrt(2 * (n + 1)) * radial * np.sin(-m * angle)
        shapes.append(shape)
    return np.stack(shapes), mask


def pieces(values, count):
    out = []
    rest = np.asarray(values, np.float64)
    for _ in range(count):
        piece = rest.astype(np.float32).astype(ml_dtypes.bfloat16)
        out.append(piece)
        rest = rest - piece.astype(np.float64)
    return out


def right_table(matrix):
    hi, lo = pieces(matrix, 2)
    return np.concatenate([hi, lo, hi], axis=0)


def left_table(matrix):
    hi, lo = pieces(matrix, 2)
    return np.concatenate([hi, lo, hi], axis=1)


def tables():
    modes, mask = zernike()
    lit = mask.sum()
    turn = 2.0 * math.pi / PIXELS
    freq = np.arange(PIXELS)
    half = np.arange(HALF)
    pupil = np.arange(-RADIUS, RADIUS + 1)

    ang = turn * (pupil[:64, None] * freq[None, :] % PIXELS)
    w1 = np.zeros((128, 256))
    w1[:64, :128] = np.cos(ang)
    w1[:64, 128:] = -np.sin(ang)
    w1[64:, :128] = np.sin(ang)
    w1[64:, 128:] = np.cos(ang)
    hi, lo = pieces(w1.T, 2)
    w1t = np.concatenate([np.concatenate([hi, lo], 1), np.concatenate([hi, 0 * lo], 1)], 0)
    turn65 = np.ones((8, 256), np.float32)
    turn65[1, :128] = turn65[1, 128:] = (-1.0) ** freq

    l2 = np.zeros((128, PAD))
    ang = turn * (half[:, None] * pupil[None, :] % PIXELS)
    l2[:64, :65] = np.cos(ang)
    l2[64:, :65] = np.sin(ang)
    l2[64, :65] = np.cos(turn * (64 * pupil % PIXELS))
    l2[:, 65] = l2[:, 32]

    ang = turn * (half[:, None] * half[None, :] % PIXELS)
    q = np.zeros((128, 128))
    q[:64, :64] = 2.0 * np.cos(ang)
    q[64:, 64:] = -2.0 * np.sin(ang)
    q[:64, 0] = 1.0
    q[:64, 64] = (-1.0) ** half
    q[64, :] = 0.0
    q[64, 1:64] = 2.0 * (-1.0) ** half[1:]
    q[64, 0] = 1.0
    q[64, 64] = 1.0
    q = q / (lit * PIXELS * PIXELS)

    weight = np.full((128,), -8.0)
    weight[0] = -4.0
    weight[64] = -4.0
    qt = q.T * weight[None, :]

    qd = np.zeros((128, 128))
    ang = turn * (half[:, None] * freq[None, :] % PIXELS)
    qd[:64] = np.cos(ang)
    qd[64:] = -np.sin(ang)
    qd[64] = (-1.0) ** freq

    ang = turn * (freq[:, None] * freq[None, :] % PIXELS)
    w4 = np.zeros((256, 256))
    w4[:128, :128] = np.cos(ang)
    w4[:128, 128:] = -np.sin(ang)
    w4[128:, :128] = np.sin(ang)
    w4[128:, 128:] = np.cos(ang)

    rows_table = np.polynomial.legendre.legvander(pupil / RADIUS, DEGREE - 1)
    t = np.zeros((MODES, TERMS, 128))
    t[:, :DEGREE, :64] = np.einsum("ip,kpx->kix", np.linalg.pinv(rows_table), modes)[:, :, :64]
    t[:, DEGREE, 0] = modes[:, 32, 64]
    t[:, :, 64:] = t[:, :, :64]
    th, tm, tl = pieces(t, 3)
    t1 = np.zeros((256, TERMS * 128), ml_dtypes.bfloat16)
    for at, part in ((0, th), (36, th), (72, tm), (128, th), (164, tl), (200, tm)):
        t1[at : at + MODES] = part.reshape(MODES, -1)
    t[:, :, :64] *= -1.0
    th, tm = pieces(t, 2)
    t2 = np.zeros((TERMS * 128, 128), ml_dtypes.bfloat16)
    t2[:, :MODES] = th.reshape(MODES, -1).T
    t2[:, 64 : 64 + MODES] = tm.reshape(MODES, -1).T

    y = np.zeros((SIDE, 16))
    y[:65, :DEGREE] = rows_table
    y[65, DEGREE] = 1.0
    yh, ym, yl = pieces(y, 3)
    y1 = np.concatenate([yh, yh, ym, yh, yl, ym], axis=1)
    y = np.zeros((16, PAD))
    y[:DEGREE, :65] = rows_table.T
    y[DEGREE, 65] = 1.0
    y2 = left_table(y)

    def packed(values, other):
        out = np.zeros((SIDE, 128))
        out[:65, :64] = values[:, :64]
        out[65, 0] = values[32, 64]
        out[:, 64:] = other * out[:, :64]
        return out

    lens = np.stack(
        [
            packed(mask, 1.0),
            packed(np.cos(DIVERSITY * modes[2] * mask), 1.0),
            packed(-np.sin(DIVERSITY * modes[2] * mask), -1.0),
        ]
    ).astype(np.float32)

    edges = np.minimum(freq, PIXELS - 1 - freq)
    taper = np.zeros((8, 128), np.float32)
    for kind in range(4):
        width = (kind + 1) * PIXELS // 16
        taper[kind] = np.where(
            edges < width, 0.5 - 0.5 * np.cos(math.pi * (edges + 0.5) / width), 1.0
        )

    flip = np.zeros((128, 128))
    flip[(-freq) % PIXELS, freq] = 1.0
    flip = np.concatenate([flip] * 3, axis=0).astype(ml_dtypes.bfloat16)

    return dict(
        w1=right_table(w1),
        w1t=w1t,
        turn65=turn65,
        l2=left_table(l2),
        l2t=left_table(l2.T),
        q=left_table(q),
        qt=left_table(qt),
        w4=right_table(w4),
        w4t=right_table(w4.T),
        qd=qd.astype(np.float32),
        t1=t1,
        t2=t2,
        y1=y1,
        y2=y2,
        lens=lens,
        taper=taper,
        flip=flip,
    )


NAMES = (
    "w1", "w1t", "turn65", "l2", "l2t", "q", "qt", "w4", "w4t", "qd", "t1", "t2", "y1", "y2", "lens", "taper", "flip",
)


def sincos(x):
    k = jnp.floor(x * np.float32(1.0 / math.pi) + 0.5)
    r = x - k * np.float32(3.140625)
    r = r - k * np.float32(0.0009670257568359375)
    r = r - k * np.float32(6.2771141529083251953e-7)
    odd = k - 2.0 * jnp.floor(k * 0.5)
    sign = 1.0 - 2.0 * odd
    r2 = r * r
    s = np.float32(-2.3868346521031027639830001794722295e-8)
    for c in (
        2.7526e-6,
        -1.98408735e-4,
        8.33333114e-3,
        -1.66666667e-1,
    ):
        s = s * r2 + np.float32(c)
    s = (s * r2 * r + r) * sign
    c_ = np.float32(-2.6e-7)
    for c in (
        2.4771e-5,
        -1.38888e-3,
        4.16666e-2,
        -0.5,
        1.0,
    ):
        c_ = c_ * r2 + np.float32(c)
    return s, c_ * sign


def cosine(x):
    k = jnp.floor(x * np.float32(1.0 / math.pi) + 0.5)
    r = x - k * np.float32(3.140625)
    r = r - k * np.float32(0.0009670257568359375)
    r = r - k * np.float32(6.2771141529083251953e-7)
    sign = 1.0 - 2.0 * (k - 2.0 * jnp.floor(k * 0.5))
    r2 = r * r
    out = np.float32(-2.6e-7)
    for c in (2.4771e-5, -1.38888e-3, 4.16666e-2, -0.5, 1.0):
        out = out * r2 + np.float32(c)
    return out * sign


def two(x):
    hi = x.astype(BF16)
    return hi, (x - hi.astype(F32)).astype(BF16)


def three(x):
    hi = x.astype(BF16)
    rest = x - hi.astype(F32)
    mid = rest.astype(BF16)
    return hi, mid, (rest - mid.astype(F32)).astype(BF16)


def right(x, table):
    hi, lo = two(x)
    return jnp.dot(jnp.concatenate([hi, hi, lo], axis=1), table, preferred_element_type=F32)


def left(table, x):
    hi, lo = two(x)
    return jnp.dot(table, jnp.concatenate([hi, hi, lo], axis=0), preferred_element_type=F32)


def skewed(count, ahead, first, second):
    waiting = []
    for i in range(count):
        waiting.append(first(i))
        if len(waiting) > ahead:
            second(waiting.pop(0))
    for x in waiting:
        second(x)


def patched(whole, first):
    return jnp.concatenate([first, whole[8:]], axis=0)


def kernel(
    nf, nr, nc,
    images, corners, kinds, coefs_in, step, noise, smooth,
    w1, w1t, turn65, l2, l2t, q, qt, w4, w4t, qd, t1, t2, y1, y2, lens, taper, flip,
    coefs_out, object_out,
    coefs, halo, bent, dbent, fields, waves, otf, data, sums, parts, objs, norm1, norm2, turned,
    rs_send, rs_recv, ag_send, ag_recv, n1_send, n1_recv, n2_send, n2_recv, h_send, h_recv,
):
    me = lax.axis_index("frame")
    row = lax.axis_index("row")
    col = lax.axis_index("col")
    place = row * nc + col
    nplace = nr * nc
    per = 16 // nf
    own = min(per, TILES)
    owners = TILES // own
    pair = nf // 2
    chips = max(pair, 1) * nplace

    lanes = lax.broadcasted_iota(jnp.int32, (8, 128), 1)
    subs = lax.broadcasted_iota(jnp.int32, (8, 128), 0)
    m00 = (lanes == 0) & (subs == 0)
    m064 = (lanes == 64) & (subs == 0)

    def loop(first, last, act):
        def body(k, _):
            act(k)
            return 0

        if last > first:
            lax.fori_loop(first, last, body, 0)

    halo[...] = jnp.zeros(halo.shape, F32)

    def after(index, step, count):
        moved = index + step
        return jnp.where(moved >= count, moved - count, moved)

    frames = [after(me, k, nf) for k in range(nf)]
    rows = [after(row, k, nr) for k in range(nr)]
    cols = [after(col, k, nc) for k in range(nc)]

    def far(steps):
        k, dr, dc = steps
        dy, dx = k // 2, dc * 2 + k % 2
        return min(dy, 4 - dy) + min(dr, nr - dr) + min(dx, 4 - dx)

    others = [(k, dr, dc) for k in range(max(pair, 1)) for dr in range(nr) for dc in range(nc)]
    others = sorted(others, key=far, reverse=True)
    others = [x for x in others if x != (0, 0, 0)]

    def there(steps):
        k, dr, dc = steps
        return {"frame": frames[2 * k], "row": rows[dr], "col": cols[dc]}

    npeers = (nf - 1) + max(pair, 1) * (nplace - 1)
    if npeers:
        barrier = pltpu.get_barrier_semaphore()

        for k in range(1, nf):
            pl.semaphore_signal(barrier, inc=1, device_id={"frame": frames[k]}, device_id_type=MESH)
        for x in others:
            if x[1:] != (0, 0):
                pl.semaphore_signal(barrier, inc=1, device_id=there(x), device_id_type=MESH)

    coefs[...] = jnp.zeros((ITEMS, 128), F32)
    bent[...] = jnp.zeros((ITEMS * 16, 128), F32)
    for f in range(FRAMES):
        for s in range(FIELDS):
            coefs[pl.ds(s * 4 + f, 1), pl.ds(0, MODES)] = coefs_in[f, s // 2, pl.ds(s % 2, 1), :]

    rows64 = lax.broadcasted_iota(jnp.int32, (HALF, 128), 0).astype(F32)
    cols8 = lanes.astype(F32)

    def data_field(s):
        r, c_ = s // 2, lax.rem(s, 2)
        kind = kinds[r, c_]
        window = jnp.where(
            kind == 0, taper[pl.ds(0, 1), :],
            jnp.where(
                kind == 1, taper[pl.ds(1, 1), :],
                jnp.where(kind == 2, taper[pl.ds(2, 1), :], taper[pl.ds(3, 1), :]),
            ),
        )
        rotor = jnp.concatenate(two(qd[...] * window), axis=1)
        both = jnp.concatenate([window, window], axis=1)
        ready = []
        middle = []
        turns = []
        for f in range(FRAMES):
            c0 = corners[0, r, c_, f].astype(F32)
            c1 = corners[1, r, c_, f].astype(F32)
            image = jnp.concatenate([images[f, r, c_, 0], images[f, r, c_, 1]], axis=1)
            lines = jnp.dot(
                rotor, jnp.concatenate([image, image], axis=0), preferred_element_type=F32
            )
            lines = lines * both
            cycles = rows64 * (c0 * np.float32(1.0 / PIXELS))
            cycles = cycles - jnp.floor(cycles + 0.5)
            rs, rc = sincos(cycles * np.float32(2.0 * math.pi))
            cycles = cols8 * (c1 * np.float32(1.0 / PIXELS))
            cycles = cycles - jnp.floor(cycles + 0.5)
            cs, cc = sincos(cycles * np.float32(2.0 * math.pi))
            turns.append((cs[:1] * np.float32(1.0 / PIXELS), cc[:1] * np.float32(1.0 / PIXELS)))
            c0h = c0 * 0.5
            alternate = (1.0 - 4.0 * jnp.abs(c0h - jnp.floor(c0h))) * np.float32(1.0 / PIXELS)
            for c in range(2):
                zr = lines[:64, c * 128 : c * 128 + 128]
                zi = lines[64:, c * 128 : c * 128 + 128]
                middle.append(jnp.sum(zi[:1], axis=1, keepdims=True) * alternate)
                zi = patched(zi, jnp.where(subs == 0, 0.0, zi[:8]))
                ready.append(jnp.concatenate([zr * rc - zi * rs, zr * rs + zi * rc], axis=1))
        spec = right(jnp.concatenate(ready, axis=0), w4[...])
        for f in range(FRAMES):
            cs, cc = turns[f]
            for c in range(2):
                at = (f * 2 + c) * 64
                dr = spec[at : at + 64, :128]
                di = spec[at : at + 64, 128:]
                data[s * 4 + f, pl.ds(c * 64, 64), pl.ds(0, 128)] = dr * cc - di * cs
                di = dr * cs + di * cc
                data[s * 4 + f, pl.ds(c * 64, 64), pl.ds(128, 128)] = patched(
                    di, jnp.where(m00, middle[f * 2 + c], di[:8])
                )

    loop(0, FIELDS, data_field)

    def remote(src, dst, send, recv, device):
        return pltpu.make_async_remote_copy(
            src_ref=src, dst_ref=dst, send_sem=send, recv_sem=recv,
            device_id=device, device_id_type=MESH,
        )

    def owner(s, k):
        return lax.rem(s, 2) * owners + k

    def landed(ref, sem):
        pltpu.make_async_copy(ref, ref, sem).wait()

    def mine(s):
        return me // owners == lax.rem(s, 2) if nf > 1 else s >= 0

    def send_field(it, s):
        if nf > 1:
            for k in range(owners):
                peer = owner(s, k)
                copy = remote(
                    sums.at[it, s, pl.ds(k * own, own)], parts.at[it, s // 2, me],
                    rs_send.at[it, s], rs_recv.at[it, s // 2], {"frame": peer},
                )
                pl.when(peer != me)(copy.start)

    def reduce_field(it, s):
        @pl.when(mine(s))
        def _():
            k = lax.rem(me, owners)
            if nf > 1:
                landed(parts.at[it, s // 2, pl.ds(0, nf - 1)], rs_recv.at[it, s // 2])
            for j in range(own):
                tile = k * own + j
                total = sums[it, s, tile]
                for other in range(1, nf):
                    total = total + parts[it, s // 2, frames[other], j]
                first = tile == 0
                real, imag, power = total[0], total[1], total[2]
                n = noise[0, 0]
                other = jnp.where(m00 & first, pltpu.roll(imag, 64, 1), power)
                objs[it, s, tile, 0] = real / (power + n)
                objs[it, s, tile, 1] = jnp.where(m064 & first, 0.0, imag / (other + n))
            at = pl.ds(k * own, own)
            for j in range(1, nf):
                remote(
                    objs.at[it, s, at], objs.at[it, s, at],
                    ag_send.at[it, s // 2], ag_recv.at[it, s], {"frame": frames[j]},
                ).start()

    def wait_field(it, s):
        if nf > 1:
            pl.when(mine(s))(lambda: landed(objs.at[it, s, pl.ds(0, TILES - own)], ag_recv.at[it, s]))
            pl.when(jnp.logical_not(mine(s)))(lambda: landed(objs.at[it, s], ag_recv.at[it, s]))

    def n1_copy(it, slot):
        return remote(
            norm1.at[it, lax.rem(me, 2)], norm1.at[it, slot],
            n1_send.at[it], n1_recv.at[it], {"frame": me + 1 - 2 * lax.rem(me, 2)},
        )

    def n2_copy(it, steps):
        slot = me // 2 * nplace + place
        return remote(
            norm2.at[it, slot], norm2.at[it, slot], n2_send.at[it], n2_recv.at[it], there(steps)
        )

    def halo_copies(it):
        def one(axis, index, count, delta, slot):
            peer = jnp.clip(index + delta, 0, count - 1)
            inside = (index + delta >= 0) & (index + delta < count)
            return inside, remote(
                halo.at[it, 4], halo.at[it, slot], h_send.at[it, slot], h_recv.at[it, slot], {axis: peer}
            )

        out = []
        if nr > 1:
            out += [one("row", row, nr, 1, 0), one("row", row, nr, -1, 1)]
        if nc > 1:
            out += [one("col", col, nc, 1, 2), one("col", col, nc, -1, 3)]
        return out

    def halo_sides():
        out = []
        if nr > 1:
            out += [(0, row > 0), (1, row < nr - 1)]
        if nc > 1:
            out += [(2, col > 0), (3, col < nc - 1)]
        return out

    def forward(it, s):
        stacks = []
        for f in range(FRAMES):
            x = bent[pl.ds(pl.multiple_of((s * 4 + f) * 16, 16), 16), :]
            h, m, l = three(x)
            stacks.append(jnp.concatenate([h, m, h, l, h, m], axis=0))
        phases = jnp.dot(y1[...], jnp.concatenate(stacks, axis=1), preferred_element_type=F32)
        quarter = jnp.where(lanes[:1] < 64, 0.0, np.float32(0.5 * math.pi))
        none = jnp.zeros((PAD - SIDE, 128), F32)
        lines = []
        for g in range(0, FRAMES, GROUP):
            pupil = []
            for f in range(g, g + GROUP):
                item = s * 4 + f
                one0 = cosine(phases[:, f * 128 : f * 128 + 128] - quarter) * lens[0]
                two0 = pltpu.roll(one0, 64, 1)
                one1 = one0 * lens[1] + two0 * lens[2]
                fields[item, 0] = two0
                fields[item, 1] = two0 * lens[1] - one0 * lens[2]
                pupil += [one0, none, one1, none]
            lines.append(right(jnp.concatenate(pupil, axis=0), w1[...]))
        lines = jnp.concatenate(lines, axis=0)
        z = []

        def first(f):
            evens = []
            odds = []
            for c in range(2):
                at = (f * 2 + c) * PAD
                wave = left(
                    l2[...],
                    jnp.concatenate(
                        [
                            lines[at : at + 64], lines[at + 64 : at + 72] * turn65[...],
                            lines[at + 72 : at + 80],
                        ],
                        axis=0,
                    ),
                )
                waves[s * 4 + f, c] = wave
                a, b = wave[:64, :128], wave[:64, 128:]
                e, d = wave[64:, :128], wave[64:, 128:]
                ab = a * a + b * b
                ed = e * e + d * d
                even = ab + ed
                odd = 2.0 * (a * d - b * e)
                evens.append(patched(even, jnp.where(subs == 0, ab[:8], even[:8])))
                odds.append(patched(odd, jnp.where(subs == 0, ed[:8], odd[:8])))
            return jnp.concatenate(
                [jnp.concatenate(evens, axis=1), jnp.concatenate(odds, axis=1)], axis=0
            )

        def second(spread):
            half = left(q[...], spread)
            for c in range(2):
                at = slice(c * 128, c * 128 + 128)
                z.append(jnp.concatenate([half[:64, at], half[64:, at]], axis=1))

        def third():
            if len(z) % (2 * GROUP) == 0:
                out.append(right(jnp.concatenate(z[-2 * GROUP :], axis=0), w4[...]))

        out = []
        skewed(FRAMES, SKEW, first, lambda x: (second(x), third()))
        z = jnp.concatenate(out, axis=0)
        for f in range(FRAMES):
            otf[s * 4 + f] = z[f * 128 : f * 128 + 128]
        for t in range(TILES):
            cr = ci = pw = None
            for f in range(FRAMES):
                for c in range(2):
                    at = f * 128 + c * 64 + t * 8
                    zr, zi = z[at : at + 8, :128], z[at : at + 8, 128:]
                    dr = data[s * 4 + f, pl.ds(c * 64 + t * 8, 8), pl.ds(0, 128)]
                    di = data[s * 4 + f, pl.ds(c * 64 + t * 8, 8), pl.ds(128, 128)]
                    ii = zi * di
                    zz = zi * zi
                    im = zr * di - zi * dr
                    if t == 0:
                        im = jnp.where(m00, ii, im)
                        im = jnp.where(m064, pltpu.roll(zz, 64, 1), im)
                        ii = jnp.where(m00, 0.0, ii)
                        zz = jnp.where(m00, 0.0, zz)
                    re = zr * dr + ii
                    p = zr * zr + zz
                    cr = re if cr is None else cr + re
                    ci = im if ci is None else ci + im
                    pw = p if pw is None else pw + p
            sums[it, s, t, 0] = cr
            sums[it, s, t, 1] = ci
            sums[it, s, t, 2] = pw

    def backward(it, s):
        dz = []
        for g in range(0, FRAMES, GROUP):
            res = [[] for _ in range(2 * GROUP)]
            for t in range(TILES):
                our = objs[it, s, t, 0]
                oui = objs[it, s, t, 1]
                oor = ooi = our * our + oui * oui
                if t == 0:
                    oor = jnp.where(m00, our * our, oor)
                    ooi = jnp.where(m00, oui * oui, ooi)
                for f in range(g, g + GROUP):
                    for c in range(2):
                        at = pl.ds(c * 64 + t * 8, 8)
                        item = s * 4 + f
                        zr, zi = otf[item, at, pl.ds(0, 128)], otf[item, at, pl.ds(128, 128)]
                        dr, di = data[item, at, pl.ds(0, 128)], data[item, at, pl.ds(128, 128)]
                        ii = di * oui
                        im = di * our - dr * oui
                        if t == 0:
                            im = jnp.where(m00, ii, im)
                            ii = jnp.where(m00, 0.0, ii)
                        real = dr * our + ii - oor * zr
                        res[(f - g) * 2 + c].append(jnp.concatenate([real, im - ooi * zi], axis=1))
            dz.append(right(jnp.concatenate(sum(res, []), axis=0), w4t[...]))
        dz = jnp.concatenate(dz, axis=0)
        dlines = []
        zero = subs == 0

        def first(f):
            at = f * 128
            half = jnp.concatenate(
                [
                    jnp.concatenate([dz[at : at + 64, :128], dz[at + 64 : at + 128, :128]], axis=1),
                    jnp.concatenate([dz[at : at + 64, 128:], dz[at + 64 : at + 128, 128:]], axis=1),
                ],
                axis=0,
            )
            dspread = left(qt[...], half)
            dwaves = []
            for c in range(2):
                de = dspread[:64, c * 128 : c * 128 + 128]
                do = dspread[64:, c * 128 : c * 128 + 128]
                wave = waves[s * 4 + f, c]
                a, b = wave[:64, :128], wave[:64, 128:]
                e, d = wave[64:, :128], wave[64:, 128:]
                da = a * de + d * do
                db = b * de - e * do
                dc = e * de - b * do
                dd = d * de + a * do
                de8, do8 = de[:8], do[:8]
                da = patched(da, jnp.where(zero, a[:8] * de8, da[:8]))
                db = patched(db, jnp.where(zero, b[:8] * de8, db[:8]))
                dc = patched(dc, jnp.where(zero, e[:8] * do8, dc[:8]))
                dd = patched(dd, jnp.where(zero, d[:8] * do8, dd[:8]))
                dwaves.append(jnp.concatenate(
                    [jnp.concatenate([da, db], axis=1), jnp.concatenate([dc, dd], axis=1)], axis=0
                ))
            return dwaves

        def second(dwaves):
            for dwave in dwaves:
                x = left(l2t[...], dwave)
                dlines.append(
                    jnp.concatenate([x[:64], x[64:72] * turn65[...], x[72:]], axis=0)
                )

        def third():
            if len(dlines) % (2 * GROUP) == 0:
                x = jnp.concatenate(dlines[-2 * GROUP :], axis=0)
                x = jnp.dot(
                    jnp.concatenate(two(x), axis=1), w1t[...], preferred_element_type=F32
                )
                dpupil.append(x[:, :128] + x[:, 128:])

        dpupil = []
        skewed(FRAMES, SKEW, first, lambda x: (second(x), third()))
        dpupil = jnp.concatenate(dpupil, axis=0)
        dphase = []
        for f in range(FRAMES):
            at = f * 2 * PAD
            dphase.append(
                fields[s * 4 + f, 0] * dpupil[at : at + SIDE]
                + fields[s * 4 + f, 1] * dpupil[at + PAD : at + PAD + SIDE]
            )
        dphase = jnp.concatenate(dphase, axis=1)
        dphase = jnp.concatenate([dphase, jnp.zeros((PAD - SIDE, FRAMES * 128), F32)], axis=0)
        out = left(y2[...], dphase)
        for f in range(FRAMES):
            dbent[pl.ds(pl.multiple_of((s * 4 + f) * 16, 16), 16), :] = out[:, f * 128 : f * 128 + 128]

    def iteration(it):
        cf = coefs[...]
        ch = cf.astype(BF16).astype(F32)
        cm = (cf - ch).astype(BF16).astype(F32)
        cl = (cf - ch - cm).astype(BF16).astype(F32)
        low = ch + pltpu.roll(cm, 36, 1) + pltpu.roll(ch, 72, 1)
        high = cl + pltpu.roll(ch, 36, 1) + pltpu.roll(cm, 72, 1)
        lhs = jnp.concatenate([low, high], axis=1).astype(BF16)
        out = jnp.dot(lhs, t1[...], preferred_element_type=F32)
        for i in range(TERMS):
            bent[pl.ds(i, ITEMS, stride=16), :] = out[:, i * 128 : i * 128 + 128]

        def forward_step(s):
            forward(it, s)
            if npeers:
                pl.when((it == 0) & (s == 0))(lambda: pl.semaphore_wait(barrier, npeers))
            send_field(it, s)

        def backward_step(s):
            wait_field(it, s)
            backward(it, s)

        loop(0, FIELDS, forward_step)

        halo[it, 4] = cf
        for inside, copy in halo_copies(it):
            pl.when(inside)(copy.start)

        loop(0, FIELDS, lambda s: reduce_field(it, s))
        loop(0, FIELDS, backward_step)

        x = jnp.concatenate([dbent[pl.ds(i, ITEMS, stride=16), :] for i in range(TERMS)], axis=1)
        acc = jnp.dot(jnp.concatenate(two(x), axis=0), t2[...], preferred_element_type=F32)
        grads = acc[:16] + pltpu.roll(acc[:16], 64, 1) + acc[16:]
        lane16 = lax.broadcasted_iota(jnp.int32, (ITEMS, 128), 1)
        grads = jnp.where(lane16 < MODES, grads, 0.0)

        sq = grads * grads
        total = jnp.sum(sq[:8] + sq[8:], axis=0, keepdims=True)
        slot = me // 2 * nplace + place
        if nf > 1:
            norm1[it, lax.rem(me, 2)] = total
            n1_copy(it, lax.rem(me, 2)).start()
            n1_copy(it, 1 - lax.rem(me, 2)).wait_recv()
            total = norm1[it, 0] + norm1[it, 1]
        norm2[it, slot] = total
        for x in others:
            n2_copy(it, x).start()

        for side, inside in halo_sides():
            @pl.when(inside)
            def _(side=side):
                landed(halo.at[it, side], h_recv.at[it, side])

        above, below = halo[it, 0, 8:], halo[it, 1, :8]
        laplace = []
        for r in range(2):
            mine_ = cf[r * 8 : r * 8 + 8]
            other = cf[8 - r * 8 : 16 - r * 8]
            beside = jnp.where(
                subs < 4,
                pltpu.roll(halo[it, 2, r * 8 : r * 8 + 8], 4, 0),
                pltpu.roll(halo[it, 3, r * 8 : r * 8 + 8], 4, 0),
            )
            out = 4.0 * mine_ - other - pltpu.roll(mine_, 4, 0) - beside
            laplace.append(out - (above if r == 0 else below))
        laplace = jnp.concatenate(laplace, axis=0)

        if chips > 1:
            landed(norm2.at[it, pl.ds(0, chips - 1)], n2_recv.at[it])
        total = jnp.sum(jnp.sum(norm2[it], axis=0), axis=1, keepdims=True)
        count = ITEMS * MODES * nf * nplace
        scale = jnp.sqrt(total / count + TINY)
        coefs[...] = cf - step[0, 0] * (grads / scale + smooth[0, 0] * laplace)

    def departures(it):
        if nf > 1:
            def field(s):
                @pl.when(mine(s))
                def _():
                    if own < TILES:
                        landed(sums.at[it, s, pl.ds(0, TILES - own)], rs_send.at[it, s])
                    landed(parts.at[it, s // 2, pl.ds(0, nf - 1), :, pl.ds(0, 2)], ag_send.at[it, s // 2])

                pl.when(jnp.logical_not(mine(s)))(lambda: landed(sums.at[it, s], rs_send.at[it, s]))

            loop(0, FIELDS, field)
            n1_copy(it, lax.rem(me, 2)).wait_send()
        if chips > 1:
            landed(norm2.at[it, pl.ds(0, chips - 1)], n2_send.at[it])
        for inside, copy in halo_copies(it):
            pl.when(inside)(copy.wait_send)

    loop(0, ITERS, iteration)

    for f in range(FRAMES):
        for s in range(FIELDS):
            coefs_out[f, s // 2, pl.ds(s % 2, 1), :] = coefs[pl.ds(s * 4 + f, 1), pl.ds(0, MODES)]

    last = ITERS - 1
    for j in range(per):
        tile = me * per + j

        @pl.when(tile < 8)
        def _(j=j, tile=tile):
            for s in range(FIELDS):
                re = objs[last, s, tile, 0]
                im = objs[last, s, tile, 1]
                object_out[0, s // 2, s % 2, pl.ds(j * 8, 8), :] = re
                object_out[1, s // 2, s % 2, pl.ds(j * 8, 8), :] = jnp.where(m00 & (tile == 0), 0.0, im)

        @pl.when(tile >= 8)
        def _(j=j, tile=tile):
            g = tile - 8
            for s in range(FIELDS):
                for c in range(2):
                    at = (s * 2 + c) * 8
                    for i in range(1, 8):
                        turned[pl.ds(at + i, 1), :] = objs[last, s, 7 - g, c, pl.ds(8 - i, 1), :]
                    zero = objs[last, s, lax.rem(8 - g, 8), c, pl.ds(0, 1), :]
                    if c == 0:
                        middle = objs[last, s, 0, 1, pl.ds(0, 1), :]
                        middle = jnp.where(lanes[:1] == 0, middle, 0.0)
                    else:
                        middle = jnp.zeros((1, 128), F32)
                    turned[pl.ds(at, 1), :] = jnp.where(g == 0, middle, zero)
            out = jnp.dot(
                jnp.concatenate(three(turned[...]), axis=1), flip[...], preferred_element_type=F32
            )
            for s in range(FIELDS):
                at = s * 16
                object_out[0, s // 2, s % 2, pl.ds(j * 8, 8), :] = out[at : at + 8]
                object_out[1, s // 2, s % 2, pl.ds(j * 8, 8), :] = -out[at + 8 : at + 16]

    loop(0, ITERS, departures)


def solution(mesh):
    nf, nr, nc = (mesh.shape[name] for name in ("frame", "row", "col"))
    host = tables()
    per = 16 // nf
    vmem = pl.BlockSpec(memory_space=pltpu.VMEM)
    smem = pl.BlockSpec(memory_space=pltpu.SMEM)

    def body(images, corners, kinds, coefs, step, noise, smooth):
        own = min(per, TILES)
        chips = max(nf // 2, 1) * nr * nc
        scratch = [
            pltpu.VMEM((ITEMS, 128), F32),
            pltpu.VMEM((ITERS, 5, ITEMS, 128), F32),
            pltpu.VMEM((ITEMS * 16, 128), F32),
            pltpu.VMEM((ITEMS * 16, 128), F32),
            pltpu.VMEM((ITEMS, 2, SIDE, 128), F32),
            pltpu.VMEM((ITEMS, 2, 128, 256), F32),
            pltpu.VMEM((ITEMS, 128, 256), F32),
            pltpu.VMEM((ITEMS, 128, 256), F32),
            pltpu.VMEM((ITERS, FIELDS, TILES, 3, 8, 128), F32),
            pltpu.VMEM((ITERS, 2, nf, own, 3, 8, 128), F32),
            pltpu.VMEM((ITERS, FIELDS, TILES, 2, 8, 128), F32),
            pltpu.VMEM((ITERS, 2, 1, 128), F32),
            pltpu.VMEM((ITERS, chips, 1, 128), F32),
            pltpu.VMEM((HALF, 128), F32),
        ]
        dma = pltpu.SemaphoreType.DMA
        scratch += [dma((ITERS, FIELDS)), dma((ITERS, 2)), dma((ITERS, 2)), dma((ITERS, FIELDS))]
        scratch += [dma((ITERS,)) for _ in range(4)]
        scratch += [dma((ITERS, 4)) for _ in range(2)]
        single = lambda x: x.reshape(1, 1)
        return pl.pallas_call(
            functools.partial(kernel, nf, nr, nc),
            out_shape=(
                jax.ShapeDtypeStruct((FRAMES, 2, 2, MODES), F32),
                jax.ShapeDtypeStruct((2, 2, 2, 8 * per, 128), F32),
            ),
            in_specs=[vmem, smem, smem, vmem, smem, smem, smem] + [vmem] * len(NAMES),
            out_specs=(vmem, vmem),
            scratch_shapes=scratch,
            compiler_params=pltpu.CompilerParams(
                collective_id=0 if nf * nr * nc > 1 else None,
                has_side_effects=True,
                vmem_limit_bytes=56 * 1024 * 1024,
            ),
        )(
            images, corners.transpose(0, 2, 3, 1), kinds, coefs, single(step), single(noise), single(smooth),
            *[jnp.asarray(host[name]) for name in NAMES],
        )

    in_specs = (
        P("frame", "row", "col", None, None, None),
        P(None, "frame", "row", "col"),
        P("row", "col"),
        P("frame", "row", "col", None),
        P(),
        P(),
        P(),
    )
    out_specs = (P("frame", "row", "col", None), P(None, "row", "col", "frame", None))
    return jax.shard_map(body, mesh=mesh, in_specs=in_specs, out_specs=out_specs, check_vma=False)
```

```python
import functools
import math

import jax
import jax.numpy as jnp
import ml_dtypes
import numpy as np
from jax import lax
from jax.experimental import pallas as pl
from jax.experimental.pallas import tpu as pltpu
from jax.sharding import PartitionSpec as P

ITERS = 2
MODES = 36
SKEW = 3
ORDER = (
    ("r", 0), ("w", 0), ("r", 1), ("w", 1), ("q", 0), ("q", 1), ("q", 2), ("q", 3),
    ("l", 0), ("l", 1), ("v", 0), ("l", 2), ("l", 3), ("v", 1),
)
GROUP = 2
DEGREE = 9
TERMS = DEGREE + 1
DIVERSITY = 1.5
TINY = 1e-06
PIXELS = 128
RADIUS = 32
SIDE = 72
PAD = 80
HALF = 64
FRAMES = 4
FIELDS = 4
ITEMS = FRAMES * FIELDS
TILES = 8
F32 = jnp.float32
BF16 = jnp.bfloat16
MESH = pl.DeviceIdType.MESH


def noll_order(mode_index):
    radial_order = (math.isqrt(8 * (mode_index - 1) + 1) - 1) // 2
    position = mode_index - radial_order * (radial_order + 1) // 2
    parity = radial_order % 2
    azimuth = (position + parity) // 2 * 2 - parity
    if azimuth != 0 and mode_index % 2 == 1:
        azimuth = -azimuth
    return (radial_order, azimuth)


def zernike():
    line = np.arange(-RADIUS, RADIUS + 1) / RADIUS
    rows, cols = np.meshgrid(line, line, indexing="ij")
    radius = np.sqrt(rows * rows + cols * cols)
    angle = np.arctan2(rows, cols)
    mask = (rows * rows + cols * cols <= 1.0).astype(np.float64)
    shapes = []
    for mode_index in range(2, MODES + 2):
        n, m = noll_order(mode_index)
        radial = np.zeros_like(radius)
        for t in range((n - abs(m)) // 2 + 1):
            factor = (-1) ** t * math.factorial(n - t)
            factor /= math.factorial(t)
            factor /= math.factorial((n + abs(m)) // 2 - t)
            factor /= math.factorial((n - abs(m)) // 2 - t)
            radial = radial + factor * radius ** (n - 2 * t)
        if m == 0:
            shape = math.sqrt(n + 1) * radial
        elif m > 0:
            shape = math.sqrt(2 * (n + 1)) * radial * np.cos(m * angle)
        else:
            shape = math.sqrt(2 * (n + 1)) * radial * np.sin(-m * angle)
        shapes.append(shape)
    return np.stack(shapes), mask


def pieces(values, count):
    out = []
    rest = np.asarray(values, np.float64)
    for _ in range(count):
        piece = rest.astype(np.float32).astype(ml_dtypes.bfloat16)
        out.append(piece)
        rest = rest - piece.astype(np.float64)
    return out


def right_table(matrix):
    hi, lo = pieces(matrix, 2)
    return np.concatenate([hi, lo, hi], axis=0)


def left_table(matrix):
    hi, lo = pieces(matrix, 2)
    return np.concatenate([hi, lo, hi], axis=1)


def tables():
    modes, mask = zernike()
    lit = mask.sum()
    turn = 2.0 * math.pi / PIXELS
    freq = np.arange(PIXELS)
    half = np.arange(HALF)
    pupil = np.arange(-RADIUS, RADIUS + 1)

    ang = turn * (pupil[:64, None] * freq[None, :] % PIXELS)
    w1 = np.zeros((128, 256))
    w1[:64, :128] = np.cos(ang)
    w1[:64, 128:] = -np.sin(ang)
    w1[64:, :128] = np.sin(ang)
    w1[64:, 128:] = np.cos(ang)
    hi, lo = pieces(w1.T, 2)
    w1t = np.concatenate([np.concatenate([hi, lo], 1), np.concatenate([hi, 0 * lo], 1)], 0)
    turn65 = np.ones((8, 256), np.float32)
    turn65[1, :128] = turn65[1, 128:] = (-1.0) ** freq

    l2 = np.zeros((128, PAD))
    ang = turn * (half[:, None] * pupil[None, :] % PIXELS)
    l2[:64, :65] = np.cos(ang)
    l2[64:, :65] = np.sin(ang)
    l2[64, :65] = np.cos(turn * (64 * pupil % PIXELS))
    l2[:, 65] = l2[:, 32]

    ang = turn * (half[:, None] * half[None, :] % PIXELS)
    q = np.zeros((128, 128))
    q[:64, :64] = 2.0 * np.cos(ang)
    q[64:, 64:] = -2.0 * np.sin(ang)
    q[:64, 0] = 1.0
    q[:64, 64] = (-1.0) ** half
    q[64, :] = 0.0
    q[64, 1:64] = 2.0 * (-1.0) ** half[1:]
    q[64, 0] = 1.0
    q[64, 64] = 1.0
    q = q / (lit * PIXELS * PIXELS)

    weight = np.full((128,), -8.0)
    weight[0] = -4.0
    weight[64] = -4.0
    qt = q.T * weight[None, :]

    qd = np.zeros((128, 128))
    ang = turn * (half[:, None] * freq[None, :] % PIXELS)
    qd[:64] = np.cos(ang)
    qd[64:] = -np.sin(ang)
    qd[64] = (-1.0) ** freq

    ang = turn * (freq[:, None] * freq[None, :] % PIXELS)
    w4 = np.zeros((256, 256))
    w4[:128, :128] = np.cos(ang)
    w4[:128, 128:] = -np.sin(ang)
    w4[128:, :128] = np.sin(ang)
    w4[128:, 128:] = np.cos(ang)

    rows_table = np.polynomial.legendre.legvander(pupil / RADIUS, DEGREE - 1)
    t = np.zeros((MODES, TERMS, 128))
    t[:, :DEGREE, :64] = np.einsum("ip,kpx->kix", np.linalg.pinv(rows_table), modes)[:, :, :64]
    t[:, DEGREE, 0] = modes[:, 32, 64]
    t[:, :, 64:] = t[:, :, :64]
    th, tm, tl = pieces(t, 3)
    t1 = np.zeros((256, TERMS * 128), ml_dtypes.bfloat16)
    for at, part in ((0, th), (36, th), (72, tm), (128, th), (164, tl), (200, tm)):
        t1[at : at + MODES] = part.reshape(MODES, -1)
    t[:, :, :64] *= -1.0
    th, tm = pieces(t, 2)
    t2 = np.zeros((TERMS * 128, 128), ml_dtypes.bfloat16)
    t2[:, :MODES] = th.reshape(MODES, -1).T
    t2[:, 64 : 64 + MODES] = tm.reshape(MODES, -1).T

    y = np.zeros((SIDE, 16))
    y[:65, :DEGREE] = rows_table
    y[65, DEGREE] = 1.0
    yh, ym, yl = pieces(y, 3)
    y1 = np.concatenate([yh, yh, ym, yh, yl, ym], axis=1)
    y = np.zeros((16, PAD))
    y[:DEGREE, :65] = rows_table.T
    y[DEGREE, 65] = 1.0
    y2 = left_table(y)

    def packed(values, other):
        out = np.zeros((SIDE, 128))
        out[:65, :64] = values[:, :64]
        out[65, 0] = values[32, 64]
        out[:, 64:] = other * out[:, :64]
        return out

    lens = np.stack(
        [
            packed(mask, 1.0),
            packed(np.cos(DIVERSITY * modes[2] * mask), 1.0),
            packed(-np.sin(DIVERSITY * modes[2] * mask), -1.0),
        ]
    ).astype(np.float32)

    edges = np.minimum(freq, PIXELS - 1 - freq)
    taper = np.zeros((8, 128), np.float32)
    for kind in range(4):
        width = (kind + 1) * PIXELS // 16
        taper[kind] = np.where(
            edges < width, 0.5 - 0.5 * np.cos(math.pi * (edges + 0.5) / width), 1.0
        )

    flip = np.zeros((128, 128))
    flip[(-freq) % PIXELS, freq] = 1.0
    flip = np.concatenate([flip] * 3, axis=0).astype(ml_dtypes.bfloat16)

    return dict(
        w1=right_table(w1),
        w1t=w1t,
        turn65=turn65,
        l2=left_table(l2),
        l2t=tall_table(l2.T),
        q=left_table(q),
        qt=tall_table(qt),
        w4=right_table(w4),
        w4t=right_table(w4.T),
        qd=qd.astype(np.float32),
        t1=t1,
        t2=t2,
        y1=y1,
        y2=y2,
        lens=lens,
        taper=taper,
        flip=flip,
    )


NAMES = (
    "w1", "w1t", "turn65", "l2", "l2t", "q", "qt", "w4", "w4t", "qd", "t1", "t2", "y1", "y2", "lens", "taper", "flip",
)


MOVED = ("w1", "w1t", "l2", "l2t", "q", "qt", "w4", "w4t", "t1", "t2", "flip")


def sincos(x):
    k = jnp.floor(x * np.float32(1.0 / math.pi) + 0.5)
    r = x - k * np.float32(3.140625)
    r = r - k * np.float32(0.0009670257568359375)
    r = r - k * np.float32(6.2771141529083251953e-7)
    odd = k - 2.0 * jnp.floor(k * 0.5)
    sign = 1.0 - 2.0 * odd
    r2 = r * r
    s = np.float32(-2.3868346521031027639830001794722295e-8)
    for c in (
        2.7526e-6,
        -1.98408735e-4,
        8.33333114e-3,
        -1.66666667e-1,
    ):
        s = s * r2 + np.float32(c)
    s = (s * r2 * r + r) * sign
    c_ = np.float32(-2.6e-7)
    for c in (
        2.4771e-5,
        -1.38888e-3,
        4.16666e-2,
        -0.5,
        1.0,
    ):
        c_ = c_ * r2 + np.float32(c)
    return s, c_ * sign


def cosine(x):
    k = jnp.floor(x * np.float32(1.0 / math.pi) + 0.5)
    r = x - k * np.float32(3.140625)
    r = r - k * np.float32(0.0009670257568359375)
    r = r - k * np.float32(6.2771141529083251953e-7)
    sign = 1.0 - 2.0 * (k - 2.0 * jnp.floor(k * 0.5))
    r2 = r * r
    out = np.float32(-2.6e-7)
    for c in (2.4771e-5, -1.38888e-3, 4.16666e-2, -0.5, 1.0):
        out = out * r2 + np.float32(c)
    return out * sign


def two(x):
    hi = x.astype(BF16)
    return hi, (x - hi.astype(F32)).astype(BF16)


def three(x):
    hi = x.astype(BF16)
    rest = x - hi.astype(F32)
    mid = rest.astype(BF16)
    return hi, mid, (rest - mid.astype(F32)).astype(BF16)


def right(x, table):
    hi, lo = two(x)
    return jnp.dot(jnp.concatenate([hi, hi, lo], axis=1), table, preferred_element_type=F32)


def left(table, x):
    hi, lo = two(x)
    return jnp.dot(table, jnp.concatenate([hi, hi, lo], axis=0), preferred_element_type=F32)


def skewed(count, ahead, first, second):
    waiting = []
    for i in range(count):
        waiting.append(first(i))
        if len(waiting) > ahead:
            second(waiting.pop(0))
    for x in waiting:
        second(x)


def tall_table(matrix):
    hi, lo = pieces(matrix, 2)
    return np.concatenate([np.concatenate([hi, hi], 1), np.concatenate([lo, 0 * lo], 1)], 0)


def tall(table, x):
    out = jnp.dot(table, jnp.concatenate(two(x), axis=0), preferred_element_type=F32)
    half = out.shape[0] // 2
    return out[:half] + out[half:]


def patched(whole, first):
    return jnp.concatenate([first, whole[8:]], axis=0)


def kernel(
    nf, nr, nc,
    images, corners, kinds, coefs_in, step, noise, smooth,
    w1, w1t, turn65, l2, l2t, q, qt, w4, w4t, qd, t1, t2, y1, y2, lens, taper, flip,
    coefs_out, object_out,
    images_, w1_, w1t_, l2_, l2t_, q_, qt_, w4_, w4t_, t1_, t2_, flip_, result,
    fill_sem, image_sem, result_sem,
    coefs, halo, bent, dbent, fields, waves, otf, data, sums, parts, objs, norm1, norm2, turned,
    rs_send, rs_recv, ag_send, ag_recv, n1_send, n1_recv, n2_send, n2_recv, h_send, h_recv,
):
    me = lax.axis_index("frame")
    row = lax.axis_index("row")
    col = lax.axis_index("col")
    place = row * nc + col
    nplace = nr * nc
    per = 16 // nf
    own = min(per, TILES)
    owners = TILES // own
    pair = nf // 2
    chips = max(pair, 1) * nplace

    lanes = lax.broadcasted_iota(jnp.int32, (8, 128), 1)
    subs = lax.broadcasted_iota(jnp.int32, (8, 128), 0)
    m00 = (lanes == 0) & (subs == 0)
    m064 = (lanes == 64) & (subs == 0)

    def loop(first, last, act):
        def body(k, _):
            act(k)
            return 0

        if last > first:
            lax.fori_loop(first, last, body, 0)

    halo[...] = jnp.zeros(halo.shape, F32)

    def after(index, step, count):
        moved = index + step
        return jnp.where(moved >= count, moved - count, moved)

    frames = [after(me, k, nf) for k in range(nf)]
    rows = [after(row, k, nr) for k in range(nr)]
    cols = [after(col, k, nc) for k in range(nc)]

    def far(steps):
        k, dr, dc = steps
        dy, dx = k // 2, dc * 2 + k % 2
        return min(dy, 4 - dy) + min(dr, nr - dr) + min(dx, 4 - dx)

    others = [(k, dr, dc) for k in range(max(pair, 1)) for dr in range(nr) for dc in range(nc)]
    others = sorted(others, key=far, reverse=True)
    others = [x for x in others if x != (0, 0, 0)]

    def there(steps):
        k, dr, dc = steps
        return {"frame": frames[2 * k], "row": rows[dr], "col": cols[dc]}

    npeers = (nf - 1) + max(pair, 1) * (nplace - 1)
    if npeers:
        barrier = pltpu.get_barrier_semaphore()

        for x in others:
            if x[1:] != (0, 0):
                pl.semaphore_signal(barrier, inc=1, device_id=there(x), device_id_type=MESH)
        for k in range(1, nf):
            pl.semaphore_signal(barrier, inc=1, device_id={"frame": frames[k]}, device_id_type=MESH)

    fills = {
        i: pltpu.make_async_copy(src, dst, fill_sem.at[i])
        for i, (src, dst) in enumerate(
            [
                (w4, w4_), (t1, t1_), (w1, w1_), (l2, l2_), (q, q_), (w4t, w4t_), (qt, qt_),
                (l2t, l2t_), (w1t, w1t_), (t2, t2_), (flip, flip_),
            ]
        )
    }
    source = images

    def image_copy(s, f):
        r, c_ = s // 2, lax.rem(s, 2)
        return pltpu.make_async_copy(source.at[f, r, c_], images_.at[s, f], image_sem.at[s, f])

    for f in range(FRAMES):
        image_copy(0, f).start()
    for i in range(5):
        fills[i].start()
    for s in range(1, FIELDS):
        for f in range(FRAMES):
            image_copy(s, f).start()
    for i in range(5, len(fills)):
        fills[i].start()
    images, w1, w1t, l2, l2t, q, qt, w4, w4t, t1, t2, flip = (
        images_, w1_, w1t_, l2_, l2t_, q_, qt_, w4_, w4t_, t1_, t2_, flip_
    )

    coefs[...] = jnp.zeros((ITEMS, 128), F32)
    bent[...] = jnp.zeros((ITEMS * 16, 128), F32)
    for f in range(FRAMES):
        for s in range(FIELDS):
            coefs[pl.ds(s * 4 + f, 1), pl.ds(0, MODES)] = coefs_in[f, s // 2, pl.ds(s % 2, 1), :]

    rows64 = lax.broadcasted_iota(jnp.int32, (HALF, 128), 0).astype(F32)
    cols8 = lanes.astype(F32)

    def data_field(s):
        r, c_ = s // 2, lax.rem(s, 2)
        for f in range(FRAMES):
            image_copy(s, f).wait()
        kind = kinds[r, c_]
        window = jnp.where(
            kind == 0, taper[pl.ds(0, 1), :],
            jnp.where(
                kind == 1, taper[pl.ds(1, 1), :],
                jnp.where(kind == 2, taper[pl.ds(2, 1), :], taper[pl.ds(3, 1), :]),
            ),
        )
        rotor = jnp.concatenate(two(qd[...] * window), axis=1)
        both = jnp.concatenate([window, window], axis=1)
        ready = []
        middle = []
        turns = []
        for f in range(FRAMES):
            c0 = corners[0, r, c_, f].astype(F32)
            c1 = corners[1, r, c_, f].astype(F32)
            image = jnp.concatenate([images[s, f, 0], images[s, f, 1]], axis=1)
            lines = jnp.dot(
                rotor, jnp.concatenate([image, image], axis=0), preferred_element_type=F32
            )
            lines = lines * both
            cycles = rows64 * (c0 * np.float32(1.0 / PIXELS))
            cycles = cycles - jnp.floor(cycles + 0.5)
            rs, rc = sincos(cycles * np.float32(2.0 * math.pi))
            cycles = cols8 * (c1 * np.float32(1.0 / PIXELS))
            cycles = cycles - jnp.floor(cycles + 0.5)
            cs, cc = sincos(cycles * np.float32(2.0 * math.pi))
            turns.append((cs[:1] * np.float32(1.0 / PIXELS), cc[:1] * np.float32(1.0 / PIXELS)))
            c0h = c0 * 0.5
            alternate = (1.0 - 4.0 * jnp.abs(c0h - jnp.floor(c0h))) * np.float32(1.0 / PIXELS)
            for c in range(2):
                zr = lines[:64, c * 128 : c * 128 + 128]
                zi = lines[64:, c * 128 : c * 128 + 128]
                middle.append(jnp.sum(zi[:1], axis=1, keepdims=True) * alternate)
                zi = patched(zi, jnp.where(subs == 0, 0.0, zi[:8]))
                ready.append(jnp.concatenate([zr * rc - zi * rs, zr * rs + zi * rc], axis=1))
        spec = right(jnp.concatenate(ready, axis=0), w4[...])
        for f in range(FRAMES):
            cs, cc = turns[f]
            for c in range(2):
                at = (f * 2 + c) * 64
                dr = spec[at : at + 64, :128]
                di = spec[at : at + 64, 128:]
                data[s * 4 + f, pl.ds(c * 64, 64), pl.ds(0, 128)] = dr * cc - di * cs
                di = dr * cs + di * cc
                data[s * 4 + f, pl.ds(c * 64, 64), pl.ds(128, 128)] = patched(
                    di, jnp.where(m00, middle[f * 2 + c], di[:8])
                )

    def remote(src, dst, send, recv, device):
        return pltpu.make_async_remote_copy(
            src_ref=src, dst_ref=dst, send_sem=send, recv_sem=recv,
            device_id=device, device_id_type=MESH,
        )

    def owner(s, k):
        return lax.rem(s, 2) * owners + k

    def landed(ref, sem):
        pltpu.make_async_copy(ref, ref, sem).wait()

    def mine(s):
        return me // owners == lax.rem(s, 2) if nf > 1 else s >= 0

    def send_field(it, s):
        if nf > 1:
            for step_ in range(owners):
                k = lax.rem(me + step_, owners)
                peer = owner(s, k)
                copy = remote(
                    sums.at[it, s, pl.ds(k * own, own)], parts.at[it, s // 2, me],
                    rs_send.at[it, s], rs_recv.at[it, s // 2], {"frame": peer},
                )
                pl.when(peer != me)(copy.start)

    def reduce_field(it, s):
        @pl.when(mine(s))
        def _():
            k = lax.rem(me, owners)
            if nf > 1:
                landed(parts.at[it, s // 2, pl.ds(0, nf - 1)], rs_recv.at[it, s // 2])
            for j in range(own):
                tile = k * own + j
                total = sums[it, s, tile]
                for other in range(1, nf):
                    total = total + parts[it, s // 2, frames[other], j]
                first = tile == 0
                real, imag, power = total[0], total[1], total[2]
                n = noise[0, 0]
                other = jnp.where(m00 & first, pltpu.roll(imag, 64, 1), power)
                objs[it, s, tile, 0] = real / (power + n)
                objs[it, s, tile, 1] = jnp.where(m064 & first, 0.0, imag / (other + n))
            at = pl.ds(k * own, own)
            for j in sorted(range(1, nf), key=lambda j: -min(j // 4, 4 - j // 4) - j // 2 % 2):
                remote(
                    objs.at[it, s, at], objs.at[it, s, at],
                    ag_send.at[it, s // 2], ag_recv.at[it, s], {"frame": frames[j]},
                ).start()

    def wait_field(it, s):
        if nf > 1:
            pl.when(mine(s))(lambda: landed(objs.at[it, s, pl.ds(0, TILES - own)], ag_recv.at[it, s]))
            pl.when(jnp.logical_not(mine(s)))(lambda: landed(objs.at[it, s], ag_recv.at[it, s]))

    def n1_copy(it, slot):
        return remote(
            norm1.at[it, lax.rem(me, 2)], norm1.at[it, slot],
            n1_send.at[it], n1_recv.at[it], {"frame": me + 1 - 2 * lax.rem(me, 2)},
        )

    def n2_copy(it, steps):
        slot = me // 2 * nplace + place
        return remote(
            norm2.at[it, slot], norm2.at[it, slot], n2_send.at[it], n2_recv.at[it], there(steps)
        )

    def halo_copies(it):
        def one(axis, index, count, delta, slot):
            peer = jnp.clip(index + delta, 0, count - 1)
            inside = (index + delta >= 0) & (index + delta < count)
            return inside, remote(
                halo.at[it, 4], halo.at[it, slot], h_send.at[it, slot], h_recv.at[it, slot], {axis: peer}
            )

        out = []
        if nr > 1:
            out += [one("row", row, nr, 1, 0), one("row", row, nr, -1, 1)]
        if nc > 1:
            out += [one("col", col, nc, 1, 2), one("col", col, nc, -1, 3)]
        return out

    def halo_sides():
        out = []
        if nr > 1:
            out += [(0, row > 0), (1, row < nr - 1)]
        if nc > 1:
            out += [(2, col > 0), (3, col < nc - 1)]
        return out

    def bend(cf):
        ch = cf.astype(BF16).astype(F32)
        cm = (cf - ch).astype(BF16).astype(F32)
        cl = (cf - ch - cm).astype(BF16).astype(F32)
        low = ch + pltpu.roll(cm, 36, 1) + pltpu.roll(ch, 72, 1)
        high = cl + pltpu.roll(ch, 36, 1) + pltpu.roll(cm, 72, 1)
        lhs = jnp.concatenate([low, high], axis=1).astype(BF16)
        return jnp.dot(lhs, t1[...], preferred_element_type=F32)

    def store_bent(out):
        for i in range(TERMS):
            bent[pl.ds(i, ITEMS, stride=16), :] = out[:, i * 128 : i * 128 + 128]

    fills[0].wait()
    fills[1].wait()
    store_bent(bend(coefs[...]))
    for i in range(2, 5):
        fills[i].wait()

    def forward(it, s):
        stacks = []
        for f in range(FRAMES):
            x = bent[pl.ds(pl.multiple_of((s * 4 + f) * 16, 16), 16), :]
            h, m, l = three(x)
            stacks.append(jnp.concatenate([h, m, h, l, h, m], axis=0))
        phases = jnp.dot(y1[...], jnp.concatenate(stacks, axis=1), preferred_element_type=F32)
        quarter = jnp.where(lanes[:1] < 64, 0.0, np.float32(0.5 * math.pi))
        none = jnp.zeros((PAD - SIDE, 128), F32)
        lines = []
        for g in range(0, FRAMES, GROUP):
            pupil = []
            for f in range(g, g + GROUP):
                item = s * 4 + f
                one0 = cosine(phases[:, f * 128 : f * 128 + 128] - quarter) * lens[0]
                two0 = pltpu.roll(one0, 64, 1)
                one1 = one0 * lens[1] + two0 * lens[2]
                fields[item, 0] = two0
                fields[item, 1] = two0 * lens[1] - one0 * lens[2]
                pupil += [one0, none, one1, none]
            lines.append(right(jnp.concatenate(pupil, axis=0), w1[...]))
        lines = jnp.concatenate(lines, axis=0)
        z = []

        def first(f):
            evens = []
            odds = []
            for c in range(2):
                at = (f * 2 + c) * PAD
                wave = left(
                    l2[...],
                    jnp.concatenate(
                        [
                            lines[at : at + 64], lines[at + 64 : at + 72] * turn65[...],
                            lines[at + 72 : at + 80],
                        ],
                        axis=0,
                    ),
                )
                waves[s * 4 + f, c] = wave
                a, b = wave[:64, :128], wave[:64, 128:]
                e, d = wave[64:, :128], wave[64:, 128:]
                ab = a * a + b * b
                ed = e * e + d * d
                even = ab + ed
                odd = 2.0 * (a * d - b * e)
                evens.append(patched(even, jnp.where(subs == 0, ab[:8], even[:8])))
                odds.append(patched(odd, jnp.where(subs == 0, ed[:8], odd[:8])))
            return jnp.concatenate(
                [jnp.concatenate(evens, axis=1), jnp.concatenate(odds, axis=1)], axis=0
            )

        def second(spread):
            half = left(q[...], spread)
            for c in range(2):
                at = slice(c * 128, c * 128 + 128)
                z.append(jnp.concatenate([half[:64, at], half[64:, at]], axis=1))

        def third():
            if len(z) % (2 * GROUP) == 0:
                out.append(right(jnp.concatenate(z[-2 * GROUP :], axis=0), w4[...]))

        out = []
        skewed(FRAMES, SKEW, first, lambda x: (second(x), third()))
        z = jnp.concatenate(out, axis=0)
        for f in range(FRAMES):
            otf[s * 4 + f] = z[f * 128 : f * 128 + 128]
        for t in range(TILES):
            cr = ci = pw = None
            for f in range(FRAMES):
                for c in range(2):
                    at = f * 128 + c * 64 + t * 8
                    zr, zi = z[at : at + 8, :128], z[at : at + 8, 128:]
                    dr = data[s * 4 + f, pl.ds(c * 64 + t * 8, 8), pl.ds(0, 128)]
                    di = data[s * 4 + f, pl.ds(c * 64 + t * 8, 8), pl.ds(128, 128)]
                    ii = zi * di
                    zz = zi * zi
                    im = zr * di - zi * dr
                    if t == 0:
                        im = jnp.where(m00, ii, im)
                        im = jnp.where(m064, pltpu.roll(zz, 64, 1), im)
                        ii = jnp.where(m00, 0.0, ii)
                        zz = jnp.where(m00, 0.0, zz)
                    re = zr * dr + ii
                    p = zr * zr + zz
                    cr = re if cr is None else cr + re
                    ci = im if ci is None else ci + im
                    pw = p if pw is None else pw + p
            sums[it, s, t, 0] = cr
            sums[it, s, t, 1] = ci
            sums[it, s, t, 2] = pw

    def backward(it, s):
        dz = {}
        zero = subs == 0

        def residual(g):
            res = [[] for _ in range(2 * GROUP)]
            for t in range(TILES):
                our = objs[it, s, t, 0]
                oui = objs[it, s, t, 1]
                oor = ooi = our * our + oui * oui
                if t == 0:
                    oor = jnp.where(m00, our * our, oor)
                    ooi = jnp.where(m00, oui * oui, ooi)
                for f in range(g, g + GROUP):
                    for c in range(2):
                        at = pl.ds(c * 64 + t * 8, 8)
                        item = s * 4 + f
                        zr, zi = otf[item, at, pl.ds(0, 128)], otf[item, at, pl.ds(128, 128)]
                        dr, di = data[item, at, pl.ds(0, 128)], data[item, at, pl.ds(128, 128)]
                        ii = di * oui
                        im = di * our - dr * oui
                        if t == 0:
                            im = jnp.where(m00, ii, im)
                            ii = jnp.where(m00, 0.0, ii)
                        real = dr * our + ii - oor * zr
                        res[(f - g) * 2 + c].append(jnp.concatenate([real, im - ooi * zi], axis=1))
            return jnp.concatenate(sum(res, []), axis=0)

        def first(f):
            at = f % GROUP * 128
            dz_ = dz[f // GROUP]
            half = jnp.concatenate(
                [
                    jnp.concatenate([dz_[at : at + 64, :128], dz_[at + 64 : at + 128, :128]], axis=1),
                    jnp.concatenate([dz_[at : at + 64, 128:], dz_[at + 64 : at + 128, 128:]], axis=1),
                ],
                axis=0,
            )
            dspread = tall(qt[...], half)
            dwaves = []
            for c in range(2):
                de = dspread[:64, c * 128 : c * 128 + 128]
                do = dspread[64:, c * 128 : c * 128 + 128]
                wave = waves[s * 4 + f, c]
                a, b = wave[:64, :128], wave[:64, 128:]
                e, d = wave[64:, :128], wave[64:, 128:]
                da = a * de + d * do
                db = b * de - e * do
                dc = e * de - b * do
                dd = d * de + a * do
                de8, do8 = de[:8], do[:8]
                da = patched(da, jnp.where(zero, a[:8] * de8, da[:8]))
                db = patched(db, jnp.where(zero, b[:8] * de8, db[:8]))
                dc = patched(dc, jnp.where(zero, e[:8] * do8, dc[:8]))
                dd = patched(dd, jnp.where(zero, d[:8] * do8, dd[:8]))
                dwaves.append(jnp.concatenate(
                    [jnp.concatenate([da, db], axis=1), jnp.concatenate([dc, dd], axis=1)], axis=0
                ))
            return dwaves

        def second(dwaves):
            out = []
            for dwave in dwaves:
                x = tall(l2t[...], dwave)
                out.append(jnp.concatenate([x[:64], x[64:72] * turn65[...], x[72:]], axis=0))
            return out

        def third(x):
            x = jnp.dot(
                jnp.concatenate(two(jnp.concatenate(x, axis=0)), axis=1), w1t[...],
                preferred_element_type=F32,
            )
            return x[:, :128] + x[:, 128:]

        res, dwaves, dlines, dpupil = {}, {}, {}, {}
        for what, i in ORDER:
            if what == "r":
                res[i] = residual(i * GROUP)
            elif what == "w":
                dz[i] = right(res[i], w4t[...])
            elif what == "q":
                dwaves[i] = first(i)
            elif what == "l":
                dlines[i] = second(dwaves[i])
            else:
                dpupil[i] = third(sum([dlines[f] for f in range(i * GROUP, i * GROUP + GROUP)], []))
        dpupil = jnp.concatenate([dpupil[i] for i in sorted(dpupil)], axis=0)
        dphase = []
        for f in range(FRAMES):
            at = f * 2 * PAD
            dphase.append(
                fields[s * 4 + f, 0] * dpupil[at : at + SIDE]
                + fields[s * 4 + f, 1] * dpupil[at + PAD : at + PAD + SIDE]
            )
        dphase = jnp.concatenate(dphase, axis=1)
        dphase = jnp.concatenate([dphase, jnp.zeros((PAD - SIDE, FRAMES * 128), F32)], axis=0)
        out = left(y2[...], dphase)
        for f in range(FRAMES):
            dbent[pl.ds(pl.multiple_of((s * 4 + f) * 16, 16), 16), :] = out[:, f * 128 : f * 128 + 128]

    def result_copy():
        return pltpu.make_async_copy(result, object_out, result_sem)

    def write_object():
        last = ITERS - 1
        for j in range(per):
            tile = me * per + j

            @pl.when(tile < 8)
            def _(j=j, tile=tile):
                for s in range(FIELDS):
                    re = objs[last, s, tile, 0]
                    im = objs[last, s, tile, 1]
                    result[0, s // 2, s % 2, pl.ds(j * 8, 8), :] = re
                    result[1, s // 2, s % 2, pl.ds(j * 8, 8), :] = jnp.where(m00 & (tile == 0), 0.0, im)

            @pl.when(tile >= 8)
            def _(j=j, tile=tile):
                g = tile - 8
                for s in range(FIELDS):
                    for c in range(2):
                        at = (s * 2 + c) * 8
                        for i in range(1, 8):
                            turned[pl.ds(at + i, 1), :] = objs[last, s, 7 - g, c, pl.ds(8 - i, 1), :]
                        zero = objs[last, s, lax.rem(8 - g, 8), c, pl.ds(0, 1), :]
                        if c == 0:
                            middle = objs[last, s, 0, 1, pl.ds(0, 1), :]
                            middle = jnp.where(lanes[:1] == 0, middle, 0.0)
                        else:
                            middle = jnp.zeros((1, 128), F32)
                        turned[pl.ds(at, 1), :] = jnp.where(g == 0, middle, zero)
                out = jnp.dot(
                    jnp.concatenate(three(turned[...]), axis=1), flip[...], preferred_element_type=F32
                )
                for s in range(FIELDS):
                    at = s * 16
                    result[0, s // 2, s % 2, pl.ds(j * 8, 8), :] = out[at : at + 8]
                    result[1, s // 2, s % 2, pl.ds(j * 8, 8), :] = -out[at + 8 : at + 16]
        result_copy().start()

    def iteration(it):
        cf = coefs[...]

        def forward_step(s):
            pl.when(it == 0)(lambda: data_field(s))
            forward(it, s)

            first = (it == 0) & (s == 2)
            if npeers:
                pl.when(first)(lambda: pl.semaphore_wait(barrier, npeers))
            pl.when(first)(lambda: loop(0, 2, lambda s: send_field(it, s)))
            pl.when((it > 0) | (s >= 2))(lambda: send_field(it, s))

        def backward_step(s):
            wait_field(it, s)
            backward(it, s)

        loop(0, FIELDS, forward_step)

        halo[it, 4] = cf
        for inside, copy in halo_copies(it):
            pl.when(inside)(copy.start)

        loop(0, FIELDS, lambda s: reduce_field(it, s))

        @pl.when(it == 0)
        def _():
            for i in range(5, len(fills)):
                fills[i].wait()

        loop(0, FIELDS, backward_step)

        x = jnp.concatenate([dbent[pl.ds(i, ITEMS, stride=16), :] for i in range(TERMS)], axis=1)
        acc = jnp.dot(jnp.concatenate(two(x), axis=0), t2[...], preferred_element_type=F32)
        grads = acc[:16] + pltpu.roll(acc[:16], 64, 1) + acc[16:]
        lane16 = lax.broadcasted_iota(jnp.int32, (ITEMS, 128), 1)
        grads = jnp.where(lane16 < MODES, grads, 0.0)

        sq = grads * grads
        total = jnp.sum(sq[:8] + sq[8:], axis=0, keepdims=True)
        slot = me // 2 * nplace + place
        if nf > 1:
            norm1[it, lax.rem(me, 2)] = total
            n1_copy(it, lax.rem(me, 2)).start()
            n1_copy(it, 1 - lax.rem(me, 2)).wait_recv()
            total = norm1[it, 0] + norm1[it, 1]
        norm2[it, slot] = total
        for x in others:
            n2_copy(it, x).start()

        for side, inside in halo_sides():
            @pl.when(inside)
            def _(side=side):
                landed(halo.at[it, side], h_recv.at[it, side])

        above, below = halo[it, 0, 8:], halo[it, 1, :8]
        laplace = []
        for r in range(2):
            mine_ = cf[r * 8 : r * 8 + 8]
            other = cf[8 - r * 8 : 16 - r * 8]
            beside = jnp.where(
                subs < 4,
                pltpu.roll(halo[it, 2, r * 8 : r * 8 + 8], 4, 0),
                pltpu.roll(halo[it, 3, r * 8 : r * 8 + 8], 4, 0),
            )
            out = 4.0 * mine_ - other - pltpu.roll(mine_, 4, 0) - beside
            laplace.append(out - (above if r == 0 else below))
        laplace = jnp.concatenate(laplace, axis=0)
        smoothed = cf - step[0, 0] * smooth[0, 0] * laplace
        out = bend(jnp.concatenate([smoothed, grads], axis=0))
        pl.when(it == ITERS - 1)(write_object)

        if chips > 1:
            landed(norm2.at[it, pl.ds(0, chips - 1)], n2_recv.at[it])
        total = jnp.sum(jnp.sum(norm2[it], axis=0), axis=1, keepdims=True)
        count = ITEMS * MODES * nf * nplace
        scale = jnp.sqrt(total / count + TINY)
        pace = step[0, 0] / scale
        coefs[...] = smoothed - pace * grads
        store_bent(out[:ITEMS] - pace * out[ITEMS:])

    def departures(it):
        if nf > 1:
            def field(s):
                @pl.when(mine(s))
                def _():
                    if own < TILES:
                        landed(sums.at[it, s, pl.ds(0, TILES - own)], rs_send.at[it, s])
                    landed(parts.at[it, s // 2, pl.ds(0, nf - 1), :, pl.ds(0, 2)], ag_send.at[it, s // 2])

                pl.when(jnp.logical_not(mine(s)))(lambda: landed(sums.at[it, s], rs_send.at[it, s]))

            loop(0, FIELDS, field)
            n1_copy(it, lax.rem(me, 2)).wait_send()
        if chips > 1:
            landed(norm2.at[it, pl.ds(0, chips - 1)], n2_send.at[it])
        for inside, copy in halo_copies(it):
            pl.when(inside)(copy.wait_send)

    loop(0, ITERS, iteration)

    for f in range(FRAMES):
        for s in range(FIELDS):
            coefs_out[f, s // 2, pl.ds(s % 2, 1), :] = coefs[pl.ds(s * 4 + f, 1), pl.ds(0, MODES)]

    result_copy().wait()
    loop(0, ITERS, departures)


def solution(mesh):
    nf, nr, nc = (mesh.shape[name] for name in ("frame", "row", "col"))
    host = tables()
    per = 16 // nf
    vmem = pl.BlockSpec(memory_space=pltpu.VMEM)
    smem = pl.BlockSpec(memory_space=pltpu.SMEM)
    hbm = pl.BlockSpec(memory_space=pl.ANY)

    def body(images, corners, kinds, coefs, step, noise, smooth):
        own = min(per, TILES)
        chips = max(nf // 2, 1) * nr * nc
        scratch = [pltpu.VMEM((FIELDS, FRAMES, 2, PIXELS, PIXELS), BF16)]
        scratch += [pltpu.VMEM(host[name].shape, BF16) for name in MOVED]
        scratch += [
            pltpu.VMEM((2, 2, 2, 8 * per, 128), F32),
            pltpu.SemaphoreType.DMA((len(MOVED),)),
            pltpu.SemaphoreType.DMA((FIELDS, FRAMES)),
            pltpu.SemaphoreType.DMA,
        ]
        scratch += [
            pltpu.VMEM((ITEMS, 128), F32),
            pltpu.VMEM((ITERS, 5, ITEMS, 128), F32),
            pltpu.VMEM((ITEMS * 16, 128), F32),
            pltpu.VMEM((ITEMS * 16, 128), F32),
            pltpu.VMEM((ITEMS, 2, SIDE, 128), F32),
            pltpu.VMEM((ITEMS, 2, 128, 256), F32),
            pltpu.VMEM((ITEMS, 128, 256), F32),
            pltpu.VMEM((ITEMS, 128, 256), F32),
            pltpu.VMEM((ITERS, FIELDS, TILES, 3, 8, 128), F32),
            pltpu.VMEM((ITERS, 2, nf, own, 3, 8, 128), F32),
            pltpu.VMEM((ITERS, FIELDS, TILES, 2, 8, 128), F32),
            pltpu.VMEM((ITERS, 2, 1, 128), F32),
            pltpu.VMEM((ITERS, chips, 1, 128), F32),
            pltpu.VMEM((HALF, 128), F32),
        ]
        dma = pltpu.SemaphoreType.DMA
        scratch += [dma((ITERS, FIELDS)), dma((ITERS, 2)), dma((ITERS, 2)), dma((ITERS, FIELDS))]
        scratch += [dma((ITERS,)) for _ in range(4)]
        scratch += [dma((ITERS, 4)) for _ in range(2)]
        single = lambda x: x.reshape(1, 1)
        return pl.pallas_call(
            functools.partial(kernel, nf, nr, nc),
            out_shape=(
                jax.ShapeDtypeStruct((FRAMES, 2, 2, MODES), F32),
                jax.ShapeDtypeStruct((2, 2, 2, 8 * per, 128), F32),
            ),
            in_specs=[hbm, smem, smem, vmem, smem, smem, smem]
            + [hbm if name in MOVED else vmem for name in NAMES],
            out_specs=(vmem, hbm),
            scratch_shapes=scratch,
            compiler_params=pltpu.CompilerParams(
                collective_id=0 if nf * nr * nc > 1 else None,
                has_side_effects=True,
                vmem_limit_bytes=56 * 1024 * 1024,
            ),
        )(
            images, corners.transpose(0, 2, 3, 1), kinds, coefs, single(step), single(noise), single(smooth),
            *[jnp.asarray(host[name]) for name in NAMES],
        )

    in_specs = (
        P("frame", "row", "col", None, None, None),
        P(None, "frame", "row", "col"),
        P("row", "col"),
        P("frame", "row", "col", None),
        P(),
        P(),
        P(),
    )
    out_specs = (P("frame", "row", "col", None), P(None, "row", "col", "frame", None))
    return jax.shard_map(body, mesh=mesh, in_specs=in_specs, out_specs=out_specs, check_vma=False)
```

```python
import functools
import math

import jax
import jax.numpy as jnp
import ml_dtypes
import numpy as np
from jax import lax
from jax.experimental import pallas as pl
from jax.experimental.pallas import tpu as pltpu
from jax.sharding import PartitionSpec as P

ITERS = 2
MODES = 36
SKEW = 3
ORDER = (
    ("r", 0), ("w", 0), ("r", 1), ("w", 1), ("q", 0), ("q", 1), ("q", 2), ("q", 3),
    ("l", 0), ("l", 1), ("v", 0), ("l", 2), ("l", 3), ("v", 1),
)
GROUP = 2
DEGREE = 9
TERMS = DEGREE + 1
DIVERSITY = 1.5
TINY = 1e-06
PIXELS = 128
RADIUS = 32
SIDE = 72
PAD = 80
HALF = 64
FRAMES = 4
FIELDS = 4
ITEMS = FRAMES * FIELDS
TILES = 8
F32 = jnp.float32
BF16 = jnp.bfloat16
MESH = pl.DeviceIdType.MESH


def noll_order(mode_index):
    radial_order = (math.isqrt(8 * (mode_index - 1) + 1) - 1) // 2
    position = mode_index - radial_order * (radial_order + 1) // 2
    parity = radial_order % 2
    azimuth = (position + parity) // 2 * 2 - parity
    if azimuth != 0 and mode_index % 2 == 1:
        azimuth = -azimuth
    return (radial_order, azimuth)


def zernike():
    line = np.arange(-RADIUS, RADIUS + 1) / RADIUS
    rows, cols = np.meshgrid(line, line, indexing="ij")
    radius = np.sqrt(rows * rows + cols * cols)
    angle = np.arctan2(rows, cols)
    mask = (rows * rows + cols * cols <= 1.0).astype(np.float64)
    shapes = []
    for mode_index in range(2, MODES + 2):
        n, m = noll_order(mode_index)
        radial = np.zeros_like(radius)
        for t in range((n - abs(m)) // 2 + 1):
            factor = (-1) ** t * math.factorial(n - t)
            factor /= math.factorial(t)
            factor /= math.factorial((n + abs(m)) // 2 - t)
            factor /= math.factorial((n - abs(m)) // 2 - t)
            radial = radial + factor * radius ** (n - 2 * t)
        if m == 0:
            shape = math.sqrt(n + 1) * radial
        elif m > 0:
            shape = math.sqrt(2 * (n + 1)) * radial * np.cos(m * angle)
        else:
            shape = math.sqrt(2 * (n + 1)) * radial * np.sin(-m * angle)
        shapes.append(shape)
    return np.stack(shapes), mask


def pieces(values, count):
    out = []
    rest = np.asarray(values, np.float64)
    for _ in range(count):
        piece = rest.astype(np.float32).astype(ml_dtypes.bfloat16)
        out.append(piece)
        rest = rest - piece.astype(np.float64)
    return out


def right_table(matrix):
    hi, lo = pieces(matrix, 2)
    return np.concatenate([hi, lo, hi], axis=0)


def left_table(matrix):
    hi, lo = pieces(matrix, 2)
    return np.concatenate([hi, lo, hi], axis=1)


def tables():
    modes, mask = zernike()
    lit = mask.sum()
    turn = 2.0 * math.pi / PIXELS
    freq = np.arange(PIXELS)
    half = np.arange(HALF)
    pupil = np.arange(-RADIUS, RADIUS + 1)

    ang = turn * (pupil[:64, None] * freq[None, :] % PIXELS)
    w1 = np.zeros((128, 256))
    w1[:64, :128] = np.cos(ang)
    w1[:64, 128:] = -np.sin(ang)
    w1[64:, :128] = np.sin(ang)
    w1[64:, 128:] = np.cos(ang)
    hi, lo = pieces(w1.T, 2)
    w1t = np.concatenate([np.concatenate([hi, lo], 1), np.concatenate([hi, 0 * lo], 1)], 0)
    turn65 = np.ones((8, 256), np.float32)
    turn65[1, :128] = turn65[1, 128:] = (-1.0) ** freq

    l2 = np.zeros((128, PAD))
    ang = turn * (half[:, None] * pupil[None, :] % PIXELS)
    l2[:64, :65] = np.cos(ang)
    l2[64:, :65] = np.sin(ang)
    l2[64, :65] = np.cos(turn * (64 * pupil % PIXELS))
    l2[:, 65] = l2[:, 32]

    ang = turn * (half[:, None] * half[None, :] % PIXELS)
    q = np.zeros((128, 128))
    q[:64, :64] = 2.0 * np.cos(ang)
    q[64:, 64:] = -2.0 * np.sin(ang)
    q[:64, 0] = 1.0
    q[:64, 64] = (-1.0) ** half
    q[64, :] = 0.0
    q[64, 1:64] = 2.0 * (-1.0) ** half[1:]
    q[64, 0] = 1.0
    q[64, 64] = 1.0
    q = q / (lit * PIXELS * PIXELS)

    weight = np.full((128,), -8.0)
    weight[0] = -4.0
    weight[64] = -4.0
    qt = q.T * weight[None, :]

    qd = np.zeros((128, 128))
    ang = turn * (half[:, None] * freq[None, :] % PIXELS)
    qd[:64] = np.cos(ang)
    qd[64:] = -np.sin(ang)
    qd[64] = (-1.0) ** freq

    ang = turn * (freq[:, None] * freq[None, :] % PIXELS)
    w4 = np.zeros((256, 256))
    w4[:128, :128] = np.cos(ang)
    w4[:128, 128:] = -np.sin(ang)
    w4[128:, :128] = np.sin(ang)
    w4[128:, 128:] = np.cos(ang)

    rows_table = np.polynomial.legendre.legvander(pupil / RADIUS, DEGREE - 1)
    t = np.zeros((MODES, TERMS, 128))
    t[:, :DEGREE, :64] = np.einsum("ip,kpx->kix", np.linalg.pinv(rows_table), modes)[:, :, :64]
    t[:, DEGREE, 0] = modes[:, 32, 64]
    t[:, :, 64:] = t[:, :, :64]
    th, tm, tl = pieces(t, 3)
    t1 = np.zeros((256, TERMS * 128), ml_dtypes.bfloat16)
    for at, part in ((0, th), (36, th), (72, tm), (128, th), (164, tl), (200, tm)):
        t1[at : at + MODES] = part.reshape(MODES, -1)
    t[:, :, :64] *= -1.0
    th, tm = pieces(t, 2)
    t2 = np.zeros((TERMS * 128, 128), ml_dtypes.bfloat16)
    t2[:, :MODES] = th.reshape(MODES, -1).T
    t2[:, 64 : 64 + MODES] = tm.reshape(MODES, -1).T

    y = np.zeros((SIDE, 16))
    y[:65, :DEGREE] = rows_table
    y[65, DEGREE] = 1.0
    yh, ym, yl = pieces(y, 3)
    y1 = np.concatenate([yh, yh, ym, yh, yl, ym], axis=1)
    y = np.zeros((16, PAD))
    y[:DEGREE, :65] = rows_table.T
    y[DEGREE, 65] = 1.0
    y2 = left_table(y)

    def packed(values, other):
        out = np.zeros((SIDE, 128))
        out[:65, :64] = values[:, :64]
        out[65, 0] = values[32, 64]
        out[:, 64:] = other * out[:, :64]
        return out

    lens = np.stack(
        [
            packed(mask, 1.0),
            packed(np.cos(DIVERSITY * modes[2] * mask), 1.0),
            packed(-np.sin(DIVERSITY * modes[2] * mask), -1.0),
        ]
    ).astype(np.float32)

    edges = np.minimum(freq, PIXELS - 1 - freq)
    taper = np.zeros((8, 128), np.float32)
    for kind in range(4):
        width = (kind + 1) * PIXELS // 16
        taper[kind] = np.where(
            edges < width, 0.5 - 0.5 * np.cos(math.pi * (edges + 0.5) / width), 1.0
        )

    flip = np.zeros((128, 128))
    flip[(-freq) % PIXELS, freq] = 1.0
    flip = np.concatenate([flip] * 3, axis=0).astype(ml_dtypes.bfloat16)

    return dict(
        w1=right_table(w1),
        w1t=w1t,
        turn65=turn65,
        l2=left_table(l2),
        l2t=tall_table(l2.T),
        q=left_table(q),
        qt=tall_table(qt),
        w4=right_table(w4),
        w4t=right_table(w4.T),
        qd=qd.astype(np.float32),
        t1=t1,
        t2=t2,
        y1=y1,
        y2=y2,
        lens=lens,
        taper=taper,
        flip=flip,
    )


NAMES = (
    "w1", "w1t", "turn65", "l2", "l2t", "q", "qt", "w4", "w4t", "qd", "t1", "t2", "y1", "y2", "lens", "taper", "flip",
)


MOVED = ("w1", "w1t", "l2", "l2t", "q", "qt", "w4", "w4t", "t1", "t2", "flip")


def sincos(x):
    k = jnp.floor(x * np.float32(1.0 / math.pi) + 0.5)
    r = x - k * np.float32(3.140625)
    r = r - k * np.float32(0.0009670257568359375)
    r = r - k * np.float32(6.2771141529083251953e-7)
    odd = k - 2.0 * jnp.floor(k * 0.5)
    sign = 1.0 - 2.0 * odd
    r2 = r * r
    s = np.float32(-2.3868346521031027639830001794722295e-8)
    for c in (
        2.7526e-6,
        -1.98408735e-4,
        8.33333114e-3,
        -1.66666667e-1,
    ):
        s = s * r2 + np.float32(c)
    s = (s * r2 * r + r) * sign
    c_ = np.float32(-2.6e-7)
    for c in (
        2.4771e-5,
        -1.38888e-3,
        4.16666e-2,
        -0.5,
        1.0,
    ):
        c_ = c_ * r2 + np.float32(c)
    return s, c_ * sign


def cosine(x):
    k = jnp.floor(x * np.float32(1.0 / math.pi) + 0.5)
    r = x - k * np.float32(3.140625)
    r = r - k * np.float32(0.0009670257568359375)
    r = r - k * np.float32(6.2771141529083251953e-7)
    sign = 1.0 - 2.0 * (k - 2.0 * jnp.floor(k * 0.5))
    r2 = r * r
    out = np.float32(-2.6e-7)
    for c in (2.4771e-5, -1.38888e-3, 4.16666e-2, -0.5, 1.0):
        out = out * r2 + np.float32(c)
    return out * sign


def two(x):
    hi = x.astype(BF16)
    return hi, (x - hi.astype(F32)).astype(BF16)


def three(x):
    hi = x.astype(BF16)
    rest = x - hi.astype(F32)
    mid = rest.astype(BF16)
    return hi, mid, (rest - mid.astype(F32)).astype(BF16)


def right(x, table):
    hi, lo = two(x)
    return jnp.dot(jnp.concatenate([hi, hi, lo], axis=1), table, preferred_element_type=F32)


def left(table, x):
    hi, lo = two(x)
    return jnp.dot(table, jnp.concatenate([hi, hi, lo], axis=0), preferred_element_type=F32)


def skewed(count, ahead, first, second):
    waiting = []
    for i in range(count):
        waiting.append(first(i))
        if len(waiting) > ahead:
            second(waiting.pop(0))
    for x in waiting:
        second(x)


def tall_table(matrix):
    hi, lo = pieces(matrix, 2)
    return np.concatenate([np.concatenate([hi, hi], 1), np.concatenate([lo, 0 * lo], 1)], 0)


def tall(table, x):
    out = jnp.dot(table, jnp.concatenate(two(x), axis=0), preferred_element_type=F32)
    half = out.shape[0] // 2
    return out[:half] + out[half:]


def patched(whole, first):
    return jnp.concatenate([first, whole[8:]], axis=0)


def kernel(
    nf, nr, nc,
    images, corners, kinds, coefs_in, step, noise, smooth,
    w1, w1t, turn65, l2, l2t, q, qt, w4, w4t, qd, t1, t2, y1, y2, lens, taper, flip,
    coefs_out, object_out,
    images_, w1_, w1t_, l2_, l2t_, q_, qt_, w4_, w4t_, t1_, t2_, flip_, result,
    fill_sem, image_sem, result_sem,
    coefs, halo, bent, dbent, fields, waves, otf, data, sums, parts, objs, norm1, norm2, turned,
    rs_send, rs_recv, ag_send, ag_recv, n1_send, n1_recv, n2_send, n2_recv, h_send, h_recv,
):
    me = lax.axis_index("frame")
    row = lax.axis_index("row")
    col = lax.axis_index("col")
    place = row * nc + col
    nplace = nr * nc
    per = 16 // nf
    own = min(per, TILES)
    owners = TILES // own
    pair = nf // 2
    chips = max(pair, 1) * nplace

    lanes = lax.broadcasted_iota(jnp.int32, (8, 128), 1)
    subs = lax.broadcasted_iota(jnp.int32, (8, 128), 0)
    m00 = (lanes == 0) & (subs == 0)
    m064 = (lanes == 64) & (subs == 0)

    def loop(first, last, act):
        def body(k, _):
            act(k)
            return 0

        if last > first:
            lax.fori_loop(first, last, body, 0)

    halo[...] = jnp.zeros(halo.shape, F32)

    fills = {
        i: pltpu.make_async_copy(src, dst, fill_sem.at[i])
        for i, (src, dst) in enumerate(
            [
                (w4, w4_), (t1, t1_), (w1, w1_), (l2, l2_), (q, q_), (w4t, w4t_), (qt, qt_),
                (l2t, l2t_), (w1t, w1t_), (t2, t2_), (flip, flip_),
            ]
        )
    }
    source = images

    def image_copy(s, f):
        r, c_ = s // 2, lax.rem(s, 2)
        return pltpu.make_async_copy(source.at[f, r, c_], images_.at[s, f], image_sem.at[s, f])

    for f in range(FRAMES):
        image_copy(0, f).start()
    for i in range(5):
        fills[i].start()
    for s in range(1, FIELDS):
        for f in range(FRAMES):
            image_copy(s, f).start()
    for i in range(5, len(fills)):
        fills[i].start()
    images, w1, w1t, l2, l2t, q, qt, w4, w4t, t1, t2, flip = (
        images_, w1_, w1t_, l2_, l2t_, q_, qt_, w4_, w4t_, t1_, t2_, flip_
    )

    def after(index, step, count):
        moved = index + step
        return jnp.where(moved >= count, moved - count, moved)

    frames = [after(me, k, nf) for k in range(nf)]
    rows = [after(row, k, nr) for k in range(nr)]
    cols = [after(col, k, nc) for k in range(nc)]

    def far(steps):
        k, dr, dc = steps
        dy, dx = k // 2, dc * 2 + k % 2
        return min(dy, 4 - dy) + min(dr, nr - dr) + min(dx, 4 - dx)

    others = [(k, dr, dc) for k in range(max(pair, 1)) for dr in range(nr) for dc in range(nc)]
    others = sorted(others, key=far, reverse=True)
    others = [x for x in others if x != (0, 0, 0)]

    def there(steps):
        k, dr, dc = steps
        return {"frame": frames[2 * k], "row": rows[dr], "col": cols[dc]}

    npeers = (nf - 1) + max(pair, 1) * (nplace - 1)
    if npeers:
        barrier = pltpu.get_barrier_semaphore()

        for x in others:
            if x[1:] != (0, 0):
                pl.semaphore_signal(barrier, inc=1, device_id=there(x), device_id_type=MESH)
        for k in range(1, nf):
            pl.semaphore_signal(barrier, inc=1, device_id={"frame": frames[k]}, device_id_type=MESH)

    coefs[...] = jnp.zeros((ITEMS, 128), F32)
    bent[...] = jnp.zeros((ITEMS * 16, 128), F32)
    for f in range(FRAMES):
        for s in range(FIELDS):
            coefs[pl.ds(s * 4 + f, 1), pl.ds(0, MODES)] = coefs_in[f, s // 2, pl.ds(s % 2, 1), :]

    rows64 = lax.broadcasted_iota(jnp.int32, (HALF, 128), 0).astype(F32)
    cols8 = lanes.astype(F32)

    def data_field(s):
        r, c_ = s // 2, lax.rem(s, 2)
        for f in range(FRAMES):
            image_copy(s, f).wait()
        kind = kinds[r, c_]
        window = jnp.where(
            kind == 0, taper[pl.ds(0, 1), :],
            jnp.where(
                kind == 1, taper[pl.ds(1, 1), :],
                jnp.where(kind == 2, taper[pl.ds(2, 1), :], taper[pl.ds(3, 1), :]),
            ),
        )
        rotor = jnp.concatenate(two(qd[...] * window), axis=1)
        both = jnp.concatenate([window, window], axis=1)
        ready = []
        middle = []
        turns = []
        for f in range(FRAMES):
            c0 = corners[0, r, c_, f].astype(F32)
            c1 = corners[1, r, c_, f].astype(F32)
            image = jnp.concatenate([images[s, f, 0], images[s, f, 1]], axis=1)
            lines = jnp.dot(
                rotor, jnp.concatenate([image, image], axis=0), preferred_element_type=F32
            )
            lines = lines * both
            cycles = rows64 * (c0 * np.float32(1.0 / PIXELS))
            cycles = cycles - jnp.floor(cycles + 0.5)
            rs, rc = sincos(cycles * np.float32(2.0 * math.pi))
            cycles = cols8 * (c1 * np.float32(1.0 / PIXELS))
            cycles = cycles - jnp.floor(cycles + 0.5)
            cs, cc = sincos(cycles * np.float32(2.0 * math.pi))
            turns.append((cs[:1] * np.float32(1.0 / PIXELS), cc[:1] * np.float32(1.0 / PIXELS)))
            c0h = c0 * 0.5
            alternate = (1.0 - 4.0 * jnp.abs(c0h - jnp.floor(c0h))) * np.float32(1.0 / PIXELS)
            for c in range(2):
                zr = lines[:64, c * 128 : c * 128 + 128]
                zi = lines[64:, c * 128 : c * 128 + 128]
                middle.append(jnp.sum(zi[:1], axis=1, keepdims=True) * alternate)
                zi = patched(zi, jnp.where(subs == 0, 0.0, zi[:8]))
                ready.append(jnp.concatenate([zr * rc - zi * rs, zr * rs + zi * rc], axis=1))
        spec = right(jnp.concatenate(ready, axis=0), w4[...])
        for f in range(FRAMES):
            cs, cc = turns[f]
            for c in range(2):
                at = (f * 2 + c) * 64
                dr = spec[at : at + 64, :128]
                di = spec[at : at + 64, 128:]
                data[s * 4 + f, pl.ds(c * 64, 64), pl.ds(0, 128)] = dr * cc - di * cs
                di = dr * cs + di * cc
                data[s * 4 + f, pl.ds(c * 64, 64), pl.ds(128, 128)] = patched(
                    di, jnp.where(m00, middle[f * 2 + c], di[:8])
                )

    def remote(src, dst, send, recv, device):
        return pltpu.make_async_remote_copy(
            src_ref=src, dst_ref=dst, send_sem=send, recv_sem=recv,
            device_id=device, device_id_type=MESH,
        )

    def owner(s, k):
        return lax.rem(s, 2) * owners + k

    def landed(ref, sem):
        pltpu.make_async_copy(ref, ref, sem).wait()

    def mine(s):
        return me // owners == lax.rem(s, 2) if nf > 1 else s >= 0

    def send_field(it, s):
        if nf > 1:
            for step_ in range(owners):
                k = lax.rem(me + step_, owners)
                peer = owner(s, k)
                copy = remote(
                    sums.at[it, s, pl.ds(k * own, own)], parts.at[it, s // 2, me],
                    rs_send.at[it, s], rs_recv.at[it, s // 2], {"frame": peer},
                )
                pl.when(peer != me)(copy.start)

    def reduce_field(it, s):
        @pl.when(mine(s))
        def _():
            k = lax.rem(me, owners)
            if nf > 1:
                landed(parts.at[it, s // 2, pl.ds(0, nf - 1)], rs_recv.at[it, s // 2])
            for j in range(own):
                tile = k * own + j
                total = sums[it, s, tile]
                for other in range(1, nf):
                    total = total + parts[it, s // 2, frames[other], j]
                first = tile == 0
                real, imag, power = total[0], total[1], total[2]
                n = noise[0, 0]
                other = jnp.where(m00 & first, pltpu.roll(imag, 64, 1), power)
                objs[it, s, tile, 0] = real / (power + n)
                objs[it, s, tile, 1] = jnp.where(m064 & first, 0.0, imag / (other + n))
            at = pl.ds(k * own, own)
            for j in sorted(range(1, nf), key=lambda j: -min(j // 4, 4 - j // 4) - j // 2 % 2):
                remote(
                    objs.at[it, s, at], objs.at[it, s, at],
                    ag_send.at[it, s // 2], ag_recv.at[it, s], {"frame": frames[j]},
                ).start()

    def wait_field(it, s):
        if nf > 1:
            pl.when(mine(s))(lambda: landed(objs.at[it, s, pl.ds(0, TILES - own)], ag_recv.at[it, s]))
            pl.when(jnp.logical_not(mine(s)))(lambda: landed(objs.at[it, s], ag_recv.at[it, s]))

    def n1_copy(it, slot):
        return remote(
            norm1.at[it, lax.rem(me, 2)], norm1.at[it, slot],
            n1_send.at[it], n1_recv.at[it], {"frame": me + 1 - 2 * lax.rem(me, 2)},
        )

    def n2_copy(it, steps):
        slot = me // 2 * nplace + place
        return remote(
            norm2.at[it, slot], norm2.at[it, slot], n2_send.at[it], n2_recv.at[it], there(steps)
        )

    def halo_copies(it):
        def one(axis, index, count, delta, slot):
            peer = jnp.clip(index + delta, 0, count - 1)
            inside = (index + delta >= 0) & (index + delta < count)
            return inside, remote(
                halo.at[it, 4], halo.at[it, slot], h_send.at[it, slot], h_recv.at[it, slot], {axis: peer}
            )

        out = []
        if nr > 1:
            out += [one("row", row, nr, 1, 0), one("row", row, nr, -1, 1)]
        if nc > 1:
            out += [one("col", col, nc, 1, 2), one("col", col, nc, -1, 3)]
        return out

    def halo_sides():
        out = []
        if nr > 1:
            out += [(0, row > 0), (1, row < nr - 1)]
        if nc > 1:
            out += [(2, col > 0), (3, col < nc - 1)]
        return out

    def bend(cf):
        ch = cf.astype(BF16).astype(F32)
        cm = (cf - ch).astype(BF16).astype(F32)
        cl = (cf - ch - cm).astype(BF16).astype(F32)
        low = ch + pltpu.roll(cm, 36, 1) + pltpu.roll(ch, 72, 1)
        high = cl + pltpu.roll(ch, 36, 1) + pltpu.roll(cm, 72, 1)
        lhs = jnp.concatenate([low, high], axis=1).astype(BF16)
        return jnp.dot(lhs, t1[...], preferred_element_type=F32)

    def store_bent(out):
        for i in range(TERMS):
            bent[pl.ds(i, ITEMS, stride=16), :] = out[:, i * 128 : i * 128 + 128]

    fills[0].wait()
    fills[1].wait()
    store_bent(bend(coefs[...]))
    for i in range(2, 5):
        fills[i].wait()

    def forward(it, s):
        stacks = []
        for f in range(FRAMES):
            x = bent[pl.ds(pl.multiple_of((s * 4 + f) * 16, 16), 16), :]
            h, m, l = three(x)
            stacks.append(jnp.concatenate([h, m, h, l, h, m], axis=0))
        phases = jnp.dot(y1[...], jnp.concatenate(stacks, axis=1), preferred_element_type=F32)
        quarter = jnp.where(lanes[:1] < 64, 0.0, np.float32(0.5 * math.pi))
        none = jnp.zeros((PAD - SIDE, 128), F32)
        lines = []
        for g in range(0, FRAMES, GROUP):
            pupil = []
            for f in range(g, g + GROUP):
                item = s * 4 + f
                one0 = cosine(phases[:, f * 128 : f * 128 + 128] - quarter) * lens[0]
                two0 = pltpu.roll(one0, 64, 1)
                one1 = one0 * lens[1] + two0 * lens[2]
                fields[item, 0] = two0
                fields[item, 1] = two0 * lens[1] - one0 * lens[2]
                pupil += [one0, none, one1, none]
            lines.append(right(jnp.concatenate(pupil, axis=0), w1[...]))
        lines = jnp.concatenate(lines, axis=0)
        z = []

        def first(f):
            evens = []
            odds = []
            for c in range(2):
                at = (f * 2 + c) * PAD
                wave = left(
                    l2[...],
                    jnp.concatenate(
                        [
                            lines[at : at + 64], lines[at + 64 : at + 72] * turn65[...],
                            lines[at + 72 : at + 80],
                        ],
                        axis=0,
                    ),
                )
                waves[s * 4 + f, c] = wave
                a, b = wave[:64, :128], wave[:64, 128:]
                e, d = wave[64:, :128], wave[64:, 128:]
                ab = a * a + b * b
                ed = e * e + d * d
                even = ab + ed
                odd = 2.0 * (a * d - b * e)
                evens.append(patched(even, jnp.where(subs == 0, ab[:8], even[:8])))
                odds.append(patched(odd, jnp.where(subs == 0, ed[:8], odd[:8])))
            return jnp.concatenate(
                [jnp.concatenate(evens, axis=1), jnp.concatenate(odds, axis=1)], axis=0
            )

        def second(spread):
            half = left(q[...], spread)
            for c in range(2):
                at = slice(c * 128, c * 128 + 128)
                z.append(jnp.concatenate([half[:64, at], half[64:, at]], axis=1))

        def third():
            if len(z) % (2 * GROUP) == 0:
                out.append(right(jnp.concatenate(z[-2 * GROUP :], axis=0), w4[...]))

        out = []
        skewed(FRAMES, SKEW, first, lambda x: (second(x), third()))
        z = jnp.concatenate(out, axis=0)
        for f in range(FRAMES):
            otf[s * 4 + f] = z[f * 128 : f * 128 + 128]
        for t in range(TILES):
            cr = ci = pw = None
            for f in range(FRAMES):
                for c in range(2):
                    at = f * 128 + c * 64 + t * 8
                    zr, zi = z[at : at + 8, :128], z[at : at + 8, 128:]
                    dr = data[s * 4 + f, pl.ds(c * 64 + t * 8, 8), pl.ds(0, 128)]
                    di = data[s * 4 + f, pl.ds(c * 64 + t * 8, 8), pl.ds(128, 128)]
                    ii = zi * di
                    zz = zi * zi
                    im = zr * di - zi * dr
                    if t == 0:
                        im = jnp.where(m00, ii, im)
                        im = jnp.where(m064, pltpu.roll(zz, 64, 1), im)
                        ii = jnp.where(m00, 0.0, ii)
                        zz = jnp.where(m00, 0.0, zz)
                    re = zr * dr + ii
                    p = zr * zr + zz
                    cr = re if cr is None else cr + re
                    ci = im if ci is None else ci + im
                    pw = p if pw is None else pw + p
            sums[it, s, t, 0] = cr
            sums[it, s, t, 1] = ci
            sums[it, s, t, 2] = pw

    def backward(it, s):
        dz = {}
        zero = subs == 0

        def residual(g):
            res = [[] for _ in range(2 * GROUP)]
            for t in range(TILES):
                our = objs[it, s, t, 0]
                oui = objs[it, s, t, 1]
                oor = ooi = our * our + oui * oui
                if t == 0:
                    oor = jnp.where(m00, our * our, oor)
                    ooi = jnp.where(m00, oui * oui, ooi)
                for f in range(g, g + GROUP):
                    for c in range(2):
                        at = pl.ds(c * 64 + t * 8, 8)
                        item = s * 4 + f
                        zr, zi = otf[item, at, pl.ds(0, 128)], otf[item, at, pl.ds(128, 128)]
                        dr, di = data[item, at, pl.ds(0, 128)], data[item, at, pl.ds(128, 128)]
                        ii = di * oui
                        im = di * our - dr * oui
                        if t == 0:
                            im = jnp.where(m00, ii, im)
                            ii = jnp.where(m00, 0.0, ii)
                        real = dr * our + ii - oor * zr
                        res[(f - g) * 2 + c].append(jnp.concatenate([real, im - ooi * zi], axis=1))
            return jnp.concatenate(sum(res, []), axis=0)

        def first(f):
            at = f % GROUP * 128
            dz_ = dz[f // GROUP]
            half = jnp.concatenate(
                [
                    jnp.concatenate([dz_[at : at + 64, :128], dz_[at + 64 : at + 128, :128]], axis=1),
                    jnp.concatenate([dz_[at : at + 64, 128:], dz_[at + 64 : at + 128, 128:]], axis=1),
                ],
                axis=0,
            )
            dspread = tall(qt[...], half)
            dwaves = []
            for c in range(2):
                de = dspread[:64, c * 128 : c * 128 + 128]
                do = dspread[64:, c * 128 : c * 128 + 128]
                wave = waves[s * 4 + f, c]
                a, b = wave[:64, :128], wave[:64, 128:]
                e, d = wave[64:, :128], wave[64:, 128:]
                da = a * de + d * do
                db = b * de - e * do
                dc = e * de - b * do
                dd = d * de + a * do
                de8, do8 = de[:8], do[:8]
                da = patched(da, jnp.where(zero, a[:8] * de8, da[:8]))
                db = patched(db, jnp.where(zero, b[:8] * de8, db[:8]))
                dc = patched(dc, jnp.where(zero, e[:8] * do8, dc[:8]))
                dd = patched(dd, jnp.where(zero, d[:8] * do8, dd[:8]))
                dwaves.append(jnp.concatenate(
                    [jnp.concatenate([da, db], axis=1), jnp.concatenate([dc, dd], axis=1)], axis=0
                ))
            return dwaves

        def second(dwaves):
            out = []
            for dwave in dwaves:
                x = tall(l2t[...], dwave)
                out.append(jnp.concatenate([x[:64], x[64:72] * turn65[...], x[72:]], axis=0))
            return out

        def third(x):
            x = jnp.dot(
                jnp.concatenate(two(jnp.concatenate(x, axis=0)), axis=1), w1t[...],
                preferred_element_type=F32,
            )
            return x[:, :128] + x[:, 128:]

        res, dwaves, dlines, dpupil = {}, {}, {}, {}
        for what, i in ORDER:
            if what == "r":
                res[i] = residual(i * GROUP)
            elif what == "w":
                dz[i] = right(res[i], w4t[...])
            elif what == "q":
                dwaves[i] = first(i)
            elif what == "l":
                dlines[i] = second(dwaves[i])
            else:
                dpupil[i] = third(sum([dlines[f] for f in range(i * GROUP, i * GROUP + GROUP)], []))
        dpupil = jnp.concatenate([dpupil[i] for i in sorted(dpupil)], axis=0)
        dphase = []
        for f in range(FRAMES):
            at = f * 2 * PAD
            dphase.append(
                fields[s * 4 + f, 0] * dpupil[at : at + SIDE]
                + fields[s * 4 + f, 1] * dpupil[at + PAD : at + PAD + SIDE]
            )
        dphase = jnp.concatenate(dphase, axis=1)
        dphase = jnp.concatenate([dphase, jnp.zeros((PAD - SIDE, FRAMES * 128), F32)], axis=0)
        out = left(y2[...], dphase)
        for f in range(FRAMES):
            dbent[pl.ds(pl.multiple_of((s * 4 + f) * 16, 16), 16), :] = out[:, f * 128 : f * 128 + 128]

    def result_copy():
        return pltpu.make_async_copy(result, object_out, result_sem)

    def write_object():
        last = ITERS - 1
        for j in range(per):
            tile = me * per + j

            @pl.when(tile < 8)
            def _(j=j, tile=tile):
                for s in range(FIELDS):
                    re = objs[last, s, tile, 0]
                    im = objs[last, s, tile, 1]
                    result[0, s // 2, s % 2, pl.ds(j * 8, 8), :] = re
                    result[1, s // 2, s % 2, pl.ds(j * 8, 8), :] = jnp.where(m00 & (tile == 0), 0.0, im)

            @pl.when(tile >= 8)
            def _(j=j, tile=tile):
                g = tile - 8
                for s in range(FIELDS):
                    for c in range(2):
                        at = (s * 2 + c) * 8
                        for i in range(1, 8):
                            turned[pl.ds(at + i, 1), :] = objs[last, s, 7 - g, c, pl.ds(8 - i, 1), :]
                        zero = objs[last, s, lax.rem(8 - g, 8), c, pl.ds(0, 1), :]
                        if c == 0:
                            middle = objs[last, s, 0, 1, pl.ds(0, 1), :]
                            middle = jnp.where(lanes[:1] == 0, middle, 0.0)
                        else:
                            middle = jnp.zeros((1, 128), F32)
                        turned[pl.ds(at, 1), :] = jnp.where(g == 0, middle, zero)
                out = jnp.dot(
                    jnp.concatenate(three(turned[...]), axis=1), flip[...], preferred_element_type=F32
                )
                for s in range(FIELDS):
                    at = s * 16
                    result[0, s // 2, s % 2, pl.ds(j * 8, 8), :] = out[at : at + 8]
                    result[1, s // 2, s % 2, pl.ds(j * 8, 8), :] = -out[at + 8 : at + 16]
        result_copy().start()

    def iteration(it):
        cf = coefs[...]

        def forward_step(s):
            pl.when(it == 0)(lambda: data_field(s))
            forward(it, s)

            first = (it == 0) & (s == 2)
            if npeers:
                pl.when(first)(lambda: pl.semaphore_wait(barrier, npeers))
            pl.when(first)(lambda: loop(0, 2, lambda s: send_field(it, s)))
            pl.when((it > 0) | (s >= 2))(lambda: send_field(it, s))

        def backward_step(s):
            wait_field(it, s)
            backward(it, s)

        loop(0, FIELDS, forward_step)

        halo[it, 4] = cf
        for inside, copy in halo_copies(it):
            pl.when(inside)(copy.start)

        loop(0, FIELDS, lambda s: reduce_field(it, s))

        @pl.when(it == 0)
        def _():
            for i in range(5, len(fills)):
                fills[i].wait()

        loop(0, FIELDS, backward_step)

        x = jnp.concatenate([dbent[pl.ds(i, ITEMS, stride=16), :] for i in range(TERMS)], axis=1)
        acc = jnp.dot(jnp.concatenate(two(x), axis=0), t2[...], preferred_element_type=F32)
        grads = acc[:16] + pltpu.roll(acc[:16], 64, 1) + acc[16:]
        lane16 = lax.broadcasted_iota(jnp.int32, (ITEMS, 128), 1)
        grads = jnp.where(lane16 < MODES, grads, 0.0)

        sq = grads * grads
        total = jnp.sum(sq[:8] + sq[8:], axis=0, keepdims=True)
        slot = me // 2 * nplace + place
        if nf > 1:
            norm1[it, lax.rem(me, 2)] = total
            n1_copy(it, lax.rem(me, 2)).start()
            n1_copy(it, 1 - lax.rem(me, 2)).wait_recv()
            total = norm1[it, 0] + norm1[it, 1]
        norm2[it, slot] = total
        for x in others:
            n2_copy(it, x).start()

        for side, inside in halo_sides():
            @pl.when(inside)
            def _(side=side):
                landed(halo.at[it, side], h_recv.at[it, side])

        above, below = halo[it, 0, 8:], halo[it, 1, :8]
        laplace = []
        for r in range(2):
            mine_ = cf[r * 8 : r * 8 + 8]
            other = cf[8 - r * 8 : 16 - r * 8]
            beside = jnp.where(
                subs < 4,
                pltpu.roll(halo[it, 2, r * 8 : r * 8 + 8], 4, 0),
                pltpu.roll(halo[it, 3, r * 8 : r * 8 + 8], 4, 0),
            )
            out = 4.0 * mine_ - other - pltpu.roll(mine_, 4, 0) - beside
            laplace.append(out - (above if r == 0 else below))
        laplace = jnp.concatenate(laplace, axis=0)
        smoothed = cf - step[0, 0] * smooth[0, 0] * laplace
        out = bend(jnp.concatenate([smoothed, grads], axis=0))
        pl.when(it == ITERS - 1)(write_object)

        if chips > 1:
            landed(norm2.at[it, pl.ds(0, chips - 1)], n2_recv.at[it])
        total = jnp.sum(jnp.sum(norm2[it], axis=0), axis=1, keepdims=True)
        count = ITEMS * MODES * nf * nplace
        scale = jnp.sqrt(total / count + TINY)
        pace = step[0, 0] / scale
        coefs[...] = smoothed - pace * grads
        store_bent(out[:ITEMS] - pace * out[ITEMS:])

    def departures(it):
        if nf > 1:
            def field(s):
                @pl.when(mine(s))
                def _():
                    if own < TILES:
                        landed(sums.at[it, s, pl.ds(0, TILES - own)], rs_send.at[it, s])
                    landed(parts.at[it, s // 2, pl.ds(0, nf - 1), :, pl.ds(0, 2)], ag_send.at[it, s // 2])

                pl.when(jnp.logical_not(mine(s)))(lambda: landed(sums.at[it, s], rs_send.at[it, s]))

            loop(0, FIELDS, field)
            n1_copy(it, lax.rem(me, 2)).wait_send()
        if chips > 1:
            landed(norm2.at[it, pl.ds(0, chips - 1)], n2_send.at[it])
        for inside, copy in halo_copies(it):
            pl.when(inside)(copy.wait_send)

    loop(0, ITERS, iteration)

    for f in range(FRAMES):
        for s in range(FIELDS):
            coefs_out[f, s // 2, pl.ds(s % 2, 1), :] = coefs[pl.ds(s * 4 + f, 1), pl.ds(0, MODES)]

    result_copy().wait()
    loop(0, ITERS, departures)


def deliver(coefs, objects, coefs_out, object_out):
    coefs_out[...] = coefs[...]
    object_out[...] = objects[...]


def solution(mesh):
    nf, nr, nc = (mesh.shape[name] for name in ("frame", "row", "col"))
    host = tables()
    per = 16 // nf
    vmem = pl.BlockSpec(memory_space=pltpu.VMEM)
    smem = pl.BlockSpec(memory_space=pltpu.SMEM)
    hbm = pl.BlockSpec(memory_space=pl.ANY)

    def body(images, corners, kinds, coefs, step, noise, smooth):
        own = min(per, TILES)
        chips = max(nf // 2, 1) * nr * nc
        scratch = [pltpu.VMEM((FIELDS, FRAMES, 2, PIXELS, PIXELS), BF16)]
        scratch += [pltpu.VMEM(host[name].shape, BF16) for name in MOVED]
        scratch += [
            pltpu.VMEM((2, 2, 2, 8 * per, 128), F32),
            pltpu.SemaphoreType.DMA((len(MOVED),)),
            pltpu.SemaphoreType.DMA((FIELDS, FRAMES)),
            pltpu.SemaphoreType.DMA,
        ]
        scratch += [
            pltpu.VMEM((ITEMS, 128), F32),
            pltpu.VMEM((ITERS, 5, ITEMS, 128), F32),
            pltpu.VMEM((ITEMS * 16, 128), F32),
            pltpu.VMEM((ITEMS * 16, 128), F32),
            pltpu.VMEM((ITEMS, 2, SIDE, 128), F32),
            pltpu.VMEM((ITEMS, 2, 128, 256), F32),
            pltpu.VMEM((ITEMS, 128, 256), F32),
            pltpu.VMEM((ITEMS, 128, 256), F32),
            pltpu.VMEM((ITERS, FIELDS, TILES, 3, 8, 128), F32),
            pltpu.VMEM((ITERS, 2, nf, own, 3, 8, 128), F32),
            pltpu.VMEM((ITERS, FIELDS, TILES, 2, 8, 128), F32),
            pltpu.VMEM((ITERS, 2, 1, 128), F32),
            pltpu.VMEM((ITERS, chips, 1, 128), F32),
            pltpu.VMEM((HALF, 128), F32),
        ]
        dma = pltpu.SemaphoreType.DMA
        scratch += [dma((ITERS, FIELDS)), dma((ITERS, 2)), dma((ITERS, 2)), dma((ITERS, FIELDS))]
        scratch += [dma((ITERS,)) for _ in range(4)]
        scratch += [dma((ITERS, 4)) for _ in range(2)]
        single = lambda x: x.reshape(1, 1)
        raw = pl.pallas_call(
            functools.partial(kernel, nf, nr, nc),
            out_shape=(
                jax.ShapeDtypeStruct((FRAMES, 2, 2, MODES), F32),
                jax.ShapeDtypeStruct((2, 2, 2, 8 * per, 128), F32),
            ),
            in_specs=[hbm, smem, smem, vmem, smem, smem, smem]
            + [hbm if name in MOVED else vmem for name in NAMES],
            out_specs=(vmem, hbm),
            scratch_shapes=scratch,
            compiler_params=pltpu.CompilerParams(
                collective_id=0 if nf * nr * nc > 1 else None,
                has_side_effects=True,
                vmem_limit_bytes=56 * 1024 * 1024,
            ),
        )(
            images, corners.transpose(0, 2, 3, 1), kinds, coefs, single(step), single(noise), single(smooth),
            *[jnp.asarray(host[name]) for name in NAMES],
        )
        return pl.pallas_call(
            deliver,
            out_shape=tuple(jax.ShapeDtypeStruct(x.shape, x.dtype) for x in raw),
            in_specs=[vmem, vmem],
            out_specs=(vmem, vmem),
        )(*raw)

    in_specs = (
        P("frame", "row", "col", None, None, None),
        P(None, "frame", "row", "col"),
        P("row", "col"),
        P("frame", "row", "col", None),
        P(),
        P(),
        P(),
    )
    out_specs = (P("frame", "row", "col", None), P(None, "row", "col", "frame", None))
    return jax.shard_map(body, mesh=mesh, in_specs=in_specs, out_specs=out_specs, check_vma=False)
```

```python
import functools
import math

import jax
import jax.numpy as jnp
import ml_dtypes
import numpy as np
from jax import lax
from jax.experimental import pallas as pl
from jax.experimental.pallas import tpu as pltpu
from jax.sharding import PartitionSpec as P

ITERS = 2
MODES = 36
SKEW = 3
ORDER = (
    ("r", 0), ("w", 0), ("r", 1), ("w", 1), ("q", 0), ("q", 1), ("q", 2), ("q", 3),
    ("l", 0), ("l", 1), ("v", 0), ("l", 2), ("l", 3), ("v", 1),
)
GROUP = 2
DEGREE = 9
TERMS = DEGREE + 1
DIVERSITY = 1.5
TINY = 1e-06
PIXELS = 128
RADIUS = 32
SIDE = 72
PAD = 80
HALF = 64
FRAMES = 4
FIELDS = 4
ITEMS = FRAMES * FIELDS
TILES = 8
F32 = jnp.float32
BF16 = jnp.bfloat16
MESH = pl.DeviceIdType.MESH


def noll_order(mode_index):
    radial_order = (math.isqrt(8 * (mode_index - 1) + 1) - 1) // 2
    position = mode_index - radial_order * (radial_order + 1) // 2
    parity = radial_order % 2
    azimuth = (position + parity) // 2 * 2 - parity
    if azimuth != 0 and mode_index % 2 == 1:
        azimuth = -azimuth
    return (radial_order, azimuth)


def zernike():
    line = np.arange(-RADIUS, RADIUS + 1) / RADIUS
    rows, cols = np.meshgrid(line, line, indexing="ij")
    radius = np.sqrt(rows * rows + cols * cols)
    angle = np.arctan2(rows, cols)
    mask = (rows * rows + cols * cols <= 1.0).astype(np.float64)
    shapes = []
    for mode_index in range(2, MODES + 2):
        n, m = noll_order(mode_index)
        radial = np.zeros_like(radius)
        for t in range((n - abs(m)) // 2 + 1):
            factor = (-1) ** t * math.factorial(n - t)
            factor /= math.factorial(t)
            factor /= math.factorial((n + abs(m)) // 2 - t)
            factor /= math.factorial((n - abs(m)) // 2 - t)
            radial = radial + factor * radius ** (n - 2 * t)
        if m == 0:
            shape = math.sqrt(n + 1) * radial
        elif m > 0:
            shape = math.sqrt(2 * (n + 1)) * radial * np.cos(m * angle)
        else:
            shape = math.sqrt(2 * (n + 1)) * radial * np.sin(-m * angle)
        shapes.append(shape)
    return np.stack(shapes), mask


def pieces(values, count):
    out = []
    rest = np.asarray(values, np.float64)
    for _ in range(count):
        piece = rest.astype(np.float32).astype(ml_dtypes.bfloat16)
        out.append(piece)
        rest = rest - piece.astype(np.float64)
    return out


def right_table(matrix):
    hi, lo = pieces(matrix, 2)
    return np.concatenate([hi, lo, hi], axis=0)


def left_table(matrix):
    hi, lo = pieces(matrix, 2)
    return np.concatenate([hi, lo, hi], axis=1)


def tables():
    modes, mask = zernike()
    lit = mask.sum()
    turn = 2.0 * math.pi / PIXELS
    freq = np.arange(PIXELS)
    half = np.arange(HALF)
    pupil = np.arange(-RADIUS, RADIUS + 1)

    ang = turn * (pupil[:64, None] * freq[None, :] % PIXELS)
    w1 = np.zeros((128, 256))
    w1[:64, :128] = np.cos(ang)
    w1[:64, 128:] = -np.sin(ang)
    w1[64:, :128] = np.sin(ang)
    w1[64:, 128:] = np.cos(ang)
    hi, lo = pieces(w1.T, 2)
    w1t = np.concatenate([np.concatenate([hi, lo], 1), np.concatenate([hi, 0 * lo], 1)], 0)
    turn65 = np.ones((8, 256), np.float32)
    turn65[1, :128] = turn65[1, 128:] = (-1.0) ** freq

    l2 = np.zeros((128, PAD))
    ang = turn * (half[:, None] * pupil[None, :] % PIXELS)
    l2[:64, :65] = np.cos(ang)
    l2[64:, :65] = np.sin(ang)
    l2[64, :65] = np.cos(turn * (64 * pupil % PIXELS))
    l2[:, 65] = l2[:, 32]

    ang = turn * (half[:, None] * half[None, :] % PIXELS)
    q = np.zeros((128, 128))
    q[:64, :64] = 2.0 * np.cos(ang)
    q[64:, 64:] = -2.0 * np.sin(ang)
    q[:64, 0] = 1.0
    q[:64, 64] = (-1.0) ** half
    q[64, :] = 0.0
    q[64, 1:64] = 2.0 * (-1.0) ** half[1:]
    q[64, 0] = 1.0
    q[64, 64] = 1.0
    q = q / (lit * PIXELS * PIXELS)

    weight = np.full((128,), -8.0)
    weight[0] = -4.0
    weight[64] = -4.0
    qt = q.T * weight[None, :]

    qd = np.zeros((128, 128))
    ang = turn * (half[:, None] * freq[None, :] % PIXELS)
    qd[:64] = np.cos(ang)
    qd[64:] = -np.sin(ang)
    qd[64] = (-1.0) ** freq

    ang = turn * (freq[:, None] * freq[None, :] % PIXELS)
    w4 = np.zeros((256, 256))
    w4[:128, :128] = np.cos(ang)
    w4[:128, 128:] = -np.sin(ang)
    w4[128:, :128] = np.sin(ang)
    w4[128:, 128:] = np.cos(ang)

    rows_table = np.polynomial.legendre.legvander(pupil / RADIUS, DEGREE - 1)
    t = np.zeros((MODES, TERMS, 128))
    t[:, :DEGREE, :64] = np.einsum("ip,kpx->kix", np.linalg.pinv(rows_table), modes)[:, :, :64]
    t[:, DEGREE, 0] = modes[:, 32, 64]
    t[:, :, 64:] = t[:, :, :64]
    th, tm, tl = pieces(t, 3)
    t1 = np.zeros((256, TERMS * 128), ml_dtypes.bfloat16)
    for at, part in ((0, th), (36, th), (72, tm), (128, th), (164, tl), (200, tm)):
        t1[at : at + MODES] = part.reshape(MODES, -1)
    t[:, :, :64] *= -1.0
    th, tm = pieces(t, 2)
    t2 = np.zeros((TERMS * 128, 128), ml_dtypes.bfloat16)
    t2[:, :MODES] = th.reshape(MODES, -1).T
    t2[:, 64 : 64 + MODES] = tm.reshape(MODES, -1).T

    y = np.zeros((PAD, 16))
    y[:65, :DEGREE] = rows_table
    y[65, DEGREE] = 1.0
    yh, ym, yl = pieces(y, 3)
    y1 = np.concatenate([yh, yh, ym, yh, yl, ym], axis=1)
    y = np.zeros((16, PAD))
    y[:DEGREE, :65] = rows_table.T
    y[DEGREE, 65] = 1.0
    y2 = left_table(y)

    def packed(values, other):
        out = np.zeros((SIDE, 128))
        out[:65, :64] = values[:, :64]
        out[65, 0] = values[32, 64]
        out[:, 64:] = other * out[:, :64]
        return out

    lens = np.stack(
        [
            packed(mask, 1.0),
            packed(np.cos(DIVERSITY * modes[2] * mask), 1.0),
            packed(-np.sin(DIVERSITY * modes[2] * mask), -1.0),
        ]
    ).astype(np.float32)

    edges = np.minimum(freq, PIXELS - 1 - freq)
    taper = np.zeros((8, 128), np.float32)
    for kind in range(4):
        width = (kind + 1) * PIXELS // 16
        taper[kind] = np.where(
            edges < width, 0.5 - 0.5 * np.cos(math.pi * (edges + 0.5) / width), 1.0
        )

    flip = np.zeros((128, 128))
    flip[(-freq) % PIXELS, freq] = 1.0
    flip = np.concatenate([flip] * 3, axis=0).astype(ml_dtypes.bfloat16)

    return dict(
        w1=right_table(w1),
        w1t=w1t,
        turn65=turn65,
        l2=left_table(l2),
        l2t=tall_table(l2.T),
        q=left_table(q),
        qt=tall_table(qt),
        w4=right_table(w4),
        w4t=right_table(w4.T),
        qd=qd.astype(np.float32),
        t1=t1,
        t2=t2,
        y1=y1,
        y2=y2,
        lens=lens,
        taper=taper,
        flip=flip,
    )


NAMES = (
    "w1", "w1t", "turn65", "l2", "l2t", "q", "qt", "w4", "w4t", "qd", "t1", "t2", "y1", "y2", "lens", "taper", "flip",
)


MOVED = ("w1", "w1t", "l2", "l2t", "q", "qt", "w4", "w4t", "t1", "t2", "flip")


def sincos(x):
    k = jnp.floor(x * np.float32(1.0 / math.pi) + 0.5)
    r = x - k * np.float32(3.140625)
    r = r - k * np.float32(0.0009670257568359375)
    r = r - k * np.float32(6.2771141529083251953e-7)
    odd = k - 2.0 * jnp.floor(k * 0.5)
    sign = 1.0 - 2.0 * odd
    r2 = r * r
    s = np.float32(-2.3868346521031027639830001794722295e-8)
    for c in (
        2.7526e-6,
        -1.98408735e-4,
        8.33333114e-3,
        -1.66666667e-1,
    ):
        s = s * r2 + np.float32(c)
    s = (s * r2 * r + r) * sign
    c_ = np.float32(-2.6e-7)
    for c in (
        2.4771e-5,
        -1.38888e-3,
        4.16666e-2,
        -0.5,
        1.0,
    ):
        c_ = c_ * r2 + np.float32(c)
    return s, c_ * sign


def cosine(x):
    k = jnp.floor(x * np.float32(1.0 / math.pi) + 0.5)
    r = x - k * np.float32(3.140625)
    r = r - k * np.float32(0.0009670257568359375)
    r = r - k * np.float32(6.2771141529083251953e-7)
    sign = 1.0 - 2.0 * (k - 2.0 * jnp.floor(k * 0.5))
    r2 = r * r
    out = np.float32(-2.6e-7)
    for c in (2.4771e-5, -1.38888e-3, 4.16666e-2, -0.5, 1.0):
        out = out * r2 + np.float32(c)
    return out * sign


def two(x):
    hi = x.astype(BF16)
    return hi, (x - hi.astype(F32)).astype(BF16)


def three(x):
    hi = x.astype(BF16)
    rest = x - hi.astype(F32)
    mid = rest.astype(BF16)
    return hi, mid, (rest - mid.astype(F32)).astype(BF16)


def right(x, table):
    hi, lo = two(x)
    return jnp.dot(jnp.concatenate([hi, hi, lo], axis=1), table, preferred_element_type=F32)


def left(table, x):
    hi, lo = two(x)
    return jnp.dot(table, jnp.concatenate([hi, hi, lo], axis=0), preferred_element_type=F32)


def skewed(count, ahead, first, second):
    waiting = []
    for i in range(count):
        waiting.append(first(i))
        if len(waiting) > ahead:
            second(waiting.pop(0))
    for x in waiting:
        second(x)


def tall_table(matrix):
    hi, lo = pieces(matrix, 2)
    return np.concatenate([np.concatenate([hi, hi], 1), np.concatenate([lo, 0 * lo], 1)], 0)


def tall(table, x):
    out = jnp.dot(table, jnp.concatenate(two(x), axis=0), preferred_element_type=F32)
    half = out.shape[0] // 2
    return out[:half] + out[half:]


def patched(whole, first):
    return jnp.concatenate([first, whole[8:]], axis=0)


def kernel(
    nf, nr, nc,
    images, corners, kinds, coefs_in, step, noise, smooth,
    w1, w1t, turn65, l2, l2t, q, qt, w4, w4t, qd, t1, t2, y1, y2, lens, taper, flip,
    coefs_out, object_out,
    images_, w1_, w1t_, l2_, l2t_, q_, qt_, w4_, w4t_, t1_, t2_, flip_, result,
    fill_sem, image_sem, result_sem,
    coefs, halo, bent, dbent, fields, waves, otf, data, sums, parts, objs, norm1, norm2, turned,
    rs_send, rs_recv, ag_send, ag_recv, n1_send, n1_recv, n2_send, n2_recv, h_send, h_recv,
):
    me = lax.axis_index("frame")
    row = lax.axis_index("row")
    col = lax.axis_index("col")
    place = row * nc + col
    nplace = nr * nc
    per = 16 // nf
    own = min(per, TILES)
    owners = TILES // own
    pair = nf // 2
    chips = max(pair, 1) * nplace

    lanes = lax.broadcasted_iota(jnp.int32, (8, 128), 1)
    subs = lax.broadcasted_iota(jnp.int32, (8, 128), 0)
    m00 = (lanes == 0) & (subs == 0)
    m064 = (lanes == 64) & (subs == 0)

    def loop(first, last, act):
        def body(k, _):
            act(k)
            return 0

        if last > first:
            lax.fori_loop(first, last, body, 0)

    halo[...] = jnp.zeros(halo.shape, F32)

    fills = {
        i: pltpu.make_async_copy(src, dst, fill_sem.at[i])
        for i, (src, dst) in enumerate(
            [
                (w4, w4_), (t1, t1_), (w1, w1_), (l2, l2_), (q, q_), (w4t, w4t_), (qt, qt_),
                (l2t, l2t_), (w1t, w1t_), (t2, t2_), (flip, flip_),
            ]
        )
    }
    source = images

    def image_copy(s, f):
        r, c_ = s // 2, lax.rem(s, 2)
        return pltpu.make_async_copy(source.at[f, r, c_], images_.at[s, f], image_sem.at[s, f])

    for f in range(FRAMES):
        image_copy(0, f).start()
    for i in range(5):
        fills[i].start()
    for s in range(1, FIELDS):
        for f in range(FRAMES):
            image_copy(s, f).start()
    for i in range(5, len(fills)):
        fills[i].start()
    images, w1, w1t, l2, l2t, q, qt, w4, w4t, t1, t2, flip = (
        images_, w1_, w1t_, l2_, l2t_, q_, qt_, w4_, w4t_, t1_, t2_, flip_
    )

    def after(index, step, count):
        moved = index + step
        return jnp.where(moved >= count, moved - count, moved)

    frames = [after(me, k, nf) for k in range(nf)]
    rows = [after(row, k, nr) for k in range(nr)]
    cols = [after(col, k, nc) for k in range(nc)]

    def far(steps):
        k, dr, dc = steps
        dy, dx = k // 2, dc * 2 + k % 2
        return min(dy, 4 - dy) + min(dr, nr - dr) + min(dx, 4 - dx)

    others = [(k, dr, dc) for k in range(max(pair, 1)) for dr in range(nr) for dc in range(nc)]
    others = sorted(others, key=far, reverse=True)
    others = [x for x in others if x != (0, 0, 0)]

    def there(steps):
        k, dr, dc = steps
        return {"frame": frames[2 * k], "row": rows[dr], "col": cols[dc]}

    npeers = (nf - 1) + max(pair, 1) * (nplace - 1)
    if npeers:
        barrier = pltpu.get_barrier_semaphore()

        for x in others:
            if x[1:] != (0, 0):
                pl.semaphore_signal(barrier, inc=1, device_id=there(x), device_id_type=MESH)
        for k in range(1, nf):
            pl.semaphore_signal(barrier, inc=1, device_id={"frame": frames[k]}, device_id_type=MESH)

    coefs[...] = jnp.zeros((ITEMS, 128), F32)
    bent[...] = jnp.zeros((ITEMS * 16, 128), F32)
    for f in range(FRAMES):
        for s in range(FIELDS):
            coefs[pl.ds(s * 4 + f, 1), pl.ds(0, MODES)] = coefs_in[f, s // 2, pl.ds(s % 2, 1), :]

    rows64 = lax.broadcasted_iota(jnp.int32, (HALF, 128), 0).astype(F32)
    cols8 = lanes.astype(F32)

    def data_field(s):
        r, c_ = s // 2, lax.rem(s, 2)
        for f in range(FRAMES):
            image_copy(s, f).wait()
        kind = kinds[r, c_]
        window = jnp.where(
            kind == 0, taper[pl.ds(0, 1), :],
            jnp.where(
                kind == 1, taper[pl.ds(1, 1), :],
                jnp.where(kind == 2, taper[pl.ds(2, 1), :], taper[pl.ds(3, 1), :]),
            ),
        )
        rotor = jnp.concatenate(two(qd[...] * window), axis=1)
        both = jnp.concatenate([window, window], axis=1)
        c0s = [corners[0, r, c_, f].astype(F32) for f in range(FRAMES)]
        c1s = [corners[1, r, c_, f].astype(F32) for f in range(FRAMES)]

        def choose(index, values):
            out = jnp.where(index == 0, values[0], values[1])
            return jnp.where(index == 2, values[2], jnp.where(index == 3, values[3], out))

        cycles = rows64 * (choose(lanes[:1] // 32, c0s) * np.float32(1.0 / PIXELS))
        cycles = cycles - jnp.floor(cycles + 0.5)
        row_sin, row_cos = sincos(cycles * np.float32(2.0 * math.pi))
        cycles = cols8 * (choose(subs, c1s) * np.float32(1.0 / PIXELS))
        cycles = cycles - jnp.floor(cycles + 0.5)
        col_sin, col_cos = sincos(cycles * np.float32(2.0 * math.pi))
        col_sin = col_sin * np.float32(1.0 / PIXELS)
        col_cos = col_cos * np.float32(1.0 / PIXELS)

        ready = []
        middle = []
        turns = []
        for f in range(FRAMES):
            image = jnp.concatenate([images[s, f, 0], images[s, f, 1]], axis=1)
            lines = jnp.dot(
                rotor, jnp.concatenate([image, image], axis=0), preferred_element_type=F32
            )
            lines = lines * both
            rs = jnp.broadcast_to(row_sin[:, f * 32 : f * 32 + 1], (HALF, 128))
            rc = jnp.broadcast_to(row_cos[:, f * 32 : f * 32 + 1], (HALF, 128))
            turns.append((col_sin[f : f + 1], col_cos[f : f + 1]))
            c0h = c0s[f] * 0.5
            alternate = (1.0 - 4.0 * jnp.abs(c0h - jnp.floor(c0h))) * np.float32(1.0 / PIXELS)
            for c in range(2):
                zr = lines[:64, c * 128 : c * 128 + 128]
                zi = lines[64:, c * 128 : c * 128 + 128]
                middle.append(jnp.sum(zi[:1], axis=1, keepdims=True) * alternate)
                zi = patched(zi, jnp.where(subs == 0, 0.0, zi[:8]))
                ready.append(jnp.concatenate([zr * rc - zi * rs, zr * rs + zi * rc], axis=1))
        spec = right(jnp.concatenate(ready, axis=0), w4[...])
        for f in range(FRAMES):
            cs, cc = turns[f]
            for c in range(2):
                at = (f * 2 + c) * 64
                dr = spec[at : at + 64, :128]
                di = spec[at : at + 64, 128:]
                data[s * 4 + f, pl.ds(c * 64, 64), pl.ds(0, 128)] = dr * cc - di * cs
                di = dr * cs + di * cc
                data[s * 4 + f, pl.ds(c * 64, 64), pl.ds(128, 128)] = patched(
                    di, jnp.where(m00, middle[f * 2 + c], di[:8])
                )

    def remote(src, dst, send, recv, device):
        return pltpu.make_async_remote_copy(
            src_ref=src, dst_ref=dst, send_sem=send, recv_sem=recv,
            device_id=device, device_id_type=MESH,
        )

    def owner(s, k):
        return lax.rem(s, 2) * owners + k

    def landed(ref, sem):
        pltpu.make_async_copy(ref, ref, sem).wait()

    def mine(s):
        return me // owners == lax.rem(s, 2) if nf > 1 else s >= 0

    def send_field(it, s):
        if nf > 1:
            for step_ in range(owners):
                k = lax.rem(me + step_, owners)
                peer = owner(s, k)
                copy = remote(
                    sums.at[it, s, pl.ds(k * own, own)], parts.at[it, s // 2, me],
                    rs_send.at[it, s], rs_recv.at[it, s // 2], {"frame": peer},
                )
                pl.when(peer != me)(copy.start)

    def reduce_field(it, s):
        @pl.when(mine(s))
        def _():
            k = lax.rem(me, owners)
            if nf > 1:
                landed(parts.at[it, s // 2, pl.ds(0, nf - 1)], rs_recv.at[it, s // 2])
            for j in range(own):
                tile = k * own + j
                total = sums[it, s, tile]
                for other in range(1, nf):
                    total = total + parts[it, s // 2, frames[other], j]
                first = tile == 0
                real, imag, power = total[0], total[1], total[2]
                n = noise[0, 0]
                other = jnp.where(m00 & first, pltpu.roll(imag, 64, 1), power)
                objs[it, s, tile, 0] = real / (power + n)
                objs[it, s, tile, 1] = jnp.where(m064 & first, 0.0, imag / (other + n))
            at = pl.ds(k * own, own)
            for j in sorted(range(1, nf), key=lambda j: -min(j // 4, 4 - j // 4) - j // 2 % 2):
                remote(
                    objs.at[it, s, at], objs.at[it, s, at],
                    ag_send.at[it, s // 2], ag_recv.at[it, s], {"frame": frames[j]},
                ).start()

    def wait_field(it, s):
        if nf > 1:
            pl.when(mine(s))(lambda: landed(objs.at[it, s, pl.ds(0, TILES - own)], ag_recv.at[it, s]))
            pl.when(jnp.logical_not(mine(s)))(lambda: landed(objs.at[it, s], ag_recv.at[it, s]))

    def n1_copy(it, slot):
        return remote(
            norm1.at[it, lax.rem(me, 2)], norm1.at[it, slot],
            n1_send.at[it], n1_recv.at[it], {"frame": me + 1 - 2 * lax.rem(me, 2)},
        )

    def n2_copy(it, steps):
        slot = me // 2 * nplace + place
        return remote(
            norm2.at[it, slot], norm2.at[it, slot], n2_send.at[it], n2_recv.at[it], there(steps)
        )

    def halo_copies(it):
        def one(axis, index, count, delta, slot):
            peer = jnp.clip(index + delta, 0, count - 1)
            inside = (index + delta >= 0) & (index + delta < count)
            return inside, remote(
                halo.at[it, 4], halo.at[it, slot], h_send.at[it, slot], h_recv.at[it, slot], {axis: peer}
            )

        out = []
        if nr > 1:
            out += [one("row", row, nr, 1, 0), one("row", row, nr, -1, 1)]
        if nc > 1:
            out += [one("col", col, nc, 1, 2), one("col", col, nc, -1, 3)]
        return out

    def halo_sides():
        out = []
        if nr > 1:
            out += [(0, row > 0), (1, row < nr - 1)]
        if nc > 1:
            out += [(2, col > 0), (3, col < nc - 1)]
        return out

    def bend(cf):
        ch = cf.astype(BF16).astype(F32)
        cm = (cf - ch).astype(BF16).astype(F32)
        cl = (cf - ch - cm).astype(BF16).astype(F32)
        low = ch + pltpu.roll(cm, 36, 1) + pltpu.roll(ch, 72, 1)
        high = cl + pltpu.roll(ch, 36, 1) + pltpu.roll(cm, 72, 1)
        lhs = jnp.concatenate([low, high], axis=1).astype(BF16)
        return jnp.dot(lhs, t1[...], preferred_element_type=F32)

    def store_bent(out):
        for i in range(TERMS):
            bent[pl.ds(i, ITEMS, stride=16), :] = out[:, i * 128 : i * 128 + 128]

    fills[0].wait()
    fills[1].wait()
    store_bent(bend(coefs[...]))
    for i in range(2, 5):
        fills[i].wait()

    def forward(it, s):
        stacks = []
        for f in range(FRAMES):
            x = bent[pl.ds(pl.multiple_of((s * 4 + f) * 16, 16), 16), :]
            h, m, l = three(x)
            stacks.append(jnp.concatenate([h, m, h, l, h, m], axis=0))
        phases = jnp.dot(y1[...], jnp.concatenate(stacks, axis=1), preferred_element_type=F32)
        quarter = jnp.where(lanes[:1] < 64, 0.0, np.float32(0.5 * math.pi))
        none = jnp.zeros((PAD - SIDE, 128), F32)
        lines = []
        for g in range(0, FRAMES, GROUP):
            pupil = []
            for f in range(g, g + GROUP):
                item = s * 4 + f
                one0 = cosine(phases[:SIDE, f * 128 : f * 128 + 128] - quarter) * lens[0]
                two0 = pltpu.roll(one0, 64, 1)
                one1 = one0 * lens[1] + two0 * lens[2]
                fields[item, 0] = two0
                fields[item, 1] = two0 * lens[1] - one0 * lens[2]
                pupil += [one0, none, one1, none]
            lines.append(right(jnp.concatenate(pupil, axis=0), w1[...]))
        lines = jnp.concatenate(lines, axis=0)
        z = []

        def first(f):
            evens = []
            odds = []
            for c in range(2):
                at = (f * 2 + c) * PAD
                wave = left(
                    l2[...],
                    jnp.concatenate(
                        [
                            lines[at : at + 64], lines[at + 64 : at + 72] * turn65[...],
                            lines[at + 72 : at + 80],
                        ],
                        axis=0,
                    ),
                )
                waves[s * 4 + f, c] = wave
                a, b = wave[:64, :128], wave[:64, 128:]
                e, d = wave[64:, :128], wave[64:, 128:]
                ab = a * a + b * b
                ed = e * e + d * d
                even = ab + ed
                odd = 2.0 * (a * d - b * e)
                evens.append(patched(even, jnp.where(subs == 0, ab[:8], even[:8])))
                odds.append(patched(odd, jnp.where(subs == 0, ed[:8], odd[:8])))
            return jnp.concatenate(
                [jnp.concatenate(evens, axis=1), jnp.concatenate(odds, axis=1)], axis=0
            )

        def second(spread):
            half = left(q[...], spread)
            for c in range(2):
                at = slice(c * 128, c * 128 + 128)
                z.append(jnp.concatenate([half[:64, at], half[64:, at]], axis=1))

        def third():
            if len(z) % (2 * GROUP) == 0:
                out.append(right(jnp.concatenate(z[-2 * GROUP :], axis=0), w4[...]))

        out = []
        skewed(FRAMES, SKEW, first, lambda x: (second(x), third()))
        z = jnp.concatenate(out, axis=0)
        for f in range(FRAMES):
            otf[s * 4 + f] = z[f * 128 : f * 128 + 128]
        for t in range(TILES):
            cr = ci = pw = None
            for f in range(FRAMES):
                for c in range(2):
                    at = f * 128 + c * 64 + t * 8
                    zr, zi = z[at : at + 8, :128], z[at : at + 8, 128:]
                    dr = data[s * 4 + f, pl.ds(c * 64 + t * 8, 8), pl.ds(0, 128)]
                    di = data[s * 4 + f, pl.ds(c * 64 + t * 8, 8), pl.ds(128, 128)]
                    ii = zi * di
                    zz = zi * zi
                    im = zr * di - zi * dr
                    if t == 0:
                        im = jnp.where(m00, ii, im)
                        im = jnp.where(m064, pltpu.roll(zz, 64, 1), im)
                        ii = jnp.where(m00, 0.0, ii)
                        zz = jnp.where(m00, 0.0, zz)
                    re = zr * dr + ii
                    p = zr * zr + zz
                    cr = re if cr is None else cr + re
                    ci = im if ci is None else ci + im
                    pw = p if pw is None else pw + p
            sums[it, s, t, 0] = cr
            sums[it, s, t, 1] = ci
            sums[it, s, t, 2] = pw

    def backward(it, s):
        dz = {}
        zero = subs == 0

        def residual(g):
            res = [[] for _ in range(2 * GROUP)]
            for t in range(TILES):
                our = objs[it, s, t, 0]
                oui = objs[it, s, t, 1]
                oor = ooi = our * our + oui * oui
                if t == 0:
                    oor = jnp.where(m00, our * our, oor)
                    ooi = jnp.where(m00, oui * oui, ooi)
                for f in range(g, g + GROUP):
                    for c in range(2):
                        at = pl.ds(c * 64 + t * 8, 8)
                        item = s * 4 + f
                        zr, zi = otf[item, at, pl.ds(0, 128)], otf[item, at, pl.ds(128, 128)]
                        dr, di = data[item, at, pl.ds(0, 128)], data[item, at, pl.ds(128, 128)]
                        ii = di * oui
                        im = di * our - dr * oui
                        if t == 0:
                            im = jnp.where(m00, ii, im)
                            ii = jnp.where(m00, 0.0, ii)
                        real = dr * our + ii - oor * zr
                        res[(f - g) * 2 + c].append(jnp.concatenate([real, im - ooi * zi], axis=1))
            return jnp.concatenate(sum(res, []), axis=0)

        def first(f):
            at = f % GROUP * 128
            dz_ = dz[f // GROUP]
            half = jnp.concatenate(
                [
                    jnp.concatenate([dz_[at : at + 64, :128], dz_[at + 64 : at + 128, :128]], axis=1),
                    jnp.concatenate([dz_[at : at + 64, 128:], dz_[at + 64 : at + 128, 128:]], axis=1),
                ],
                axis=0,
            )
            dspread = tall(qt[...], half)
            dwaves = []
            for c in range(2):
                de = dspread[:64, c * 128 : c * 128 + 128]
                do = dspread[64:, c * 128 : c * 128 + 128]
                wave = waves[s * 4 + f, c]
                a, b = wave[:64, :128], wave[:64, 128:]
                e, d = wave[64:, :128], wave[64:, 128:]
                da = a * de + d * do
                db = b * de - e * do
                dc = e * de - b * do
                dd = d * de + a * do
                de8, do8 = de[:8], do[:8]
                da = patched(da, jnp.where(zero, a[:8] * de8, da[:8]))
                db = patched(db, jnp.where(zero, b[:8] * de8, db[:8]))
                dc = patched(dc, jnp.where(zero, e[:8] * do8, dc[:8]))
                dd = patched(dd, jnp.where(zero, d[:8] * do8, dd[:8]))
                dwaves.append(jnp.concatenate(
                    [jnp.concatenate([da, db], axis=1), jnp.concatenate([dc, dd], axis=1)], axis=0
                ))
            return dwaves

        def second(dwaves):
            out = []
            for dwave in dwaves:
                x = tall(l2t[...], dwave)
                out.append(jnp.concatenate([x[:64], x[64:72] * turn65[...], x[72:]], axis=0))
            return out

        def third(x):
            x = jnp.dot(
                jnp.concatenate(two(jnp.concatenate(x, axis=0)), axis=1), w1t[...],
                preferred_element_type=F32,
            )
            return x[:, :128] + x[:, 128:]

        res, dwaves, dlines, dpupil = {}, {}, {}, {}
        for what, i in ORDER:
            if what == "r":
                res[i] = residual(i * GROUP)
            elif what == "w":
                dz[i] = right(res[i], w4t[...])
            elif what == "q":
                dwaves[i] = first(i)
            elif what == "l":
                dlines[i] = second(dwaves[i])
            else:
                dpupil[i] = third(sum([dlines[f] for f in range(i * GROUP, i * GROUP + GROUP)], []))
        dpupil = jnp.concatenate([dpupil[i] for i in sorted(dpupil)], axis=0)
        dphase = []
        for f in range(FRAMES):
            at = f * 2 * PAD
            dphase.append(
                fields[s * 4 + f, 0] * dpupil[at : at + SIDE]
                + fields[s * 4 + f, 1] * dpupil[at + PAD : at + PAD + SIDE]
            )
        dphase = jnp.concatenate(dphase, axis=1)
        dphase = jnp.concatenate([dphase, jnp.zeros((PAD - SIDE, FRAMES * 128), F32)], axis=0)
        out = left(y2[...], dphase)
        for f in range(FRAMES):
            dbent[pl.ds(pl.multiple_of((s * 4 + f) * 16, 16), 16), :] = out[:, f * 128 : f * 128 + 128]

    def result_copy():
        return pltpu.make_async_copy(result, object_out, result_sem)

    def write_object():
        last = ITERS - 1
        for j in range(per):
            tile = me * per + j

            @pl.when(tile < 8)
            def _(j=j, tile=tile):
                for s in range(FIELDS):
                    re = objs[last, s, tile, 0]
                    im = objs[last, s, tile, 1]
                    result[0, s // 2, s % 2, pl.ds(j * 8, 8), :] = re
                    result[1, s // 2, s % 2, pl.ds(j * 8, 8), :] = jnp.where(m00 & (tile == 0), 0.0, im)

            @pl.when(tile >= 8)
            def _(j=j, tile=tile):
                g = tile - 8
                for s in range(FIELDS):
                    for c in range(2):
                        at = (s * 2 + c) * 8
                        for i in range(1, 8):
                            turned[pl.ds(at + i, 1), :] = objs[last, s, 7 - g, c, pl.ds(8 - i, 1), :]
                        zero = objs[last, s, lax.rem(8 - g, 8), c, pl.ds(0, 1), :]
                        if c == 0:
                            middle = objs[last, s, 0, 1, pl.ds(0, 1), :]
                            middle = jnp.where(lanes[:1] == 0, middle, 0.0)
                        else:
                            middle = jnp.zeros((1, 128), F32)
                        turned[pl.ds(at, 1), :] = jnp.where(g == 0, middle, zero)
                out = jnp.dot(
                    jnp.concatenate(three(turned[...]), axis=1), flip[...], preferred_element_type=F32
                )
                for s in range(FIELDS):
                    at = s * 16
                    result[0, s // 2, s % 2, pl.ds(j * 8, 8), :] = out[at : at + 8]
                    result[1, s // 2, s % 2, pl.ds(j * 8, 8), :] = -out[at + 8 : at + 16]
        result_copy().start()

    def departures(it):
        if nf > 1:
            def field(s):
                @pl.when(mine(s))
                def _():
                    if own < TILES:
                        landed(sums.at[it, s, pl.ds(0, TILES - own)], rs_send.at[it, s])
                    landed(parts.at[it, s // 2, pl.ds(0, nf - 1), :, pl.ds(0, 2)], ag_send.at[it, s // 2])

                pl.when(jnp.logical_not(mine(s)))(lambda: landed(sums.at[it, s], rs_send.at[it, s]))

            loop(0, FIELDS, field)
            n1_copy(it, lax.rem(me, 2)).wait_send()
        for inside, copy in halo_copies(it):
            pl.when(inside)(copy.wait_send)

    def iteration(it):
        cf = coefs[...]

        def forward_step(s):
            pl.when(it == 0)(lambda: data_field(s))
            forward(it, s)

            first = (it == 0) & (s == 2)
            if npeers:
                pl.when(first)(lambda: pl.semaphore_wait(barrier, npeers))
            pl.when(first)(lambda: loop(0, 2, lambda s: send_field(it, s)))
            pl.when((it > 0) | (s >= 2))(lambda: send_field(it, s))

        def backward_step(s):
            wait_field(it, s)
            backward(it, s)

        loop(0, FIELDS, forward_step)

        halo[it, 4] = cf
        for inside, copy in halo_copies(it):
            pl.when(inside)(copy.start)

        loop(0, FIELDS, lambda s: reduce_field(it, s))

        @pl.when(it == 0)
        def _():
            for i in range(5, len(fills)):
                fills[i].wait()

        loop(0, FIELDS, backward_step)

        x = jnp.concatenate([dbent[pl.ds(i, ITEMS, stride=16), :] for i in range(TERMS)], axis=1)
        acc = jnp.dot(jnp.concatenate(two(x), axis=0), t2[...], preferred_element_type=F32)
        grads = acc[:16] + pltpu.roll(acc[:16], 64, 1) + acc[16:]
        lane16 = lax.broadcasted_iota(jnp.int32, (ITEMS, 128), 1)
        grads = jnp.where(lane16 < MODES, grads, 0.0)

        sq = grads * grads
        total = jnp.sum(sq[:8] + sq[8:], axis=0, keepdims=True)
        slot = me // 2 * nplace + place
        if nf > 1:
            norm1[it, lax.rem(me, 2)] = total
            n1_copy(it, lax.rem(me, 2)).start()
            n1_copy(it, 1 - lax.rem(me, 2)).wait_recv()
            total = norm1[it, 0] + norm1[it, 1]
        norm2[it, slot] = total
        for x in others:
            n2_copy(it, x).start()

        for side, inside in halo_sides():
            @pl.when(inside)
            def _(side=side):
                landed(halo.at[it, side], h_recv.at[it, side])

        above, below = halo[it, 0, 8:], halo[it, 1, :8]
        laplace = []
        for r in range(2):
            mine_ = cf[r * 8 : r * 8 + 8]
            other = cf[8 - r * 8 : 16 - r * 8]
            beside = jnp.where(
                subs < 4,
                pltpu.roll(halo[it, 2, r * 8 : r * 8 + 8], 4, 0),
                pltpu.roll(halo[it, 3, r * 8 : r * 8 + 8], 4, 0),
            )
            out = 4.0 * mine_ - other - pltpu.roll(mine_, 4, 0) - beside
            laplace.append(out - (above if r == 0 else below))
        laplace = jnp.concatenate(laplace, axis=0)
        smoothed = cf - step[0, 0] * smooth[0, 0] * laplace
        out = bend(jnp.concatenate([smoothed, grads], axis=0))
        pl.when(it == ITERS - 1)(write_object)
        departures(it)

        if chips > 1:
            landed(norm2.at[it, pl.ds(0, chips - 1)], n2_recv.at[it])
        total = jnp.sum(jnp.sum(norm2[it], axis=0), axis=1, keepdims=True)
        count = ITEMS * MODES * nf * nplace
        scale = jnp.sqrt(total / count + TINY)
        pace = step[0, 0] / scale
        coefs[...] = smoothed - pace * grads
        store_bent(out[:ITEMS] - pace * out[ITEMS:])

    loop(0, ITERS, iteration)

    for f in range(FRAMES):
        for s in range(FIELDS):
            coefs_out[f, s // 2, pl.ds(s % 2, 1), :] = coefs[pl.ds(s * 4 + f, 1), pl.ds(0, MODES)]

    result_copy().wait()
    if chips > 1:
        for it in range(ITERS):
            landed(norm2.at[it, pl.ds(0, chips - 1)], n2_send.at[it])


def deliver(coefs, objects, coefs_out, object_out):
    coefs_out[...] = coefs[...]
    object_out[...] = objects[...]


def solution(mesh):
    nf, nr, nc = (mesh.shape[name] for name in ("frame", "row", "col"))
    host = tables()
    per = 16 // nf
    vmem = pl.BlockSpec(memory_space=pltpu.VMEM)
    smem = pl.BlockSpec(memory_space=pltpu.SMEM)
    hbm = pl.BlockSpec(memory_space=pl.ANY)

    def body(images, corners, kinds, coefs, step, noise, smooth):
        own = min(per, TILES)
        chips = max(nf // 2, 1) * nr * nc
        scratch = [pltpu.VMEM((FIELDS, FRAMES, 2, PIXELS, PIXELS), BF16)]
        scratch += [pltpu.VMEM(host[name].shape, BF16) for name in MOVED]
        scratch += [
            pltpu.VMEM((2, 2, 2, 8 * per, 128), F32),
            pltpu.SemaphoreType.DMA((len(MOVED),)),
            pltpu.SemaphoreType.DMA((FIELDS, FRAMES)),
            pltpu.SemaphoreType.DMA,
        ]
        scratch += [
            pltpu.VMEM((ITEMS, 128), F32),
            pltpu.VMEM((ITERS, 5, ITEMS, 128), F32),
            pltpu.VMEM((ITEMS * 16, 128), F32),
            pltpu.VMEM((ITEMS * 16, 128), F32),
            pltpu.VMEM((ITEMS, 2, SIDE, 128), F32),
            pltpu.VMEM((ITEMS, 2, 128, 256), F32),
            pltpu.VMEM((ITEMS, 128, 256), F32),
            pltpu.VMEM((ITEMS, 128, 256), F32),
            pltpu.VMEM((ITERS, FIELDS, TILES, 3, 8, 128), F32),
            pltpu.VMEM((ITERS, 2, nf, own, 3, 8, 128), F32),
            pltpu.VMEM((ITERS, FIELDS, TILES, 2, 8, 128), F32),
            pltpu.VMEM((ITERS, 2, 1, 128), F32),
            pltpu.VMEM((ITERS, chips, 1, 128), F32),
            pltpu.VMEM((HALF, 128), F32),
        ]
        dma = pltpu.SemaphoreType.DMA
        scratch += [dma((ITERS, FIELDS)), dma((ITERS, 2)), dma((ITERS, 2)), dma((ITERS, FIELDS))]
        scratch += [dma((ITERS,)) for _ in range(4)]
        scratch += [dma((ITERS, 4)) for _ in range(2)]
        single = lambda x: x.reshape(1, 1)
        raw = pl.pallas_call(
            functools.partial(kernel, nf, nr, nc),
            out_shape=(
                jax.ShapeDtypeStruct((FRAMES, 2, 2, MODES), F32),
                jax.ShapeDtypeStruct((2, 2, 2, 8 * per, 128), F32),
            ),
            in_specs=[hbm, smem, smem, vmem, smem, smem, smem]
            + [hbm if name in MOVED else vmem for name in NAMES],
            out_specs=(vmem, hbm),
            scratch_shapes=scratch,
            compiler_params=pltpu.CompilerParams(
                collective_id=0 if nf * nr * nc > 1 else None,
                has_side_effects=True,
                vmem_limit_bytes=56 * 1024 * 1024,
            ),
        )(
            images, corners.transpose(0, 2, 3, 1), kinds, coefs, single(step), single(noise), single(smooth),
            *[jnp.asarray(host[name]) for name in NAMES],
        )
        return pl.pallas_call(
            deliver,
            out_shape=tuple(jax.ShapeDtypeStruct(x.shape, x.dtype) for x in raw),
            in_specs=[vmem, vmem],
            out_specs=(vmem, vmem),
        )(*raw)

    in_specs = (
        P("frame", "row", "col", None, None, None),
        P(None, "frame", "row", "col"),
        P("row", "col"),
        P("frame", "row", "col", None),
        P(),
        P(),
        P(),
    )
    out_specs = (P("frame", "row", "col", None), P(None, "row", "col", "frame", None))
    return jax.shard_map(body, mesh=mesh, in_specs=in_specs, out_specs=out_specs, check_vma=False)
```

```python
import functools
import math

import jax
import jax.numpy as jnp
import ml_dtypes
import numpy as np
from jax import lax
from jax.experimental import pallas as pl
from jax.experimental.pallas import tpu as pltpu
from jax.sharding import PartitionSpec as P

ITERS = 2
MODES = 36
SKEW = 3
ORDER = (
    ("r", 0), ("w", 0), ("r", 1), ("w", 1), ("q", 0), ("q", 1), ("q", 2), ("q", 3),
    ("l", 0), ("l", 1), ("v", 0), ("l", 2), ("l", 3), ("v", 1),
)
GROUP = 2
DEGREE = 9
TERMS = DEGREE + 1
DIVERSITY = 1.5
TINY = 1e-06
PIXELS = 128
RADIUS = 32
SIDE = 72
PAD = 80
HALF = 64
FRAMES = 4
FIELDS = 4
ITEMS = FRAMES * FIELDS
TILES = 8
F32 = jnp.float32
BF16 = jnp.bfloat16
MESH = pl.DeviceIdType.MESH


def noll_order(mode_index):
    radial_order = (math.isqrt(8 * (mode_index - 1) + 1) - 1) // 2
    position = mode_index - radial_order * (radial_order + 1) // 2
    parity = radial_order % 2
    azimuth = (position + parity) // 2 * 2 - parity
    if azimuth != 0 and mode_index % 2 == 1:
        azimuth = -azimuth
    return (radial_order, azimuth)


def zernike():
    line = np.arange(-RADIUS, RADIUS + 1) / RADIUS
    rows, cols = np.meshgrid(line, line, indexing="ij")
    radius = np.sqrt(rows * rows + cols * cols)
    angle = np.arctan2(rows, cols)
    mask = (rows * rows + cols * cols <= 1.0).astype(np.float64)
    shapes = []
    for mode_index in range(2, MODES + 2):
        n, m = noll_order(mode_index)
        radial = np.zeros_like(radius)
        for t in range((n - abs(m)) // 2 + 1):
            factor = (-1) ** t * math.factorial(n - t)
            factor /= math.factorial(t)
            factor /= math.factorial((n + abs(m)) // 2 - t)
            factor /= math.factorial((n - abs(m)) // 2 - t)
            radial = radial + factor * radius ** (n - 2 * t)
        if m == 0:
            shape = math.sqrt(n + 1) * radial
        elif m > 0:
            shape = math.sqrt(2 * (n + 1)) * radial * np.cos(m * angle)
        else:
            shape = math.sqrt(2 * (n + 1)) * radial * np.sin(-m * angle)
        shapes.append(shape)
    return np.stack(shapes), mask


def pieces(values, count):
    out = []
    rest = np.asarray(values, np.float64)
    for _ in range(count):
        piece = rest.astype(np.float32).astype(ml_dtypes.bfloat16)
        out.append(piece)
        rest = rest - piece.astype(np.float64)
    return out


def right_table(matrix):
    hi, lo = pieces(matrix, 2)
    return np.concatenate([hi, lo, hi], axis=0)


def left_table(matrix):
    hi, lo = pieces(matrix, 2)
    return np.concatenate([hi, lo, hi], axis=1)


def tables():
    modes, mask = zernike()
    lit = mask.sum()
    turn = 2.0 * math.pi / PIXELS
    freq = np.arange(PIXELS)
    half = np.arange(HALF)
    pupil = np.arange(-RADIUS, RADIUS + 1)

    ang = turn * (pupil[:64, None] * freq[None, :] % PIXELS)
    w1 = np.zeros((128, 256))
    w1[:64, :128] = np.cos(ang)
    w1[:64, 128:] = -np.sin(ang)
    w1[64:, :128] = np.sin(ang)
    w1[64:, 128:] = np.cos(ang)
    hi, lo = pieces(w1.T, 2)
    w1t = np.concatenate([np.concatenate([hi, lo], 1), np.concatenate([hi, 0 * lo], 1)], 0)
    turn65 = np.ones((8, 256), np.float32)
    turn65[1, :128] = turn65[1, 128:] = (-1.0) ** freq

    l2 = np.zeros((128, PAD))
    ang = turn * (half[:, None] * pupil[None, :] % PIXELS)
    l2[:64, :65] = np.cos(ang)
    l2[64:, :65] = np.sin(ang)
    l2[64, :65] = np.cos(turn * (64 * pupil % PIXELS))
    l2[:, 65] = l2[:, 32]

    ang = turn * (half[:, None] * half[None, :] % PIXELS)
    q = np.zeros((128, 128))
    q[:64, :64] = 2.0 * np.cos(ang)
    q[64:, 64:] = -2.0 * np.sin(ang)
    q[:64, 0] = 1.0
    q[:64, 64] = (-1.0) ** half
    q[64, :] = 0.0
    q[64, 1:64] = 2.0 * (-1.0) ** half[1:]
    q[64, 0] = 1.0
    q[64, 64] = 1.0
    q = q / (lit * PIXELS * PIXELS)

    weight = np.full((128,), -8.0)
    weight[0] = -4.0
    weight[64] = -4.0
    qt = q.T * weight[None, :]

    qd = np.zeros((128, 128))
    ang = turn * (half[:, None] * freq[None, :] % PIXELS)
    qd[:64] = np.cos(ang)
    qd[64:] = -np.sin(ang)
    qd[64] = (-1.0) ** freq

    ang = turn * (freq[:, None] * freq[None, :] % PIXELS)
    w4 = np.zeros((256, 256))
    w4[:128, :128] = np.cos(ang)
    w4[:128, 128:] = -np.sin(ang)
    w4[128:, :128] = np.sin(ang)
    w4[128:, 128:] = np.cos(ang)

    rows_table = np.polynomial.legendre.legvander(pupil / RADIUS, DEGREE - 1)
    t = np.zeros((MODES, TERMS, 128))
    t[:, :DEGREE, :64] = np.einsum("ip,kpx->kix", np.linalg.pinv(rows_table), modes)[:, :, :64]
    t[:, DEGREE, 0] = modes[:, 32, 64]
    t[:, :, 64:] = t[:, :, :64]
    th, tm, tl = pieces(t, 3)
    t1 = np.zeros((256, TERMS * 128), ml_dtypes.bfloat16)
    for at, part in ((0, th), (36, th), (72, tm), (128, th), (164, tl), (200, tm)):
        t1[at : at + MODES] = part.reshape(MODES, -1)
    t[:, :, :64] *= -1.0
    th, tm = pieces(t, 2)
    t2 = np.zeros((TERMS * 128, 128), ml_dtypes.bfloat16)
    t2[:, :MODES] = th.reshape(MODES, -1).T
    t2[:, 64 : 64 + MODES] = tm.reshape(MODES, -1).T

    y = np.zeros((PAD, 16))
    y[:65, :DEGREE] = rows_table
    y[65, DEGREE] = 1.0
    yh, ym, yl = pieces(y, 3)
    y1 = np.concatenate([yh, yh, ym, yh, yl, ym], axis=1)
    y = np.zeros((16, PAD))
    y[:DEGREE, :65] = rows_table.T
    y[DEGREE, 65] = 1.0
    y2 = left_table(y)

    def packed(values, other):
        out = np.zeros((SIDE, 128))
        out[:65, :64] = values[:, :64]
        out[65, 0] = values[32, 64]
        out[:, 64:] = other * out[:, :64]
        return out

    lens = np.stack(
        [
            packed(mask, 1.0),
            packed(np.cos(DIVERSITY * modes[2] * mask), 1.0),
            packed(-np.sin(DIVERSITY * modes[2] * mask), -1.0),
        ]
    ).astype(np.float32)

    edges = np.minimum(freq, PIXELS - 1 - freq)
    taper = np.zeros((8, 128), np.float32)
    for kind in range(4):
        width = (kind + 1) * PIXELS // 16
        taper[kind] = np.where(
            edges < width, 0.5 - 0.5 * np.cos(math.pi * (edges + 0.5) / width), 1.0
        )

    flip = np.zeros((128, 128))
    flip[(-freq) % PIXELS, freq] = 1.0
    flip = np.concatenate([flip] * 3, axis=0).astype(ml_dtypes.bfloat16)

    return dict(
        w1=right_table(w1),
        w1t=w1t,
        turn65=turn65,
        l2=left_table(l2),
        l2t=tall_table(l2.T),
        q=left_table(q),
        qt=tall_table(qt),
        w4=right_table(w4),
        w4t=right_table(w4.T),
        qd=qd.astype(np.float32),
        t1=t1,
        t2=t2,
        y1=y1,
        y2=y2,
        lens=lens,
        taper=taper,
        flip=flip,
    )


NAMES = (
    "w1", "w1t", "turn65", "l2", "l2t", "q", "qt", "w4", "w4t", "qd", "t1", "t2", "y1", "y2", "lens", "taper", "flip",
)


MOVED = ("w1", "w1t", "l2", "l2t", "q", "qt", "w4", "w4t", "t1", "t2", "flip")


def sincos(x):
    k = jnp.floor(x * np.float32(1.0 / math.pi) + 0.5)
    r = x - k * np.float32(3.140625)
    r = r - k * np.float32(0.0009670257568359375)
    r = r - k * np.float32(6.2771141529083251953e-7)
    odd = k - 2.0 * jnp.floor(k * 0.5)
    sign = 1.0 - 2.0 * odd
    r2 = r * r
    s = np.float32(-2.3868346521031027639830001794722295e-8)
    for c in (
        2.7526e-6,
        -1.98408735e-4,
        8.33333114e-3,
        -1.66666667e-1,
    ):
        s = s * r2 + np.float32(c)
    s = (s * r2 * r + r) * sign
    c_ = np.float32(-2.6e-7)
    for c in (
        2.4771e-5,
        -1.38888e-3,
        4.16666e-2,
        -0.5,
        1.0,
    ):
        c_ = c_ * r2 + np.float32(c)
    return s, c_ * sign


def cosine(x):
    k = jnp.floor(x * np.float32(1.0 / math.pi) + 0.5)
    r = x - k * np.float32(3.140625)
    r = r - k * np.float32(0.0009670257568359375)
    r = r - k * np.float32(6.2771141529083251953e-7)
    sign = 1.0 - 2.0 * (k - 2.0 * jnp.floor(k * 0.5))
    r2 = r * r
    out = np.float32(-2.6e-7)
    for c in (2.4771e-5, -1.38888e-3, 4.16666e-2, -0.5, 1.0):
        out = out * r2 + np.float32(c)
    return out * sign


def two(x):
    hi = x.astype(BF16)
    return hi, (x - hi.astype(F32)).astype(BF16)


def three(x):
    hi = x.astype(BF16)
    rest = x - hi.astype(F32)
    mid = rest.astype(BF16)
    return hi, mid, (rest - mid.astype(F32)).astype(BF16)


def right(x, table):
    hi, lo = two(x)
    return jnp.dot(jnp.concatenate([hi, hi, lo], axis=1), table, preferred_element_type=F32)


def left(table, x):
    hi, lo = two(x)
    return jnp.dot(table, jnp.concatenate([hi, hi, lo], axis=0), preferred_element_type=F32)


def skewed(count, ahead, first, second):
    waiting = []
    for i in range(count):
        waiting.append(first(i))
        if len(waiting) > ahead:
            second(waiting.pop(0))
    for x in waiting:
        second(x)


def tall_table(matrix):
    hi, lo = pieces(matrix, 2)
    return np.concatenate([np.concatenate([hi, hi], 1), np.concatenate([lo, 0 * lo], 1)], 0)


def tall(table, x):
    out = jnp.dot(table, jnp.concatenate(two(x), axis=0), preferred_element_type=F32)
    half = out.shape[0] // 2
    return out[:half] + out[half:]


def patched(whole, first):
    return jnp.concatenate([first, whole[8:]], axis=0)


def kernel(
    nf, nr, nc,
    images, corners, kinds, coefs_in, step, noise, smooth,
    w1, w1t, turn65, l2, l2t, q, qt, w4, w4t, qd, t1, t2, y1, y2, lens, taper, flip,
    coefs_out, object_out,
    images_, w1_, w1t_, l2_, l2t_, q_, qt_, w4_, w4t_, t1_, t2_, flip_, result,
    fill_sem, image_sem, result_sem,
    coefs, halo, bent, dbent, fields, waves, otf, data, sums, parts, objs, norm1, norm2, turned,
    rs_send, rs_recv, ag_send, ag_recv, n1_send, n1_recv, n2_send, n2_recv, h_send, h_recv,
):
    me = lax.axis_index("frame")
    row = lax.axis_index("row")
    col = lax.axis_index("col")
    place = row * nc + col
    nplace = nr * nc
    per = 16 // nf
    own = min(per, TILES)
    owners = TILES // own
    pair = nf // 2
    chips = max(pair, 1) * nplace

    lanes = lax.broadcasted_iota(jnp.int32, (8, 128), 1)
    subs = lax.broadcasted_iota(jnp.int32, (8, 128), 0)
    m00 = (lanes == 0) & (subs == 0)
    m064 = (lanes == 64) & (subs == 0)

    def loop(first, last, act):
        def body(k, _):
            act(k)
            return 0

        if last > first:
            lax.fori_loop(first, last, body, 0)

    halo[...] = jnp.zeros(halo.shape, F32)

    fills = {
        i: pltpu.make_async_copy(src, dst, fill_sem.at[i])
        for i, (src, dst) in enumerate(
            [
                (w4, w4_), (t1, t1_), (w1, w1_), (l2, l2_), (q, q_), (w4t, w4t_), (qt, qt_),
                (l2t, l2t_), (w1t, w1t_), (t2, t2_), (flip, flip_),
            ]
        )
    }
    source = images

    def image_copy(s, f):
        r, c_ = s // 2, lax.rem(s, 2)
        return pltpu.make_async_copy(source.at[f, r, c_], images_.at[s, f], image_sem.at[s, f])

    for f in range(FRAMES):
        image_copy(0, f).start()
    for i in range(5):
        fills[i].start()
    for s in range(1, FIELDS):
        for f in range(FRAMES):
            image_copy(s, f).start()
    for i in range(5, len(fills)):
        fills[i].start()
    images, w1, w1t, l2, l2t, q, qt, w4, w4t, t1, t2, flip = (
        images_, w1_, w1t_, l2_, l2t_, q_, qt_, w4_, w4t_, t1_, t2_, flip_
    )

    def after(index, step, count):
        moved = index + step
        return jnp.where(moved >= count, moved - count, moved)

    frames = [after(me, k, nf) for k in range(nf)]
    rows = [after(row, k, nr) for k in range(nr)]
    cols = [after(col, k, nc) for k in range(nc)]

    def far(steps):
        k, dr, dc = steps
        dy, dx = k // 2, dc * 2 + k % 2
        return min(dy, 4 - dy) + min(dr, nr - dr) + min(dx, 4 - dx)

    others = [(k, dr, dc) for k in range(max(pair, 1)) for dr in range(nr) for dc in range(nc)]
    others = sorted(others, key=far, reverse=True)
    others = [x for x in others if x != (0, 0, 0)]

    def there(steps):
        k, dr, dc = steps
        return {"frame": frames[2 * k], "row": rows[dr], "col": cols[dc]}

    npeers = (nf - 1) + max(pair, 1) * (nplace - 1)
    if npeers:
        barrier = pltpu.get_barrier_semaphore()

        for x in others:
            if x[1:] != (0, 0):
                pl.semaphore_signal(barrier, inc=1, device_id=there(x), device_id_type=MESH)
        for k in range(1, nf):
            pl.semaphore_signal(barrier, inc=1, device_id={"frame": frames[k]}, device_id_type=MESH)

    coefs[...] = jnp.zeros((ITEMS, 128), F32)
    bent[...] = jnp.zeros((ITEMS * 16, 128), F32)
    for f in range(FRAMES):
        for s in range(FIELDS):
            coefs[pl.ds(s * 4 + f, 1), pl.ds(0, MODES)] = coefs_in[f, s // 2, pl.ds(s % 2, 1), :]

    rows64 = lax.broadcasted_iota(jnp.int32, (HALF, 128), 0).astype(F32)
    cols8 = lanes.astype(F32)

    def data_field(s):
        r, c_ = s // 2, lax.rem(s, 2)
        for f in range(FRAMES):
            image_copy(s, f).wait()
        kind = kinds[r, c_]
        window = jnp.where(
            kind == 0, taper[pl.ds(0, 1), :],
            jnp.where(
                kind == 1, taper[pl.ds(1, 1), :],
                jnp.where(kind == 2, taper[pl.ds(2, 1), :], taper[pl.ds(3, 1), :]),
            ),
        )
        rotor = jnp.concatenate(two(qd[...] * window), axis=1)
        both = jnp.concatenate([window, window], axis=1)
        c0s = [corners[0, r, c_, f].astype(F32) for f in range(FRAMES)]
        c1s = [corners[1, r, c_, f].astype(F32) for f in range(FRAMES)]

        def choose(index, values):
            out = jnp.where(index == 0, values[0], values[1])
            return jnp.where(index == 2, values[2], jnp.where(index == 3, values[3], out))

        cycles = rows64 * (choose(lanes[:1] // 32, c0s) * np.float32(1.0 / PIXELS))
        cycles = cycles - jnp.floor(cycles + 0.5)
        row_sin, row_cos = sincos(cycles * np.float32(2.0 * math.pi))
        cycles = cols8 * (choose(subs, c1s) * np.float32(1.0 / PIXELS))
        cycles = cycles - jnp.floor(cycles + 0.5)
        col_sin, col_cos = sincos(cycles * np.float32(2.0 * math.pi))
        col_sin = col_sin * np.float32(1.0 / PIXELS)
        col_cos = col_cos * np.float32(1.0 / PIXELS)

        ready = []
        middle = []
        turns = []
        for f in range(FRAMES):
            image = jnp.concatenate([images[s, f, 0], images[s, f, 1]], axis=1)
            lines = jnp.dot(
                rotor, jnp.concatenate([image, image], axis=0), preferred_element_type=F32
            )
            lines = lines * both
            rs = jnp.broadcast_to(row_sin[:, f * 32 : f * 32 + 1], (HALF, 128))
            rc = jnp.broadcast_to(row_cos[:, f * 32 : f * 32 + 1], (HALF, 128))
            turns.append((col_sin[f : f + 1], col_cos[f : f + 1]))
            c0h = c0s[f] * 0.5
            alternate = (1.0 - 4.0 * jnp.abs(c0h - jnp.floor(c0h))) * np.float32(1.0 / PIXELS)
            for c in range(2):
                zr = lines[:64, c * 128 : c * 128 + 128]
                zi = lines[64:, c * 128 : c * 128 + 128]
                middle.append(jnp.sum(zi[:1], axis=1, keepdims=True) * alternate)
                zi = patched(zi, jnp.where(subs == 0, 0.0, zi[:8]))
                ready.append(jnp.concatenate([zr * rc - zi * rs, zr * rs + zi * rc], axis=1))
        spec = right(jnp.concatenate(ready, axis=0), w4[...])
        for f in range(FRAMES):
            cs, cc = turns[f]
            for c in range(2):
                at = (f * 2 + c) * 64
                dr = spec[at : at + 64, :128]
                di = spec[at : at + 64, 128:]
                data[s * 4 + f, pl.ds(c * 64, 64), pl.ds(0, 128)] = dr * cc - di * cs
                di = dr * cs + di * cc
                data[s * 4 + f, pl.ds(c * 64, 64), pl.ds(128, 128)] = patched(
                    di, jnp.where(m00, middle[f * 2 + c], di[:8])
                )

    def remote(src, dst, send, recv, device):
        return pltpu.make_async_remote_copy(
            src_ref=src, dst_ref=dst, send_sem=send, recv_sem=recv,
            device_id=device, device_id_type=MESH,
        )

    def owner(s, k):
        return lax.rem(s, 2) * owners + k

    def landed(ref, sem):
        pltpu.make_async_copy(ref, ref, sem).wait()

    def mine(s):
        return me // owners == lax.rem(s, 2) if nf > 1 else s >= 0

    def send_field(it, s):
        if nf > 1:
            for step_ in range(owners):
                k = lax.rem(me + step_, owners)
                peer = owner(s, k)
                copy = remote(
                    sums.at[it, s, pl.ds(k * own, own)], parts.at[it, s // 2, me],
                    rs_send.at[it, s], rs_recv.at[it, s // 2], {"frame": peer},
                )
                pl.when(peer != me)(copy.start)

    def reduce_field(it, s):
        @pl.when(mine(s))
        def _():
            k = lax.rem(me, owners)
            if nf > 1:
                landed(parts.at[it, s // 2, pl.ds(0, nf - 1)], rs_recv.at[it, s // 2])
            for j in range(own):
                tile = k * own + j
                total = sums[it, s, tile]
                for other in range(1, nf):
                    total = total + parts[it, s // 2, frames[other], j]
                first = tile == 0
                real, imag, power = total[0], total[1], total[2]
                n = noise[0, 0]
                other = jnp.where(m00 & first, pltpu.roll(imag, 64, 1), power)
                objs[it, s, tile, 0] = real / (power + n)
                objs[it, s, tile, 1] = jnp.where(m064 & first, 0.0, imag / (other + n))
            at = pl.ds(k * own, own)
            for j in range(1, nf):
                remote(
                    objs.at[it, s, at], objs.at[it, s, at],
                    ag_send.at[it, s // 2], ag_recv.at[it, s], {"frame": frames[j]},
                ).start()

    def wait_field(it, s):
        if nf > 1:
            pl.when(mine(s))(lambda: landed(objs.at[it, s, pl.ds(0, TILES - own)], ag_recv.at[it, s]))
            pl.when(jnp.logical_not(mine(s)))(lambda: landed(objs.at[it, s], ag_recv.at[it, s]))

    def n1_copy(it, slot):
        return remote(
            norm1.at[it, lax.rem(me, 2)], norm1.at[it, slot],
            n1_send.at[it], n1_recv.at[it], {"frame": me + 1 - 2 * lax.rem(me, 2)},
        )

    def n2_copy(it, steps):
        slot = me // 2 * nplace + place
        return remote(
            norm2.at[it, slot], norm2.at[it, slot], n2_send.at[it], n2_recv.at[it], there(steps)
        )

    def halo_copies(it):
        def one(axis, index, count, delta, slot):
            peer = jnp.clip(index + delta, 0, count - 1)
            inside = (index + delta >= 0) & (index + delta < count)
            return inside, remote(
                halo.at[it, 4], halo.at[it, slot], h_send.at[it, slot], h_recv.at[it, slot], {axis: peer}
            )

        out = []
        if nr > 1:
            out += [one("row", row, nr, 1, 0), one("row", row, nr, -1, 1)]
        if nc > 1:
            out += [one("col", col, nc, 1, 2), one("col", col, nc, -1, 3)]
        return out

    def halo_sides():
        out = []
        if nr > 1:
            out += [(0, row > 0), (1, row < nr - 1)]
        if nc > 1:
            out += [(2, col > 0), (3, col < nc - 1)]
        return out

    def bend(cf):
        ch = cf.astype(BF16).astype(F32)
        cm = (cf - ch).astype(BF16).astype(F32)
        cl = (cf - ch - cm).astype(BF16).astype(F32)
        low = ch + pltpu.roll(cm, 36, 1) + pltpu.roll(ch, 72, 1)
        high = cl + pltpu.roll(ch, 36, 1) + pltpu.roll(cm, 72, 1)
        lhs = jnp.concatenate([low, high], axis=1).astype(BF16)
        return jnp.dot(lhs, t1[...], preferred_element_type=F32)

    def store_bent(out):
        for i in range(TERMS):
            bent[pl.ds(i, ITEMS, stride=16), :] = out[:, i * 128 : i * 128 + 128]

    fills[0].wait()
    fills[1].wait()
    store_bent(bend(coefs[...]))
    for i in range(2, 5):
        fills[i].wait()

    def forward(it, s):
        stacks = []
        for f in range(FRAMES):
            x = bent[pl.ds(pl.multiple_of((s * 4 + f) * 16, 16), 16), :]
            h, m, l = three(x)
            stacks.append(jnp.concatenate([h, m, h, l, h, m], axis=0))
        phases = jnp.dot(y1[...], jnp.concatenate(stacks, axis=1), preferred_element_type=F32)
        quarter = jnp.where(lanes[:1] < 64, 0.0, np.float32(0.5 * math.pi))
        none = jnp.zeros((PAD - SIDE, 128), F32)
        lines = []
        for g in range(0, FRAMES, GROUP):
            pupil = []
            for f in range(g, g + GROUP):
                item = s * 4 + f
                one0 = cosine(phases[:SIDE, f * 128 : f * 128 + 128] - quarter) * lens[0]
                two0 = pltpu.roll(one0, 64, 1)
                one1 = one0 * lens[1] + two0 * lens[2]
                fields[item, 0] = two0
                fields[item, 1] = two0 * lens[1] - one0 * lens[2]
                pupil += [one0, none, one1, none]
            lines.append(right(jnp.concatenate(pupil, axis=0), w1[...]))
        lines = jnp.concatenate(lines, axis=0)
        z = []

        def first(f):
            evens = []
            odds = []
            for c in range(2):
                at = (f * 2 + c) * PAD
                wave = left(
                    l2[...],
                    jnp.concatenate(
                        [
                            lines[at : at + 64], lines[at + 64 : at + 72] * turn65[...],
                            lines[at + 72 : at + 80],
                        ],
                        axis=0,
                    ),
                )
                waves[s * 4 + f, c] = wave
                a, b = wave[:64, :128], wave[:64, 128:]
                e, d = wave[64:, :128], wave[64:, 128:]
                ab = a * a + b * b
                ed = e * e + d * d
                even = ab + ed
                odd = 2.0 * (a * d - b * e)
                evens.append(patched(even, jnp.where(subs == 0, ab[:8], even[:8])))
                odds.append(patched(odd, jnp.where(subs == 0, ed[:8], odd[:8])))
            return jnp.concatenate(
                [jnp.concatenate(evens, axis=1), jnp.concatenate(odds, axis=1)], axis=0
            )

        def second(spread):
            half = left(q[...], spread)
            for c in range(2):
                at = slice(c * 128, c * 128 + 128)
                z.append(jnp.concatenate([half[:64, at], half[64:, at]], axis=1))

        def third():
            if len(z) % (2 * GROUP) == 0:
                out.append(right(jnp.concatenate(z[-2 * GROUP :], axis=0), w4[...]))

        out = []
        skewed(FRAMES, SKEW, first, lambda x: (second(x), third()))
        z = jnp.concatenate(out, axis=0)
        for f in range(FRAMES):
            otf[s * 4 + f] = z[f * 128 : f * 128 + 128]
        for t in range(TILES):
            cr = ci = pw = None
            for f in range(FRAMES):
                for c in range(2):
                    at = f * 128 + c * 64 + t * 8
                    zr, zi = z[at : at + 8, :128], z[at : at + 8, 128:]
                    dr = data[s * 4 + f, pl.ds(c * 64 + t * 8, 8), pl.ds(0, 128)]
                    di = data[s * 4 + f, pl.ds(c * 64 + t * 8, 8), pl.ds(128, 128)]
                    ii = zi * di
                    zz = zi * zi
                    im = zr * di - zi * dr
                    if t == 0:
                        im = jnp.where(m00, ii, im)
                        im = jnp.where(m064, pltpu.roll(zz, 64, 1), im)
                        ii = jnp.where(m00, 0.0, ii)
                        zz = jnp.where(m00, 0.0, zz)
                    re = zr * dr + ii
                    p = zr * zr + zz
                    cr = re if cr is None else cr + re
                    ci = im if ci is None else ci + im
                    pw = p if pw is None else pw + p
            sums[it, s, t, 0] = cr
            sums[it, s, t, 1] = ci
            sums[it, s, t, 2] = pw

    def backward(it, s):
        dz = {}
        zero = subs == 0

        def residual(g):
            res = [[] for _ in range(2 * GROUP)]
            for t in range(TILES):
                our = objs[it, s, t, 0]
                oui = objs[it, s, t, 1]
                oor = ooi = our * our + oui * oui
                if t == 0:
                    oor = jnp.where(m00, our * our, oor)
                    ooi = jnp.where(m00, oui * oui, ooi)
                for f in range(g, g + GROUP):
                    for c in range(2):
                        at = pl.ds(c * 64 + t * 8, 8)
                        item = s * 4 + f
                        zr, zi = otf[item, at, pl.ds(0, 128)], otf[item, at, pl.ds(128, 128)]
                        dr, di = data[item, at, pl.ds(0, 128)], data[item, at, pl.ds(128, 128)]
                        ii = di * oui
                        im = di * our - dr * oui
                        if t == 0:
                            im = jnp.where(m00, ii, im)
                            ii = jnp.where(m00, 0.0, ii)
                        real = dr * our + ii - oor * zr
                        res[(f - g) * 2 + c].append(jnp.concatenate([real, im - ooi * zi], axis=1))
            return jnp.concatenate(sum(res, []), axis=0)

        def first(f):
            at = f % GROUP * 128
            dz_ = dz[f // GROUP]
            half = jnp.concatenate(
                [
                    jnp.concatenate([dz_[at : at + 64, :128], dz_[at + 64 : at + 128, :128]], axis=1),
                    jnp.concatenate([dz_[at : at + 64, 128:], dz_[at + 64 : at + 128, 128:]], axis=1),
                ],
                axis=0,
            )
            dspread = tall(qt[...], half)
            dwaves = []
            for c in range(2):
                de = dspread[:64, c * 128 : c * 128 + 128]
                do = dspread[64:, c * 128 : c * 128 + 128]
                wave = waves[s * 4 + f, c]
                a, b = wave[:64, :128], wave[:64, 128:]
                e, d = wave[64:, :128], wave[64:, 128:]
                da = a * de + d * do
                db = b * de - e * do
                dc = e * de - b * do
                dd = d * de + a * do
                de8, do8 = de[:8], do[:8]
                da = patched(da, jnp.where(zero, a[:8] * de8, da[:8]))
                db = patched(db, jnp.where(zero, b[:8] * de8, db[:8]))
                dc = patched(dc, jnp.where(zero, e[:8] * do8, dc[:8]))
                dd = patched(dd, jnp.where(zero, d[:8] * do8, dd[:8]))
                dwaves.append(jnp.concatenate(
                    [jnp.concatenate([da, db], axis=1), jnp.concatenate([dc, dd], axis=1)], axis=0
                ))
            return dwaves

        def second(dwaves):
            out = []
            for dwave in dwaves:
                x = tall(l2t[...], dwave)
                out.append(jnp.concatenate([x[:64], x[64:72] * turn65[...], x[72:]], axis=0))
            return out

        def third(x):
            x = jnp.dot(
                jnp.concatenate(two(jnp.concatenate(x, axis=0)), axis=1), w1t[...],
                preferred_element_type=F32,
            )
            return x[:, :128] + x[:, 128:]

        res, dwaves, dlines, dpupil = {}, {}, {}, {}
        for what, i in ORDER:
            if what == "r":
                res[i] = residual(i * GROUP)
            elif what == "w":
                dz[i] = right(res[i], w4t[...])
            elif what == "q":
                dwaves[i] = first(i)
            elif what == "l":
                dlines[i] = second(dwaves[i])
            else:
                dpupil[i] = third(sum([dlines[f] for f in range(i * GROUP, i * GROUP + GROUP)], []))
        dpupil = jnp.concatenate([dpupil[i] for i in sorted(dpupil)], axis=0)
        dphase = []
        for f in range(FRAMES):
            at = f * 2 * PAD
            dphase.append(
                fields[s * 4 + f, 0] * dpupil[at : at + SIDE]
                + fields[s * 4 + f, 1] * dpupil[at + PAD : at + PAD + SIDE]
            )
        dphase = jnp.concatenate(dphase, axis=1)
        dphase = jnp.concatenate([dphase, jnp.zeros((PAD - SIDE, FRAMES * 128), F32)], axis=0)
        out = left(y2[...], dphase)
        for f in range(FRAMES):
            dbent[pl.ds(pl.multiple_of((s * 4 + f) * 16, 16), 16), :] = out[:, f * 128 : f * 128 + 128]

    def result_copy():
        return pltpu.make_async_copy(result, object_out, result_sem)

    def write_object():
        last = ITERS - 1
        for j in range(per):
            tile = me * per + j

            @pl.when(tile < 8)
            def _(j=j, tile=tile):
                for s in range(FIELDS):
                    re = objs[last, s, tile, 0]
                    im = objs[last, s, tile, 1]
                    result[0, s // 2, s % 2, pl.ds(j * 8, 8), :] = re
                    result[1, s // 2, s % 2, pl.ds(j * 8, 8), :] = jnp.where(m00 & (tile == 0), 0.0, im)

            @pl.when(tile >= 8)
            def _(j=j, tile=tile):
                g = tile - 8
                for s in range(FIELDS):
                    for c in range(2):
                        at = (s * 2 + c) * 8
                        for i in range(1, 8):
                            turned[pl.ds(at + i, 1), :] = objs[last, s, 7 - g, c, pl.ds(8 - i, 1), :]
                        zero = objs[last, s, lax.rem(8 - g, 8), c, pl.ds(0, 1), :]
                        if c == 0:
                            middle = objs[last, s, 0, 1, pl.ds(0, 1), :]
                            middle = jnp.where(lanes[:1] == 0, middle, 0.0)
                        else:
                            middle = jnp.zeros((1, 128), F32)
                        turned[pl.ds(at, 1), :] = jnp.where(g == 0, middle, zero)
                out = jnp.dot(
                    jnp.concatenate(three(turned[...]), axis=1), flip[...], preferred_element_type=F32
                )
                for s in range(FIELDS):
                    at = s * 16
                    result[0, s // 2, s % 2, pl.ds(j * 8, 8), :] = out[at : at + 8]
                    result[1, s // 2, s % 2, pl.ds(j * 8, 8), :] = -out[at + 8 : at + 16]
        result_copy().start()

    def departures(it):
        if nf > 1:
            def field(s):
                @pl.when(mine(s))
                def _():
                    if own < TILES:
                        landed(sums.at[it, s, pl.ds(0, TILES - own)], rs_send.at[it, s])
                    landed(parts.at[it, s // 2, pl.ds(0, nf - 1), :, pl.ds(0, 2)], ag_send.at[it, s // 2])

                pl.when(jnp.logical_not(mine(s)))(lambda: landed(sums.at[it, s], rs_send.at[it, s]))

            loop(0, FIELDS, field)
            n1_copy(it, lax.rem(me, 2)).wait_send()
        for inside, copy in halo_copies(it):
            pl.when(inside)(copy.wait_send)

    def iteration(it):
        cf = coefs[...]

        def forward_step(s):
            pl.when(it == 0)(lambda: data_field(s))
            forward(it, s)

            first = (it == 0) & (s == 1)
            if npeers:
                pl.when(first)(lambda: pl.semaphore_wait(barrier, npeers))
            pl.when(first)(lambda: loop(0, 1, lambda s: send_field(it, s)))
            pl.when((it > 0) | (s >= 1))(lambda: send_field(it, s))

        def backward_step(s):
            wait_field(it, s)
            backward(it, s)

        loop(0, FIELDS, forward_step)

        halo[it, 4] = cf
        for inside, copy in halo_copies(it):
            pl.when(inside)(copy.start)

        loop(0, FIELDS, lambda s: reduce_field(it, s))

        @pl.when(it == 0)
        def _():
            for i in range(5, len(fills)):
                fills[i].wait()

        loop(0, FIELDS, backward_step)

        x = jnp.concatenate([dbent[pl.ds(i, ITEMS, stride=16), :] for i in range(TERMS)], axis=1)
        acc = jnp.dot(jnp.concatenate(two(x), axis=0), t2[...], preferred_element_type=F32)
        grads = acc[:16] + pltpu.roll(acc[:16], 64, 1) + acc[16:]
        lane16 = lax.broadcasted_iota(jnp.int32, (ITEMS, 128), 1)
        grads = jnp.where(lane16 < MODES, grads, 0.0)

        sq = grads * grads
        total = jnp.sum(sq[:8] + sq[8:], axis=0, keepdims=True)
        slot = me // 2 * nplace + place
        if nf > 1:
            norm1[it, lax.rem(me, 2)] = total
            n1_copy(it, lax.rem(me, 2)).start()
            n1_copy(it, 1 - lax.rem(me, 2)).wait_recv()
            total = norm1[it, 0] + norm1[it, 1]
        norm2[it, slot] = total
        for x in others:
            n2_copy(it, x).start()

        for side, inside in halo_sides():
            @pl.when(inside)
            def _(side=side):
                landed(halo.at[it, side], h_recv.at[it, side])

        above, below = halo[it, 0, 8:], halo[it, 1, :8]
        laplace = []
        for r in range(2):
            mine_ = cf[r * 8 : r * 8 + 8]
            other = cf[8 - r * 8 : 16 - r * 8]
            beside = jnp.where(
                subs < 4,
                pltpu.roll(halo[it, 2, r * 8 : r * 8 + 8], 4, 0),
                pltpu.roll(halo[it, 3, r * 8 : r * 8 + 8], 4, 0),
            )
            out = 4.0 * mine_ - other - pltpu.roll(mine_, 4, 0) - beside
            laplace.append(out - (above if r == 0 else below))
        laplace = jnp.concatenate(laplace, axis=0)
        smoothed = cf - step[0, 0] * smooth[0, 0] * laplace
        out = bend(jnp.concatenate([smoothed, grads], axis=0))
        pl.when(it == ITERS - 1)(write_object)
        departures(it)

        if chips > 1:
            landed(norm2.at[it, pl.ds(0, chips - 1)], n2_recv.at[it])
        total = jnp.sum(jnp.sum(norm2[it], axis=0), axis=1, keepdims=True)
        count = ITEMS * MODES * nf * nplace
        scale = jnp.sqrt(total / count + TINY)
        pace = step[0, 0] / scale
        coefs[...] = smoothed - pace * grads
        store_bent(out[:ITEMS] - pace * out[ITEMS:])

    loop(0, ITERS, iteration)

    for f in range(FRAMES):
        for s in range(FIELDS):
            coefs_out[f, s // 2, pl.ds(s % 2, 1), :] = coefs[pl.ds(s * 4 + f, 1), pl.ds(0, MODES)]

    result_copy().wait()
    if chips > 1:
        for it in range(ITERS):
            landed(norm2.at[it, pl.ds(0, chips - 1)], n2_send.at[it])


def deliver(coefs, objects, coefs_out, object_out):
    coefs_out[...] = coefs[...]
    object_out[...] = objects[...]


def solution(mesh):
    nf, nr, nc = (mesh.shape[name] for name in ("frame", "row", "col"))
    host = tables()
    per = 16 // nf
    vmem = pl.BlockSpec(memory_space=pltpu.VMEM)
    smem = pl.BlockSpec(memory_space=pltpu.SMEM)
    hbm = pl.BlockSpec(memory_space=pl.ANY)

    def body(images, corners, kinds, coefs, step, noise, smooth):
        own = min(per, TILES)
        chips = max(nf // 2, 1) * nr * nc
        scratch = [pltpu.VMEM((FIELDS, FRAMES, 2, PIXELS, PIXELS), BF16)]
        scratch += [pltpu.VMEM(host[name].shape, BF16) for name in MOVED]
        scratch += [
            pltpu.VMEM((2, 2, 2, 8 * per, 128), F32),
            pltpu.SemaphoreType.DMA((len(MOVED),)),
            pltpu.SemaphoreType.DMA((FIELDS, FRAMES)),
            pltpu.SemaphoreType.DMA,
        ]
        scratch += [
            pltpu.VMEM((ITEMS, 128), F32),
            pltpu.VMEM((ITERS, 5, ITEMS, 128), F32),
            pltpu.VMEM((ITEMS * 16, 128), F32),
            pltpu.VMEM((ITEMS * 16, 128), F32),
            pltpu.VMEM((ITEMS, 2, SIDE, 128), F32),
            pltpu.VMEM((ITEMS, 2, 128, 256), F32),
            pltpu.VMEM((ITEMS, 128, 256), F32),
            pltpu.VMEM((ITEMS, 128, 256), F32),
            pltpu.VMEM((ITERS, FIELDS, TILES, 3, 8, 128), F32),
            pltpu.VMEM((ITERS, 2, nf, own, 3, 8, 128), F32),
            pltpu.VMEM((ITERS, FIELDS, TILES, 2, 8, 128), F32),
            pltpu.VMEM((ITERS, 2, 1, 128), F32),
            pltpu.VMEM((ITERS, chips, 1, 128), F32),
            pltpu.VMEM((HALF, 128), F32),
        ]
        dma = pltpu.SemaphoreType.DMA
        scratch += [dma((ITERS, FIELDS)), dma((ITERS, 2)), dma((ITERS, 2)), dma((ITERS, FIELDS))]
        scratch += [dma((ITERS,)) for _ in range(4)]
        scratch += [dma((ITERS, 4)) for _ in range(2)]
        single = lambda x: x.reshape(1, 1)
        raw = pl.pallas_call(
            functools.partial(kernel, nf, nr, nc),
            out_shape=(
                jax.ShapeDtypeStruct((FRAMES, 2, 2, MODES), F32),
                jax.ShapeDtypeStruct((2, 2, 2, 8 * per, 128), F32),
            ),
            in_specs=[hbm, smem, smem, vmem, smem, smem, smem]
            + [hbm if name in MOVED else vmem for name in NAMES],
            out_specs=(vmem, hbm),
            scratch_shapes=scratch,
            compiler_params=pltpu.CompilerParams(
                collective_id=0 if nf * nr * nc > 1 else None,
                has_side_effects=True,
                vmem_limit_bytes=56 * 1024 * 1024,
            ),
        )(
            images, corners.transpose(0, 2, 3, 1), kinds, coefs, single(step), single(noise), single(smooth),
            *[jnp.asarray(host[name]) for name in NAMES],
        )
        return pl.pallas_call(
            deliver,
            out_shape=tuple(jax.ShapeDtypeStruct(x.shape, x.dtype) for x in raw),
            in_specs=[vmem, vmem],
            out_specs=(vmem, vmem),
        )(*raw)

    in_specs = (
        P("frame", "row", "col", None, None, None),
        P(None, "frame", "row", "col"),
        P("row", "col"),
        P("frame", "row", "col", None),
        P(),
        P(),
        P(),
    )
    out_specs = (P("frame", "row", "col", None), P(None, "row", "col", "frame", None))
    return jax.shard_map(body, mesh=mesh, in_specs=in_specs, out_specs=out_specs, check_vma=False)
```
